128 devices in a mesh: gx: 8 (over z, core), gy: 16 (over x, y).
Axes of the slice: x: 4, y: 4, z: 4, core: 2. Of those that a mesh axis runs over, the one named last changes fastest.
Arguments:
- features: bfloat16 [8, 16, 16, 8, 8, 8, 128], P('gx', 'gy'), may hold values from -6 to 6
- cotangent: bfloat16 [8, 16, 16, 8, 8, 8, 128], P('gx', 'gy'), may hold values from -6 to 6
- kernel_weight: bfloat16 [3, 3, 3, 128, 128], replicated, may hold values from -0.109375 to 0.109375
- conv_bias: float32 [128], replicated, may hold values from -3 to 3
- send_lists: int32 [8, 16, 8, 4], P('gx', 'gy'), may hold values from 0 to 16, as said below
- kernel_map: int32 [8, 16, 16, 27], P('gx', 'gy'), may hold values from 0 to 48, as said below
Outputs:
- activated: bfloat16 [8, 16, 16, 8, 8, 8, 128], P('gx', 'gy')
- input_grad: bfloat16 [8, 16, 16, 8, 8, 8, 128], P('gx', 'gy')
- weight_grad: float32 [3, 3, 3, 128, 128], replicated
- bias_grad: float32 [128], replicated
The draws below stay inside these ranges and needn't reach their ends.
Inputs may be any that keep to these rules, and one draw needn't show every extreme that they name: send_lists[i, j, k] names distinct own bricks (0 to 15) in its first 1 to 4 slots and 16 in the rest; it is all 16 where region (i+dx, j+dy) of direction k lies outside the grid. In every draw some interior region receives 4 named bricks in all 8 lists that reach it. kernel_map[i, j, b, 13] = b. Other entries name an own brick (below 16), a received slot 16 + 4 k + r whose brick is named (r below the count named in the list k of region (i-dx, j-dy)), or 48, an absent brick. Every named received slot appears somewhere in the region's map.
All inputs are finite; a program needn't handle non-finite values.
Results may differ from the reference program's by a relative error of at most 0.008.
Values may be sent and summed in bfloat16 or wider, within the bound.
A program may use at most 128 MiB of HBM per device.

```python
import math
import jax
import jax.numpy as jnp
from jax import lax

CH = 128
EDGE = 8
BRICKS = 16
CAP = 4
VOXELS = 1048576
N_GX = 8
N_GY = 16


DIRECTIONS = ((-1, -1), (-1, 0), (-1, 1), (0, -1), (0, 1), (1, -1), (1, 0), (1, 1))


def link_tables(key):
    subkeys = jax.random.split(jax.random.fold_in(key, 7), 4)
    counts = jax.random.randint(subkeys[0], (N_GX, N_GY, 8), 1, CAP + 1)
    centre_x = jax.random.randint(subkeys[1], (), 1, N_GX - 1)
    centre_y = jax.random.randint(subkeys[2], (), 1, N_GY - 1)
    grid_x = jnp.arange(N_GX)[:, None, None]
    grid_y = jnp.arange(N_GY)[None, :, None]
    step_x = jnp.array([d[0] for d in DIRECTIONS])[None, None, :]
    step_y = jnp.array([d[1] for d in DIRECTIONS])[None, None, :]
    forced = (grid_x == centre_x - step_x) & (grid_y == centre_y - step_y)
    counts = jnp.where(forced, CAP, counts)
    inside = (grid_x + step_x >= 0) & (grid_x + step_x < N_GX) & (grid_y + step_y >= 0) & (grid_y + step_y < N_GY)
    counts = jnp.where(inside, counts, 0)
    scores = jax.random.randint(subkeys[3], (N_GX, N_GY, 8, BRICKS), 0, 65536) * BRICKS + jnp.arange(BRICKS)
    ordering = jnp.argsort(scores, axis=-1)[..., :CAP]
    slot_ids = jnp.arange(CAP)
    send_list = jnp.where(slot_ids < counts[..., None], ordering, BRICKS).astype(jnp.int32)
    padded = jnp.pad(counts, ((1, 1), (1, 1), (0, 0)))
    incoming = jnp.stack([padded[1 - DIRECTIONS[k][0]:1 - DIRECTIONS[k][0] + N_GX, 1 - DIRECTIONS[k][1]:1 - DIRECTIONS[k][1] + N_GY, k] for k in range(8)], axis=-1)
    live_slots = (slot_ids[None, None, None, :] < incoming[..., None]).reshape(N_GX, N_GY, 8 * CAP)
    return (send_list, live_slots)


def draw_send_lists(key, part):
    return link_tables(key)[0]


def draw_kernel_map(key, part):
    send_list, live_slots = link_tables(key)
    subkeys = jax.random.split(jax.random.fold_in(key, 11), 4)
    slot_total = 8 * CAP
    empty_id = BRICKS + slot_total
    pair_total = BRICKS * 26
    shape_pairs = (N_GX, N_GY, pair_total)
    scores = jax.random.randint(subkeys[0], shape_pairs, 0, 65536) * pair_total + jnp.arange(pair_total)
    pair_rank = jnp.argsort(jnp.argsort(scores, axis=-1), axis=-1)
    rank_slot = jnp.clip(pair_rank, 0, slot_total - 1)
    assigned = (pair_rank < slot_total) & jnp.take_along_axis(live_slots, rank_slot, axis=-1)
    category = jax.random.randint(subkeys[1], shape_pairs, 0, 10)
    local_pick = jax.random.randint(subkeys[2], shape_pairs, 0, BRICKS)
    slot_pick = jax.random.randint(subkeys[3], shape_pairs, 0, slot_total)
    pick_live = jnp.take_along_axis(live_slots, slot_pick, axis=-1)
    fallback = jnp.where(category < 3, empty_id, jnp.where(category < 7, local_pick, jnp.where(pick_live, BRICKS + slot_pick, empty_id)))
    entries = jnp.where(assigned, BRICKS + pair_rank, fallback).reshape(N_GX, N_GY, BRICKS, 26)
    centre = jnp.broadcast_to(jnp.arange(BRICKS)[None, None, :, None], (N_GX, N_GY, BRICKS, 1))
    return jnp.concatenate([entries[..., :13], centre, entries[..., 13:]], axis=-1).astype(jnp.int32)


def levels(stream_key, dims, pieces, low, largest):
    factor_of, own = 1.0, jax.random.fold_in(stream_key, 6)
    for dim, blocks in pieces:
        heights = jnp.exp(jax.random.uniform(jax.random.fold_in(own, dim), (blocks,), jnp.float32, low / len(pieces), largest / len(pieces)))
        factor_of = factor_of * jnp.repeat(heights, dims[dim] // blocks).reshape([-1 if axis == dim else 1 for axis in range(len(dims))])
    return factor_of


def scatter_about(rng, shape, width, limit, shards=(), kind=jnp.bfloat16):
    values = jax.random.normal(rng, shape, jnp.float32) * width
    if len(shards) > 0:
        values = levels(rng, shape, shards, -0.22, 0.18) * values
    return jnp.clip(values, min=-limit, max=limit).astype(kind)


def setup_inputs(seed: int = 0) -> dict:
    key_of = jax.random.split(jax.random.key(seed), 7)
    features = scatter_about(key_of[0], (N_GX, N_GY, BRICKS, EDGE, EDGE, EDGE, CH), 1.0, 6.0, ((0, 8), (1, 16)))
    cotangent = scatter_about(key_of[1], (N_GX, N_GY, BRICKS, EDGE, EDGE, EDGE, CH), 1.0, 6.0, ((0, 8), (1, 16)))
    kernel_weight = scatter_about(key_of[2], (3, 3, 3, CH, CH), (27 * CH) ** -0.5, 0.109375)
    conv_bias = scatter_about(key_of[3], (CH,), 0.5, 3.0, (), jnp.float32)
    send_lists = draw_send_lists(jax.random.fold_in(key_of[6], 71), 0)
    kernel_map = draw_kernel_map(jax.random.fold_in(key_of[6], 71), 0)
    return {"features": features, "cotangent": cotangent, "kernel_weight": kernel_weight, "conv_bias": conv_bias, "send_lists": send_lists, "kernel_map": kernel_map}


DIRECTIONS = ((-1, -1), (-1, 0), (-1, 1), (0, -1), (0, 1), (1, -1), (1, 0), (1, 1))

def brick_faces(bricks):
    last_idx = bricks.shape[1] - 1
    return jnp.stack([bricks[:, 0], bricks[:, last_idx], bricks[:, :, 0], bricks[:, :, last_idx], bricks[:, :, :, 0], bricks[:, :, :, last_idx]], axis=1)

def layer_cut(offset_val, edge_len):
    if offset_val < 0:
        return slice(edge_len - 1, edge_len)
    if offset_val > 0:
        return slice(0, 1)
    return slice(0, edge_len)

def place_cut(offset_val, edge_len):
    if offset_val < 0:
        return slice(0, 1)
    if offset_val > 0:
        return slice(edge_len + 1, edge_len + 2)
    return slice(1, edge_len + 1)

def assemble(volume, face_table, brick_map):
    edge_len = volume.shape[1]
    channels = volume.shape[4]
    padded = jnp.zeros((volume.shape[0], edge_len + 2, edge_len + 2, edge_len + 2, channels), volume.dtype)
    padded = padded.at[:, 1:edge_len + 1, 1:edge_len + 1, 1:edge_len + 1].set(volume)
    for o in range(27):
        a, b, c = (o // 9 - 1, o // 3 % 3 - 1, o % 3 - 1)
        if a == 0 and b == 0 and (c == 0):
            continue
        column = brick_map[:, o]
        if a != 0:
            source = face_table[:, 1 if a < 0 else 0][column]
            rim_piece = source[:, layer_cut(b, edge_len), layer_cut(c, edge_len)][:, None]
        elif b != 0:
            source = face_table[:, 3 if b < 0 else 2][column]
            rim_piece = source[:, :, layer_cut(c, edge_len)][:, :, None]
        else:
            source = face_table[:, 5 if c < 0 else 4][column]
            rim_piece = source[:, :, :, None]
        padded = padded.at[:, place_cut(a, edge_len), place_cut(b, edge_len), place_cut(c, edge_len)].set(rim_piece)
    return padded

def conv_valid(padded, kernel):
    return lax.conv_general_dilated(padded.astype(jnp.float32), kernel.astype(jnp.float32), (1, 1, 1), 'VALID', dimension_numbers=('NDHWC', 'DHWIO', 'NDHWC'), precision=lax.Precision.HIGHEST)

def weight_terms(padded, slope_grad):
    edge_len = slope_grad.shape[1]
    channels = slope_grad.shape[4]
    flat_slope = slope_grad.reshape(-1, channels).astype(jnp.float32)
    partials = []
    for o in range(27):
        a, b, c = (o // 9, o // 3 % 3, o % 3)
        window = padded[:, a:a + edge_len, b:b + edge_len, c:c + edge_len].reshape(-1, channels).astype(jnp.float32)
        partials.append(lax.dot_general(window, flat_slope, (((0,), (0,)), ((), ())), precision=lax.Precision.HIGHEST))
    return jnp.stack(partials).reshape(3, 3, 3, channels, channels)

def device_table(fields, send_lists, device_id):
    row_pos = device_id // N_GY
    col_pos = device_id % N_GY
    own_faces = brick_faces(fields[row_pos, col_pos])
    zero_brick = jnp.zeros((1,) + fields.shape[3:], fields.dtype)
    blocks = [own_faces]
    for k in range(8):
        sender_x = row_pos - DIRECTIONS[k][0]
        sender_y = col_pos - DIRECTIONS[k][1]
        inside = (sender_x >= 0) & (sender_x < N_GX) & (sender_y >= 0) & (sender_y < N_GY)
        clip_x = jnp.clip(sender_x, 0, N_GX - 1).astype(jnp.int32)
        clip_y = jnp.clip(sender_y, 0, N_GY - 1).astype(jnp.int32)
        source = jnp.concatenate([fields[clip_x, clip_y], zero_brick], axis=0)
        fetched = source[send_lists[clip_x, clip_y, k]]
        fetched = jnp.where(inside, fetched, jnp.zeros_like(fetched))
        blocks.append(brick_faces(fetched))
    blocks.append(jnp.zeros((1, 6) + fields.shape[4:], fields.dtype))
    return jnp.concatenate(blocks, axis=0)

def reference(features, cotangent, kernel_weight, conv_bias, send_lists, kernel_map):
    flipped = jnp.transpose(kernel_weight[::-1, ::-1, ::-1], (0, 1, 2, 4, 3))
    device_ids = jnp.arange(N_GX * N_GY, dtype=jnp.int32)

    def forward(device_id):
        row_pos = device_id // N_GY
        col_pos = device_id % N_GY
        padded = assemble(features[row_pos, col_pos], device_table(features, send_lists, device_id), kernel_map[row_pos, col_pos])
        linear = conv_valid(padded, kernel_weight) + conv_bias
        logistic = jax.nn.sigmoid(linear)
        activated = (linear * logistic).astype(jnp.bfloat16)
        slope_grad = (cotangent[row_pos, col_pos].astype(jnp.float32) * logistic * (1.0 + linear * (1.0 - logistic))).astype(jnp.bfloat16)
        return (activated, slope_grad)
    activated, slopes = lax.map(forward, device_ids)
    activated = activated.reshape(features.shape)
    slopes = slopes.reshape(features.shape)

    def backward(totals, device_id):
        row_pos = device_id // N_GY
        col_pos = device_id % N_GY
        brick_map = kernel_map[row_pos, col_pos]
        padded = assemble(features[row_pos, col_pos], device_table(features, send_lists, device_id), brick_map)
        grad_padded = assemble(slopes[row_pos, col_pos], device_table(slopes, send_lists, device_id), brick_map)
        input_grad = conv_valid(grad_padded, flipped).astype(jnp.bfloat16)
        weight_part = weight_terms(padded, slopes[row_pos, col_pos])
        bias_part = lax.optimization_barrier(jnp.sum(slopes[row_pos, col_pos].astype(jnp.float32), axis=(0, 1, 2, 3)))
        return ((totals[0] + weight_part, totals[1] + bias_part), input_grad)
    channels = features.shape[-1]
    start_totals = (jnp.zeros((3, 3, 3, channels, channels), jnp.float32), jnp.zeros((channels,), jnp.float32))
    sums, input_grads = lax.scan(backward, start_totals, device_ids)
    factor = 1.0 / math.sqrt(VOXELS)
    return (activated, input_grads.reshape(features.shape), sums[0] * factor, sums[1] * factor)
```

```python
import functools
import math

import jax
import jax.numpy as jnp
from jax import lax
from jax.experimental import pallas as pl
from jax.experimental.pallas import tpu as pltpu
from jax.sharding import PartitionSpec as P

MESH = pl.DeviceIdType.MESH
F32, BF16 = jnp.float32, jnp.bfloat16
DIRECTIONS = ((-1, -1), (-1, 0), (-1, 1), (0, -1), (0, 1), (1, -1), (1, 0), (1, 1))
CH = 128
ENTRY = 52
SENT = 320
A_LOW, A_HIGH, E_LOW, E_HIGH, C_LOW, C_HIGH, EDGES = 0, 8, 16, 24, 32, 40, 48
SP, SQ, SR = 1600, 160, 16


def rows16(start):
    return pl.multiple_of(start, 16)


def natural_to_bricks(nat_ref, v32, put):
    def stage(b, _):
        block = nat_ref[b].astype(F32)
        for ae in range(64):
            v32[ae // 8, pl.ds((ae % 8) * 128 + b * 8, 8)] = block[ae * 8 : ae * 8 + 8]
        return 0

    lax.fori_loop(0, 16, stage, 0)

    def turn(ae, _):
        a, e = ae // 8, ae % 8
        for c in range(8):
            put(a, e, c, v32[a, pl.ds(e * 128 + c, 16, stride=8)])
        return 0

    lax.fori_loop(0, 64, turn, 0)


def bricks_to_natural(v32, nat_ref):
    def unstage(b, _):
        for ae in range(0, 64, 2):
            pair = [
                v32[(ae + k) // 8, pl.ds(((ae + k) % 8) * 128 + b * 8, 8)] for k in range(2)
            ]
            nat_ref[b, ae * 8 : ae * 8 + 16] = jnp.concatenate(pair, axis=0).astype(BF16)
        return 0

    lax.fori_loop(0, 16, unstage, 0)


def own_table(x32, t32, faces):
    def one(b, _):
        base = b * ENTRY
        for low, p in ((A_LOW, 1), (A_HIGH, 8)):
            for e in range(8):
                t32[base + low + e] = x32[pl.ds(p * SP + (1 + e) * SQ + SR + b, 8, stride=SR)]
        for low, q in ((E_LOW, 1), (E_HIGH, 8)):
            for a in range(8):
                t32[base + low + a] = x32[pl.ds((1 + a) * SP + q * SQ + SR + b, 8, stride=SR)]
        for low, r in ((C_LOW, 1), (C_HIGH, 8)):
            for a in range(8):
                t32[base + low + a] = x32[pl.ds((1 + a) * SP + SQ + r * SR + b, 8, stride=SQ)]
        for n, (q, r) in enumerate(((1, 1), (1, 8), (8, 1), (8, 8))):
            t32[base + EDGES + n] = x32[pl.ds(SP + q * SQ + r * SR + b, 8, stride=SP)]
        faces[b, 0:128] = t32[pl.ds(base, 16)].reshape(128, CH).astype(BF16)
        for n, low in enumerate((E_LOW, E_HIGH, C_LOW, C_HIGH)):
            lines = t32[pl.ds(base + low + 1, 6)].reshape(48, CH)
            faces[b, 128 + 48 * n : 176 + 48 * n] = lines.astype(BF16)
        return 0

    lax.fori_loop(0, 16, one, 0)


def received_table(received, t32, wide):
    def one(n, _):
        base = (16 + n) * ENTRY
        k, r = n // 4, n % 4
        sides = received[k, r, 0:128].astype(F32)
        wide[0:128] = sides
        t32[pl.ds(base, 16)] = sides.reshape(16, 8, CH)
        for m, low in enumerate((E_LOW, E_HIGH, C_LOW, C_HIGH)):
            lines = received[k, r, 128 + 48 * m : 176 + 48 * m].astype(F32)
            t32[pl.ds(base + low + 1, 6)] = lines.reshape(6, 8, CH)
            if m < 2:
                wide[136 + 64 * m : 184 + 64 * m] = lines
        for a, side in ((0, 0), (7, 64)):
            low, high = wide[side : side + 8], wide[side + 56 : side + 64]
            t32[base + E_LOW + a] = low
            t32[base + E_HIGH + a] = high
            wide[128 + 8 * a : 136 + 8 * a] = low
            wide[192 + 8 * a : 200 + 8 * a] = high
            t32[base + C_LOW + a] = wide[pl.ds(side, 8, stride=8)]
            t32[base + C_HIGH + a] = wide[pl.ds(side + 7, 8, stride=8)]
        for m, start in enumerate((128, 135, 192, 199)):
            t32[base + EDGES + m] = wide[pl.ds(start, 8, stride=8)]
        return 0

    lax.fori_loop(0, 32, one, 0)
    t32[pl.ds(48 * ENTRY, ENTRY)] = jnp.zeros((ENTRY, 8, CH), F32)


def rim(kmap, t32, x32, x):
    def one(b, _):
        for o in range(27):
            a, e, c = o // 9 - 1, o // 3 % 3 - 1, o % 3 - 1
            if a == e == c == 0:
                continue
            base = kmap[b, o] * ENTRY
            p, q, r = [1 + 8 * (s > 0) - (s < 0) for s in (a, e, c)]
            dest = p * SP + q * SQ + r * SR + b
            fe, fc = 7 * (e < 0), 7 * (c < 0)
            if a != 0:
                side = base + (A_HIGH if a < 0 else A_LOW)
                if e == 0 and c == 0:
                    for n in range(8):
                        x32[pl.ds(dest + n * SQ, 8, stride=SR)] = t32[side + n]
                elif c == 0:
                    x32[pl.ds(dest, 8, stride=SR)] = t32[side + fe]
                elif e == 0:
                    line = base + (C_HIGH if c < 0 else C_LOW) + 7 * (a < 0)
                    x32[pl.ds(dest, 8, stride=SQ)] = t32[line]
                else:
                    x32[pl.ds(dest, 1)] = t32[side + fe][fc : fc + 1]
            elif e != 0:
                side = base + (E_HIGH if e < 0 else E_LOW)
                if c == 0:
                    for n in range(8):
                        x32[pl.ds(dest + n * SP, 8, stride=SR)] = t32[side + n]
                else:
                    x32[pl.ds(dest, 8, stride=SP)] = t32[base + EDGES + 2 * (e < 0) + (c < 0)]
            else:
                side = base + (C_HIGH if c < 0 else C_LOW)
                for n in range(8):
                    x32[pl.ds(dest + n * SP, 8, stride=SQ)] = t32[side + n]
        return 0

    lax.fori_loop(0, 16, one, 0)

    def pack(p, q, r):
        x[p, q, r] = x32[pl.ds(rows16(p * SP + q * SQ + r * SR), 16)].astype(BF16)

    def line(q, _):
        for p in (0, 9):
            for r in range(10):
                pack(p, q, r)
        return 0

    lax.fori_loop(0, 10, line, 0)

    def ring(p, _):
        for q in (0, 9):
            for r in range(10):
                pack(p, q, r)
        for q in range(1, 9):
            for r in (0, 9):
                pack(p, q, r)
        return 0

    lax.fori_loop(1, 9, ring, 0)


def wide_weights(w, w2, back):
    zero = jnp.zeros((CH, CH), BF16)
    for e in range(3):
        for c in range(3):
            for k, j in ((0, 1), (3, 0)):
                w2[e, (c * 4 + k) * CH : (c * 4 + k + 1) * CH, j * CH : (j + 1) * CH] = zero
            for a in range(3):
                if back:
                    tap = w[(2 - a) * 9 + (2 - e) * 3 + 2 - c].astype(F32).T.astype(BF16)
                else:
                    tap = w[a * 9 + e * 3 + c]
                for j in range(2):
                    k = a + j
                    w2[e, (c * 4 + k) * CH : (c * 4 + k + 1) * CH, j * CH : (j + 1) * CH] = tap


def conv_pair(x, w2, i):
    acc = None
    for e in range(3):
        parts = [
            x[2 * i + k, e : e + 8, c : c + 8].reshape(1024, CH)
            for c in range(3)
            for k in range(4)
        ]
        term = jnp.dot(jnp.concatenate(parts, axis=1), w2[e], preferred_element_type=F32)
        acc = term if acc is None else acc + term
    return acc


def inside(i, j):
    return (i >= 0) & (i < lax.axis_size("gx")) & (j >= 0) & (j < lax.axis_size("gy"))


def greet_neighbours(barrier):
    i, j = lax.axis_index("gx"), lax.axis_index("gy")
    count = jnp.int32(0)
    for dx, dy in DIRECTIONS:
        there = inside(i + dx, j + dy)
        count += there.astype(jnp.int32)

        @pl.when(there)
        def _():
            pl.semaphore_signal(
                barrier, inc=1, device_id=(i + dx, j + dy), device_id_type=MESH
            )

    return count


def pack_lists(lists, faces, sending):
    for k in range(8):
        for r in range(4):
            sending[k, r] = faces[jnp.minimum(lists[k, r], 15)]


def halo_copy(k, sending, received, send_sem, recv_sem):
    i, j = lax.axis_index("gx"), lax.axis_index("gy")
    dx, dy = DIRECTIONS[k]
    return pltpu.make_async_remote_copy(
        src_ref=sending.at[k],
        dst_ref=received.at[k],
        send_sem=send_sem.at[k],
        recv_sem=recv_sem.at[k],
        device_id=(i + dx, j + dy),
        device_id_type=MESH,
    )


ORDER = (0, 2, 5, 7, 3, 4, 1, 6)


def start_halo(*halo):
    i, j = lax.axis_index("gx"), lax.axis_index("gy")
    for k in ORDER:
        dx, dy = DIRECTIONS[k]

        @pl.when(inside(i + dx, j + dy))
        def _():
            halo_copy(k, *halo).start()


def wait_halo(*halo):
    i, j = lax.axis_index("gx"), lax.axis_index("gy")
    for k in ORDER:
        dx, dy = DIRECTIONS[k]

        @pl.when(inside(i - dx, j - dy))
        def _():
            halo_copy(k, *halo).wait_recv()


def wait_halo_sent(*halo):
    i, j = lax.axis_index("gx"), lax.axis_index("gy")
    for k in ORDER:
        dx, dy = DIRECTIONS[k]

        @pl.when(inside(i + dx, j + dy))
        def _():
            halo_copy(k, *halo).wait_send()


def forward_kernel(
    vol, cot, w, bias, lists, kmap, act, slopes, x,
    v32, x32, t32, wide, ct, faces, sending, received, w2, acc, send_sem, recv_sem,
):
    halo = (sending, received, send_sem, recv_sem)
    barrier = pltpu.get_barrier_semaphore()
    count = greet_neighbours(barrier)

    def put_x(a, e, c, v):
        x32[pl.ds(rows16((1 + a) * SP + (1 + e) * SQ + (1 + c) * SR), 16)] = v
        x[1 + a, 1 + e, 1 + c] = v.astype(BF16)

    natural_to_bricks(vol, v32, put_x)
    own_table(x32, t32, faces)
    pack_lists(lists, faces, sending)
    pl.semaphore_wait(barrier, count)
    start_halo(*halo)

    def put_cot(a, e, c, v):
        ct[pl.ds(rows16((a * 64 + e * 8 + c) * 16), 16)] = v

    natural_to_bricks(cot, v32, put_cot)
    wide_weights(w, w2, False)
    wait_halo(*halo)
    received_table(received, t32, wide)
    rim(kmap, t32, x32, x)

    def pair(i, _):
        acc[...] = conv_pair(x, w2, i)
        for j in range(2):

            def finish(e, _):
                a = 2 * i + j
                linear = acc[pl.ds(rows16(e * 128), 128), j * CH : (j + 1) * CH] + bias[...]
                s = 1.0 / (1.0 + jnp.exp(-linear))
                activated = linear * s
                for c in range(8):
                    v32[a, pl.ds(e * 128 + c, 16, stride=8)] = activated[c * 16 : c * 16 + 16]
                slope = (
                    ct[pl.ds(rows16(a * 1024 + e * 128), 128)]
                    * s
                    * (1.0 + linear * (1.0 - s))
                )
                slopes[pl.ds((a * 8 + e) * 8, 8)] = slope.astype(BF16).reshape(8, 16, CH)
                return 0

            lax.fori_loop(0, 8, finish, 0)
        return 0

    lax.fori_loop(0, 4, pair, 0)
    bricks_to_natural(v32, act)
    wait_halo_sent(*halo)


def forward(vol, cot, w, bias, lists, kmap):
    vm = pl.BlockSpec(memory_space=pltpu.VMEM)
    sm = pl.BlockSpec(memory_space=pltpu.SMEM)
    return pl.pallas_call(
        forward_kernel,
        out_shape=(
            jax.ShapeDtypeStruct((16, 512, CH), BF16),
            jax.ShapeDtypeStruct((512, 16, CH), BF16),
            jax.ShapeDtypeStruct((10, 10, 10, 16, CH), BF16),
        ),
        in_specs=[vm, vm, vm, vm, sm, sm],
        out_specs=(vm, vm, vm),
        scratch_shapes=[
            pltpu.VMEM((8, 1024, CH), F32),
            pltpu.VMEM((16000, CH), F32),
            pltpu.VMEM((49 * ENTRY, 8, CH), F32),
            pltpu.VMEM((256, CH), F32),
            pltpu.VMEM((8192, CH), F32),
            pltpu.VMEM((16, SENT, CH), BF16),
            pltpu.VMEM((8, 4, SENT, CH), BF16),
            pltpu.VMEM((8, 4, SENT, CH), BF16),
            pltpu.VMEM((3, 12 * CH, 2 * CH), BF16),
            pltpu.VMEM((1024, 2 * CH), F32),
            pltpu.SemaphoreType.DMA((8,)),
            pltpu.SemaphoreType.DMA((8,)),
        ],
        compiler_params=pltpu.CompilerParams(
            collective_id=0, has_side_effects=True, vmem_limit_bytes=62 * 2**20
        ),
        name="forward",
    )(vol, cot, w, bias, lists, kmap)


ROWS = 3584
HALF = ROWS // 2
SHARE = HALF // 16


def place():
    i = lax.axis_index("gx")
    return i // 2, i % 2, lax.axis_index("gy")


def sibling_copy(src, dst, sems, n):
    z, core, j = place()
    return pltpu.make_async_remote_copy(
        src_ref=src, dst_ref=dst, send_sem=sems.at[0, n], recv_sem=sems.at[1, n],
        device_id=(2 * z + 1 - core, j), device_id_type=MESH,
    )


def plane_copy(src, dst, sems, d):
    z, core, j = place()
    return pltpu.make_async_remote_copy(
        src_ref=src, dst_ref=dst, send_sem=sems.at[0, d], recv_sem=sems.at[1, d],
        device_id=(2 * z + core, (j + d) % 16), device_id_type=MESH,
    )


def column_copy(src, dst, sems, d):
    z, core, j = place()
    return pltpu.make_async_remote_copy(
        src_ref=src, dst_ref=dst, send_sem=sems.at[0, d], recv_sem=sems.at[1, d],
        device_id=(2 * ((z + d) % 4) + core, j), device_id_type=MESH,
    )


def greet_summers(barrier):
    z, core, j = place()

    def greet(i, j):
        pl.semaphore_signal(barrier, inc=1, device_id=(i, j), device_id_type=MESH)

    greet(2 * z + 1 - core, j)
    for d in range(1, 16):
        greet(2 * z + core, (j + d) % 16)
    for d in range(1, 4):
        greet(2 * ((z + d) % 4) + core, j)
    return 19


def backward_kernel(
    x, slopes, w, lists, kmap, grad, total,
    v32, g, x32, t32, wide, faces, sending, received, w2, acc, gt,
    d32, d16, from_sibling, h32, h16, from_plane, column, share, gathered, whole,
    send_sem, recv_sem, sib_sems, out_sems, col_sems, in_sems,
):
    halo = (sending, received, send_sem, recv_sem)
    z, core, j = place()
    barrier = pltpu.get_barrier_semaphore()
    count = greet_neighbours(barrier) + greet_summers(barrier)

    def spread(ae, total):
        block = slopes[pl.ds(ae * 8, 8)]
        a, e = ae // 8, ae % 8
        g[1 + a, 1 + e, 1:9] = block
        wide = block.astype(F32).reshape(128, CH)
        x32[pl.ds(rows16((1 + a) * SP + (1 + e) * SQ + SR), 128)] = wide
        return total + wide

    sums = lax.fori_loop(0, 64, spread, jnp.zeros((128, CH), F32))
    d32[27 * CH :] = jnp.concatenate(
        [jnp.sum(sums, axis=0, keepdims=True), jnp.zeros((127, CH), F32)], axis=0
    )
    own_table(x32, t32, faces)
    pack_lists(lists, faces, sending)
    pl.semaphore_wait(barrier, count)
    start_halo(*halo)

    def turn(n, _):
        for m in range(8):
            block = slopes[pl.ds(n * 64 + m * 8, 8)].astype(F32).reshape(128, CH)
            gt[n // 2, pl.ds(rows16((n % 2) * CH), CH), m * 128 : m * 128 + 128] = (
                block.T.astype(BF16)
            )
        return 0

    lax.fori_loop(0, 8, turn, 0)

    def tap(t, _):
        e, c = t // 3, t % 3
        parts = [
            jnp.concatenate(
                [x[2 * i + k, pl.ds(e, 8), pl.ds(c, 8)].reshape(1024, CH) for i in range(4)],
                axis=0,
            )
            for k in range(4)
        ]
        terms = jnp.dot(
            jnp.concatenate([gt[i] for i in range(4)], axis=1),
            jnp.concatenate(parts, axis=1),
            preferred_element_type=F32,
        )
        for a in range(3):
            term = (
                terms[:CH, a * CH : (a + 1) * CH] + terms[CH:, (a + 1) * CH : (a + 2) * CH]
            )
            d32[pl.ds(rows16((a * 9 + t) * CH), CH)] = term.T
        return 0

    lax.fori_loop(0, 9, tap, 0)
    mine = pl.ds(rows16(core * HALF), HALF)
    other = pl.ds(rows16((1 - core) * HALF), HALF)
    d16[...] = d32[other].astype(BF16)
    sibling_copy(d16, from_sibling, sib_sems, 0).start()
    wide_weights(w, w2, True)
    wait_halo(*halo)
    received_table(received, t32, wide)
    rim(kmap, t32, x32, g)

    sibling_copy(d16, from_sibling, sib_sems, 0).wait()
    h32[...] = d32[mine] + from_sibling[...].astype(F32)
    h16[...] = h32[...].astype(BF16).reshape(16, SHARE, CH)
    for d in range(1, 16):
        plane_copy(h16.at[(j + d) % 16], from_plane.at[d - 1], out_sems, d).start()

    def conv(lo, hi):
        def pair(i, _):
            acc[...] = conv_pair(g, w2, i)
            for n in range(2):

                def finish(e, _):
                    for c in range(8):
                        v32[2 * i + n, pl.ds(e * 128 + c, 16, stride=8)] = acc[
                            pl.ds(rows16(e * 128 + c * 16), 16), n * CH : (n + 1) * CH
                        ]
                    return 0

                lax.fori_loop(0, 8, finish, 0)
            return 0

        lax.fori_loop(lo, hi, pair, 0)

    conv(0, 2)
    for d in range(1, 16):
        plane_copy(h16.at[(j + d) % 16], from_plane.at[d - 1], out_sems, d).wait()
    part = h32[pl.ds(rows16(j * SHARE), SHARE)]
    for d in range(1, 16):
        part = part + from_plane[d - 1].astype(F32)
    column[z] = part.astype(BF16)
    for d in range(1, 4):
        column_copy(column.at[z], column.at[z], col_sems, d).start()
    conv(2, 3)
    for d in range(1, 4):
        column_copy(column.at[z], column.at[z], col_sems, d).wait()
    part = column[0].astype(F32)
    for n in range(1, 4):
        part = part + column[n].astype(F32)
    voxels = lax.axis_size("gx") * lax.axis_size("gy") * 8192
    share[...] = (part * (1.0 / math.sqrt(voxels))).astype(BF16)
    gathered[j] = share[...]
    for d in range(1, 16):
        plane_copy(share, gathered.at[j], in_sems, d).start()
    conv(3, 4)
    for d in range(1, 16):
        plane_copy(share, gathered.at[j], in_sems, d).wait()
    sibling_copy(gathered, whole.at[core], sib_sems, 1).start()
    bricks_to_natural(v32, grad)
    total[pl.ds(rows16(core * HALF), HALF)] = gathered[...].reshape(HALF, CH).astype(F32)
    sibling_copy(gathered, whole.at[core], sib_sems, 1).wait()
    total[pl.ds(rows16((1 - core) * HALF), HALF)] = (
        whole[1 - core].reshape(HALF, CH).astype(F32)
    )
    wait_halo_sent(*halo)


def backward(x, slopes, w, lists, kmap):
    vm = pl.BlockSpec(memory_space=pltpu.VMEM)
    sm = pl.BlockSpec(memory_space=pltpu.SMEM)
    return pl.pallas_call(
        backward_kernel,
        out_shape=(
            jax.ShapeDtypeStruct((16, 512, CH), BF16),
            jax.ShapeDtypeStruct((ROWS, CH), F32),
        ),
        in_specs=[vm, vm, vm, sm, sm],
        out_specs=(vm, vm),
        scratch_shapes=[
            pltpu.VMEM((8, 1024, CH), F32),
            pltpu.VMEM((10, 10, 10, 16, CH), BF16),
            pltpu.VMEM((16000, CH), F32),
            pltpu.VMEM((49 * ENTRY, 8, CH), F32),
            pltpu.VMEM((256, CH), F32),
            pltpu.VMEM((16, SENT, CH), BF16),
            pltpu.VMEM((8, 4, SENT, CH), BF16),
            pltpu.VMEM((8, 4, SENT, CH), BF16),
            pltpu.VMEM((3, 12 * CH, 2 * CH), BF16),
            pltpu.VMEM((1024, 2 * CH), F32),
            pltpu.VMEM((4, 2 * CH, 1024), BF16),
            pltpu.VMEM((ROWS, CH), F32),
            pltpu.VMEM((HALF, CH), BF16),
            pltpu.VMEM((HALF, CH), BF16),
            pltpu.VMEM((HALF, CH), F32),
            pltpu.VMEM((16, SHARE, CH), BF16),
            pltpu.VMEM((15, SHARE, CH), BF16),
            pltpu.VMEM((4, SHARE, CH), BF16),
            pltpu.VMEM((SHARE, CH), BF16),
            pltpu.VMEM((16, SHARE, CH), BF16),
            pltpu.VMEM((2, 16, SHARE, CH), BF16),
            pltpu.SemaphoreType.DMA((8,)),
            pltpu.SemaphoreType.DMA((8,)),
            pltpu.SemaphoreType.DMA((2, 2)),
            pltpu.SemaphoreType.DMA((2, 16)),
            pltpu.SemaphoreType.DMA((2, 4)),
            pltpu.SemaphoreType.DMA((2, 16)),
        ],
        compiler_params=pltpu.CompilerParams(
            collective_id=1, has_side_effects=True, vmem_limit_bytes=62 * 2**20
        ),
        name="backward",
    )(x, slopes, w, lists, kmap)


def shards(features, cotangent, kernel_weight, conv_bias, send_lists, kernel_map):
    w = kernel_weight.reshape(27, CH, CH)
    lists, kmap = send_lists[0, 0], kernel_map[0, 0]
    act, slopes, x = forward(
        features.reshape(16, 512, CH),
        cotangent.reshape(16, 512, CH),
        w,
        conv_bias.reshape(1, CH),
        lists,
        kmap,
    )
    grad, total = backward(x, slopes, w, lists, kmap)
    return (
        act.reshape(features.shape),
        grad.reshape(features.shape),
        total[: 27 * CH].reshape(3, 3, 3, CH, CH),
        total[27 * CH],
    )


def solution(mesh):
    block = P("gx", "gy", None, None, None, None, None)
    return jax.shard_map(
        shards,
        mesh=mesh,
        in_specs=(block, block, P(), P(), P("gx", "gy", None, None), P("gx", "gy", None, None)),
        out_specs=(block, block, P(), P()),
        check_vma=False,
    )
```

```python
import functools
import math

import jax
import jax.numpy as jnp
from jax import lax
from jax.experimental import pallas as pl
from jax.experimental.pallas import tpu as pltpu
from jax.sharding import PartitionSpec as P

MESH = pl.DeviceIdType.MESH
F32, BF16 = jnp.float32, jnp.bfloat16
DIRECTIONS = ((-1, -1), (-1, 0), (-1, 1), (0, -1), (0, 1), (1, -1), (1, 0), (1, 1))
CH = 128
ENTRY = 52
SENT = 320
A_LOW, A_HIGH, E_LOW, E_HIGH, C_LOW, C_HIGH, EDGES = 0, 8, 16, 24, 32, 40, 48
SP, SQ, SR = 1600, 160, 16


def rows16(start):
    return pl.multiple_of(start, 16)


def natural_to_bricks(nat_ref, stage_ref, put):
    def stage(b, _):
        block = nat_ref[b].astype(F32)
        for ae in range(64):
            stage_ref[pl.ds(ae * 128 + pl.multiple_of(b * 8, 8), 8)] = block[
                ae * 8 : ae * 8 + 8
            ]
        return 0

    lax.fori_loop(0, 16, stage, 0)

    def turn(ae, _):
        for c in range(8):
            put(ae // 8, ae % 8, c, stage_ref[pl.ds(ae * 128 + c, 16, stride=8)])
        return 0

    lax.fori_loop(0, 64, turn, 0)


def bricks_to_natural(stage_ref, nat_ref):
    def unstage(b, _):
        for ae in range(0, 64, 2):
            pair = [
                stage_ref[pl.ds((ae + k) * 128 + pl.multiple_of(b * 8, 8), 8)] for k in range(2)
            ]
            nat_ref[b, ae * 8 : ae * 8 + 16] = jnp.concatenate(pair, axis=0).astype(BF16)
        return 0

    lax.fori_loop(0, 16, unstage, 0)


def own_table(x32, t32, faces):
    def one(b, _):
        base = b * ENTRY
        for low, p in ((A_LOW, 1), (A_HIGH, 8)):
            for e in range(8):
                t32[base + low + e] = x32[pl.ds(p * SP + (1 + e) * SQ + SR + b, 8, stride=SR)]
        for low, q in ((E_LOW, 1), (E_HIGH, 8)):
            for a in range(8):
                t32[base + low + a] = x32[pl.ds((1 + a) * SP + q * SQ + SR + b, 8, stride=SR)]
        for low, r in ((C_LOW, 1), (C_HIGH, 8)):
            for a in range(8):
                t32[base + low + a] = x32[pl.ds((1 + a) * SP + SQ + r * SR + b, 8, stride=SQ)]
        for n, (q, r) in enumerate(((1, 1), (1, 8), (8, 1), (8, 8))):
            t32[base + EDGES + n] = x32[pl.ds(SP + q * SQ + r * SR + b, 8, stride=SP)]
        faces[b, 0:128] = t32[pl.ds(base, 16)].reshape(128, CH).astype(BF16)
        for n, low in enumerate((E_LOW, E_HIGH, C_LOW, C_HIGH)):
            lines = t32[pl.ds(base + low + 1, 6)].reshape(48, CH)
            faces[b, 128 + 48 * n : 176 + 48 * n] = lines.astype(BF16)
        return 0

    lax.fori_loop(0, 16, one, 0)


def received_table(received, t32, wide):
    def one(n, _):
        base = (16 + n) * ENTRY
        k, r = n // 4, n % 4
        sides = received[k, r, 0:128].astype(F32)
        wide[0:128] = sides
        t32[pl.ds(base, 16)] = sides.reshape(16, 8, CH)
        for m, low in enumerate((E_LOW, E_HIGH, C_LOW, C_HIGH)):
            lines = received[k, r, 128 + 48 * m : 176 + 48 * m].astype(F32)
            t32[pl.ds(base + low + 1, 6)] = lines.reshape(6, 8, CH)
            if m < 2:
                wide[136 + 64 * m : 184 + 64 * m] = lines
        for a, side in ((0, 0), (7, 64)):
            low, high = wide[side : side + 8], wide[side + 56 : side + 64]
            t32[base + E_LOW + a] = low
            t32[base + E_HIGH + a] = high
            wide[128 + 8 * a : 136 + 8 * a] = low
            wide[192 + 8 * a : 200 + 8 * a] = high
            t32[base + C_LOW + a] = wide[pl.ds(side, 8, stride=8)]
            t32[base + C_HIGH + a] = wide[pl.ds(side + 7, 8, stride=8)]
        for m, start in enumerate((128, 135, 192, 199)):
            t32[base + EDGES + m] = wide[pl.ds(start, 8, stride=8)]
        return 0

    lax.fori_loop(0, 32, one, 0)
    t32[pl.ds(48 * ENTRY, ENTRY)] = jnp.zeros((ENTRY, 8, CH), F32)


def rim(kmap, t32, x32, planes, x):
    a_planes, e_planes, c_planes = planes

    def one(b, _):
        for o in range(27):
            a, e, c = o // 9 - 1, o // 3 % 3 - 1, o % 3 - 1
            if a == e == c == 0:
                continue
            base = kmap[b, o] * ENTRY
            p, q, r = [1 + 8 * (s > 0) - (s < 0) for s in (a, e, c)]
            dest = p * SP + q * SQ + r * SR + b
            fe, fc = 7 * (e < 0), 7 * (c < 0)
            if a != 0:
                side = base + (A_HIGH if a < 0 else A_LOW)
                if e == 0 and c == 0:
                    for n in range(8):
                        x32[pl.ds(dest + n * SQ, 8, stride=SR)] = t32[side + n]
                elif c == 0:
                    x32[pl.ds(dest, 8, stride=SR)] = t32[side + fe]
                elif e == 0:
                    line = base + (C_HIGH if c < 0 else C_LOW) + 7 * (a < 0)
                    x32[pl.ds(dest, 8, stride=SQ)] = t32[line]
                else:
                    x32[pl.ds(dest, 1)] = t32[side + fe][fc : fc + 1]
            elif e != 0:
                side = base + (E_HIGH if e < 0 else E_LOW)
                if c == 0:
                    for n in range(8):
                        x32[pl.ds(dest + n * SP, 8, stride=SR)] = t32[side + n]
                else:
                    x32[pl.ds(dest, 8, stride=SP)] = t32[base + EDGES + 2 * (e < 0) + (c < 0)]
            else:
                side = base + (C_HIGH if c < 0 else C_LOW)
                for n in range(8):
                    x32[pl.ds(dest + n * SP, 8, stride=SQ)] = t32[side + n]
        return 0

    lax.fori_loop(0, 16, one, 0)

    def pack(p, q, r):
        cell = x32[pl.ds(rows16(p * SP + q * SQ + r * SR), 16)].astype(BF16)
        if x is not None:
            x[p, q, r] = cell
        return cell

    def line(q, _):
        for side in range(2):
            for r in range(10):
                a_planes[side, q // 2, q % 2, r] = pack(9 * side, q, r)
        return 0

    lax.fori_loop(0, 10, line, 0)

    def ring(p, _):
        for side in range(2):
            for r in range(10):
                e_planes[side, p // 2, p % 2, r] = pack(p, 9 * side, r)
            for q in range(1, 9):
                c_planes[side, p // 2, p % 2, q] = pack(p, q, 9 * side)
        return 0

    lax.fori_loop(1, 9, ring, 0)


def clear_rims(planes, x, g):
    _, e_planes, c_planes = planes
    row = jnp.zeros((10, 16, CH), BF16)
    for side in range(2):
        for p in (0, 9):
            e_planes[side, p // 2, p % 2] = row
            c_planes[side, p // 2, p % 2] = row
        for p in range(1, 9):
            for q in (0, 9):
                c_planes[side, p // 2, p % 2, q] = row[0]

    def clear(n, _):
        for f in (x, g):
            for side in (0, 9):
                f[side, n] = row
                f[n, side] = row
                f[n, :, side] = row
        return 0

    lax.fori_loop(0, 10, clear, 0)


def wide_weights(w, w2, wa, back):
    zero = jnp.zeros((CH, CH), BF16)

    def put(ref, n, c, k, j, tap):
        ref[n, (c * 4 + k) * CH : (c * 4 + k + 1) * CH, j * CH : (j + 1) * CH] = tap

    for c in range(3):
        for k, j in ((0, 1), (3, 0)):
            for n in range(3):
                put(w2, n, c, k, j, zero)
            for n in range(2):
                put(wa, n, c, k, j, zero)
    for a in range(3):
        for e in range(3):
            for c in range(3):
                if back:
                    tap = w[(2 - a) * 9 + (2 - e) * 3 + 2 - c].astype(F32).T.astype(BF16)
                else:
                    tap = w[a * 9 + e * 3 + c]
                for j in range(2):
                    put(w2, e, c, a + j, j, tap)
                    if a != 1:
                        put(wa, a // 2, c, e + j, j, tap)


def conv_pair(x, w2, i):
    acc = None
    for e in range(3):
        parts = [
            x[2 * i + k, e : e + 8, c : c + 8].reshape(1024, CH)
            for c in range(3)
            for k in range(4)
        ]
        term = jnp.dot(jnp.concatenate(parts, axis=1), w2[e], preferred_element_type=F32)
        acc = term if acc is None else acc + term
    return acc


def inner_conv(x, w2, lin, lo, hi):
    def pair(i, _):
        result = conv_pair(x, w2, i)
        for j in range(2):
            lin[pl.ds(rows16((2 * i + j) * 1024), 1024)] = result[:, j * CH : (j + 1) * CH]
        return 0

    lax.fori_loop(lo, hi, pair, 0)


def rim_conv(planes, w2, wa, lin):
    a_planes, e_planes, c_planes = planes

    def windows(ref, side):
        parts = [
            ref[side, k // 2 : k // 2 + 4, k % 2, s : s + 8].reshape(512, CH)
            for s in range(3)
            for k in range(4)
        ]
        return jnp.concatenate(parts, axis=1)

    for side in range(2):
        near = 7 * side
        result = jnp.dot(windows(a_planes, side), wa[side], preferred_element_type=F32)
        for i in range(4):
            for j in range(2):
                at = near * 1024 + (2 * i + j) * 128
                lin[at : at + 128] += result[i * 128 : i * 128 + 128, j * CH : (j + 1) * CH]
        result = jnp.dot(windows(e_planes, side), w2[2 * side], preferred_element_type=F32)
        for i in range(4):
            for j in range(2):
                at = (2 * i + j) * 1024 + near * 128
                lin[at : at + 128] += result[i * 128 : i * 128 + 128, j * CH : (j + 1) * CH]
        taps = jnp.concatenate(
            [w2[e, 2 * side * 4 * CH : (2 * side + 1) * 4 * CH] for e in range(3)], axis=0
        )
        result = jnp.dot(windows(c_planes, side), taps, preferred_element_type=F32)
        for i in range(4):
            for j in range(2):
                for e in range(8):
                    at = (2 * i + j) * 1024 + e * 128 + near * 16
                    row = (i * 8 + e) * 16
                    lin[at : at + 16] += result[row : row + 16, j * CH : (j + 1) * CH]


def inside(i, j):
    return (i >= 0) & (i < lax.axis_size("gx")) & (j >= 0) & (j < lax.axis_size("gy"))


def greet_neighbours(barrier):
    i, j = lax.axis_index("gx"), lax.axis_index("gy")
    count = jnp.int32(0)
    for dx, dy in DIRECTIONS:
        there = inside(i + dx, j + dy)
        count += there.astype(jnp.int32)

        @pl.when(there)
        def _():
            pl.semaphore_signal(
                barrier, inc=1, device_id=(i + dx, j + dy), device_id_type=MESH
            )

    return count


def pack_lists(lists, faces, sending):
    for k in range(8):
        for r in range(4):
            sending[k, r] = faces[jnp.minimum(lists[k, r], 15)]


def halo_copy(k, sending, received, send_sem, recv_sem):
    i, j = lax.axis_index("gx"), lax.axis_index("gy")
    dx, dy = DIRECTIONS[k]
    return pltpu.make_async_remote_copy(
        src_ref=sending.at[k],
        dst_ref=received.at[k],
        send_sem=send_sem.at[k],
        recv_sem=recv_sem.at[k],
        device_id=(i + dx, j + dy),
        device_id_type=MESH,
    )


ORDER = (0, 2, 5, 7, 3, 4, 1, 6)


def start_halo(*halo):
    i, j = lax.axis_index("gx"), lax.axis_index("gy")
    for k in ORDER:
        dx, dy = DIRECTIONS[k]

        @pl.when(inside(i + dx, j + dy))
        def _():
            halo_copy(k, *halo).start()


def wait_halo(*halo):
    i, j = lax.axis_index("gx"), lax.axis_index("gy")
    for k in ORDER:
        dx, dy = DIRECTIONS[k]

        @pl.when(inside(i - dx, j - dy))
        def _():
            halo_copy(k, *halo).wait_recv()


def wait_halo_sent(*halo):
    i, j = lax.axis_index("gx"), lax.axis_index("gy")
    for k in ORDER:
        dx, dy = DIRECTIONS[k]

        @pl.when(inside(i + dx, j + dy))
        def _():
            halo_copy(k, *halo).wait_send()


ROWS = 3584
HALF = ROWS // 2
SHARE = HALF // 16


def place():
    i = lax.axis_index("gx")
    return i // 2, i % 2, lax.axis_index("gy")


def sibling_copy(src, dst, sems, n):
    z, core, j = place()
    return pltpu.make_async_remote_copy(
        src_ref=src, dst_ref=dst, send_sem=sems.at[0, n], recv_sem=sems.at[1, n],
        device_id=(2 * z + 1 - core, j), device_id_type=MESH,
    )


def plane_copy(src, dst, sems, d):
    z, core, j = place()
    return pltpu.make_async_remote_copy(
        src_ref=src, dst_ref=dst, send_sem=sems.at[0, d], recv_sem=sems.at[1, d],
        device_id=(2 * z + core, (j + d) % 16), device_id_type=MESH,
    )


def column_copy(src, dst, sems, d):
    z, core, j = place()
    return pltpu.make_async_remote_copy(
        src_ref=src, dst_ref=dst, send_sem=sems.at[0, d], recv_sem=sems.at[1, d],
        device_id=(2 * ((z + d) % 4) + core, j), device_id_type=MESH,
    )


def greet_summers(barrier):
    z, core, j = place()

    def greet(i, j):
        pl.semaphore_signal(barrier, inc=1, device_id=(i, j), device_id_type=MESH)

    greet(2 * z + 1 - core, j)
    for d in range(1, 16):
        greet(2 * z + core, (j + d) % 16)
    for d in range(1, 4):
        greet(2 * ((z + d) % 4) + core, j)
    return 19


def credit_neighbours(credit):
    i, j = lax.axis_index("gx"), lax.axis_index("gy")
    for dx, dy in DIRECTIONS:

        @pl.when(inside(i - dx, j - dy))
        def _():
            pl.semaphore_signal(
                credit, inc=1, device_id=(i - dx, j - dy), device_id_type=MESH
            )


def kernel(
    vol, cot, w, bias, lists, kmap, act, grad, weight_total, bias_total,
    nat, lin, x32, t32, wide, ct, faces, sending, received, x, g,
    a_planes, e_planes, c_planes, w2, wa, gt,
    d32, d16, from_sibling, h32, h16, from_plane, column, share, gathered, whole,
    send_sem, recv_sem, sib_sems, out_sems, col_sems, in_sems, own_sems, credit,
):
    halo = (sending, received, send_sem, recv_sem)
    planes = (a_planes, e_planes, c_planes)
    z, core, j = place()
    take_vol = pltpu.make_async_copy(vol, nat, own_sems.at[0])
    take_cot = pltpu.make_async_copy(cot, nat, own_sems.at[1])
    give_act = pltpu.make_async_copy(nat, act, own_sems.at[2])
    give_grad = pltpu.make_async_copy(nat, grad, own_sems.at[3])
    take_vol.start()
    barrier = pltpu.get_barrier_semaphore()
    neighbours = greet_neighbours(barrier)
    summers = greet_summers(barrier)

    def put_x(a, e, c, v):
        x32[pl.ds(rows16((1 + a) * SP + (1 + e) * SQ + (1 + c) * SR), 16)] = v
        x[1 + a, 1 + e, 1 + c] = v.astype(BF16)

    take_vol.wait()
    natural_to_bricks(nat, lin, put_x)
    take_cot.start()
    own_table(x32, t32, faces)
    pack_lists(lists, faces, sending)
    pl.semaphore_wait(barrier, neighbours + summers)
    start_halo(*halo)

    def put_cot(a, e, c, v):
        ct[pl.ds(rows16((a * 64 + e * 8 + c) * 16), 16)] = v.astype(BF16)

    take_cot.wait()
    natural_to_bricks(nat, lin, put_cot)
    wide_weights(w, w2, wa, False)
    clear_rims(planes, x, g)
    inner_conv(x, w2, lin, 0, 4)
    wait_halo(*halo)
    received_table(received, t32, wide)
    credit_neighbours(credit)
    rim(kmap, t32, x32, planes, x)
    rim_conv(planes, w2, wa, lin)

    def finish(ae, _):
        a, e = ae // 8, ae % 8
        rows = pl.ds(rows16(ae * 128), 128)
        linear = lin[rows] + bias[...]
        s = 1.0 / (1.0 + jnp.exp(-linear))
        activated = linear * s
        slope = ct[rows].astype(F32) * s * (1.0 + linear * (1.0 - s))
        for c in range(8):
            lin[pl.ds(ae * 128 + c, 16, stride=8)] = activated[c * 16 : c * 16 + 16]
        x32[pl.ds(rows16((1 + a) * SP + (1 + e) * SQ + SR), 128)] = slope
        g[1 + a, 1 + e, 1:9] = slope.astype(BF16).reshape(8, 16, CH)
        return 0

    lax.fori_loop(0, 64, finish, 0)
    wait_halo_sent(*halo)
    own_table(x32, t32, faces)
    pack_lists(lists, faces, sending)
    pl.semaphore_wait(credit, neighbours)
    start_halo(*halo)

    bricks_to_natural(lin, nat)
    give_act.start()

    def turn(n, sums):
        for m in range(8):
            block = g[1 + n, 1 + m, 1:9].astype(F32).reshape(128, CH)
            gt[n // 2, pl.ds(rows16((n % 2) * CH), CH), m * 128 : m * 128 + 128] = (
                block.T.astype(BF16)
            )
            sums = sums + block
        return sums

    sums = lax.fori_loop(0, 8, turn, jnp.zeros((128, CH), F32))
    d32[27 * CH :] = jnp.concatenate(
        [jnp.sum(sums, axis=0, keepdims=True), jnp.zeros((127, CH), F32)], axis=0
    )

    def tap(t, _):
        e, c = t // 3, t % 3
        parts = [
            jnp.concatenate(
                [x[2 * i + k, pl.ds(e, 8), pl.ds(c, 8)].reshape(1024, CH) for i in range(4)],
                axis=0,
            )
            for k in range(4)
        ]
        terms = jnp.dot(
            jnp.concatenate([gt[i] for i in range(4)], axis=1),
            jnp.concatenate(parts, axis=1),
            preferred_element_type=F32,
        )
        for a in range(3):
            term = (
                terms[:CH, a * CH : (a + 1) * CH] + terms[CH:, (a + 1) * CH : (a + 2) * CH]
            )
            d32[pl.ds(rows16((a * 9 + t) * CH), CH)] = term.T
        return 0

    lax.fori_loop(0, 9, tap, 0)
    mine = pl.ds(rows16(core * HALF), HALF)
    other = pl.ds(rows16((1 - core) * HALF), HALF)
    d16[...] = d32[other].astype(BF16)
    sibling_copy(d16, from_sibling, sib_sems, 0).start()
    wide_weights(w, w2, wa, True)
    inner_conv(g, w2, lin, 0, 1)

    sibling_copy(d16, from_sibling, sib_sems, 0).wait()
    h32[...] = d32[mine] + from_sibling[...].astype(F32)
    h16[...] = h32[...].astype(BF16).reshape(16, SHARE, CH)
    for d in range(1, 16):
        plane_copy(h16.at[(j + d) % 16], from_plane.at[d - 1], out_sems, d).start()
    inner_conv(g, w2, lin, 1, 4)
    for d in range(1, 16):
        plane_copy(h16.at[(j + d) % 16], from_plane.at[d - 1], out_sems, d).wait()
    part = h32[pl.ds(rows16(j * SHARE), SHARE)]
    for d in range(1, 16):
        part = part + from_plane[d - 1].astype(F32)
    column[z] = part.astype(BF16)
    for d in range(1, 4):
        column_copy(column.at[z], column.at[z], col_sems, d).start()
    wait_halo(*halo)
    received_table(received, t32, wide)
    for d in range(1, 4):
        column_copy(column.at[z], column.at[z], col_sems, d).wait()
    part = column[0].astype(F32)
    for n in range(1, 4):
        part = part + column[n].astype(F32)
    voxels = lax.axis_size("gx") * lax.axis_size("gy") * 8192
    share[...] = (part * (1.0 / math.sqrt(voxels))).astype(BF16)
    gathered[j] = share[...]
    for d in range(1, 16):
        plane_copy(share, gathered.at[j], in_sems, d).start()
    rim(kmap, t32, x32, planes, None)
    for d in range(1, 16):
        plane_copy(share, gathered.at[j], in_sems, d).wait()
    sibling_copy(gathered, whole.at[core], sib_sems, 1).start()
    whole[core] = gathered[...]
    rim_conv(planes, w2, wa, lin)

    def settle(ae, _):
        block = lin[pl.ds(rows16(ae * 128), 128)]
        for c in range(8):
            lin[pl.ds(ae * 128 + c, 16, stride=8)] = block[c * 16 : c * 16 + 16]
        return 0

    lax.fori_loop(0, 64, settle, 0)
    give_act.wait()
    bricks_to_natural(lin, nat)
    give_grad.start()
    sibling_copy(gathered, whole.at[core], sib_sems, 1).wait()
    weight_total[0:HALF] = whole[0].reshape(HALF, CH).astype(F32)
    last = whole[1].reshape(HALF, CH).astype(F32)
    weight_total[HALF:] = last[: 27 * CH - HALF]
    bias_total[...] = last[27 * CH - HALF : 27 * CH - HALF + 8]
    wait_halo_sent(*halo)
    give_grad.wait()


def layer(vol, cot, w, bias, lists, kmap):
    vm = pl.BlockSpec(memory_space=pltpu.VMEM)
    sm = pl.BlockSpec(memory_space=pltpu.SMEM)
    hbm = pl.BlockSpec(memory_space=pl.ANY)
    field = pltpu.VMEM((10, 10, 10, 16, CH), BF16)
    planes = pltpu.VMEM((2, 5, 2, 10, 16, CH), BF16)
    return pl.pallas_call(
        kernel,
        out_shape=(
            jax.ShapeDtypeStruct((16, 512, CH), BF16),
            jax.ShapeDtypeStruct((16, 512, CH), BF16),
            jax.ShapeDtypeStruct((27 * CH, CH), F32),
            jax.ShapeDtypeStruct((8, CH), F32),
        ),
        in_specs=[hbm, hbm, vm, vm, sm, sm],
        out_specs=(hbm, hbm, vm, vm),
        scratch_shapes=[
            pltpu.VMEM((16, 512, CH), BF16),
            pltpu.VMEM((8192, CH), F32),
            pltpu.VMEM((16000, CH), F32),
            pltpu.VMEM((49 * ENTRY, 8, CH), F32),
            pltpu.VMEM((256, CH), F32),
            pltpu.VMEM((8192, CH), BF16),
            pltpu.VMEM((16, SENT, CH), BF16),
            pltpu.VMEM((8, 4, SENT, CH), BF16),
            pltpu.VMEM((8, 4, SENT, CH), BF16),
            field,
            field,
            planes,
            planes,
            planes,
            pltpu.VMEM((3, 12 * CH, 2 * CH), BF16),
            pltpu.VMEM((2, 12 * CH, 2 * CH), BF16),
            pltpu.VMEM((4, 2 * CH, 1024), BF16),
            pltpu.VMEM((ROWS, CH), F32),
            pltpu.VMEM((HALF, CH), BF16),
            pltpu.VMEM((HALF, CH), BF16),
            pltpu.VMEM((HALF, CH), F32),
            pltpu.VMEM((16, SHARE, CH), BF16),
            pltpu.VMEM((15, SHARE, CH), BF16),
            pltpu.VMEM((4, SHARE, CH), BF16),
            pltpu.VMEM((SHARE, CH), BF16),
            pltpu.VMEM((16, SHARE, CH), BF16),
            pltpu.VMEM((2, 16, SHARE, CH), BF16),
            pltpu.SemaphoreType.DMA((8,)),
            pltpu.SemaphoreType.DMA((8,)),
            pltpu.SemaphoreType.DMA((2, 2)),
            pltpu.SemaphoreType.DMA((2, 16)),
            pltpu.SemaphoreType.DMA((2, 4)),
            pltpu.SemaphoreType.DMA((2, 16)),
            pltpu.SemaphoreType.DMA((4,)),
            pltpu.SemaphoreType.REGULAR,
        ],
        compiler_params=pltpu.CompilerParams(
            collective_id=0, has_side_effects=True, vmem_limit_bytes=63 * 2**20
        ),
        name="layer",
    )(vol, cot, w, bias, lists, kmap)


def shards(features, cotangent, kernel_weight, conv_bias, send_lists, kernel_map):
    act, grad, weight_total, bias_total = layer(
        features.reshape(16, 512, CH),
        cotangent.reshape(16, 512, CH),
        kernel_weight.reshape(27, CH, CH),
        conv_bias.reshape(1, CH),
        send_lists[0, 0],
        kernel_map[0, 0],
    )
    return (
        act.reshape(features.shape),
        grad.reshape(features.shape),
        weight_total.reshape(kernel_weight.shape),
        bias_total[0],
    )


def solution(mesh):
    block = P("gx", "gy", None, None, None, None, None)
    return jax.shard_map(
        shards,
        mesh=mesh,
        in_specs=(block, block, P(), P(), P("gx", "gy", None, None), P("gx", "gy", None, None)),
        out_specs=(block, block, P(), P()),
        check_vma=False,
    )
```

```python
import functools
import math

import jax
import jax.numpy as jnp
from jax import lax
from jax.experimental import pallas as pl
from jax.experimental.pallas import tpu as pltpu
from jax.sharding import PartitionSpec as P

MESH = pl.DeviceIdType.MESH
F32, BF16 = jnp.float32, jnp.bfloat16
DIRECTIONS = ((-1, -1), (-1, 0), (-1, 1), (0, -1), (0, 1), (1, -1), (1, 0), (1, 1))
CH = 128
ENTRY = 52
SENT = 320
A_LOW, A_HIGH, E_LOW, E_HIGH, C_LOW, C_HIGH, EDGES = 0, 8, 16, 24, 32, 40, 48
SP, SQ, SR = 1711, 171, 17
LINE = 136


def rows16(start):
    return pl.multiple_of(start, 16)


def natural_to_bricks(nat, x32):
    def stage(b, _):
        block = nat[b].astype(F32)
        for ae in range(64):
            at = (1 + ae // 8) * SP + (1 + ae % 8) * SQ + SR
            x32[pl.ds(at + b, 8, stride=SR)] = block[ae * 8 : ae * 8 + 8]
        return 0

    lax.fori_loop(0, 16, stage, 0)


def each_inner(x32, put):
    def plane(a, _):
        for e in range(8):
            for c in range(8):
                at = (1 + a) * SP + (1 + e) * SQ + (1 + c) * SR
                put(a, e, c, x32[pl.ds(at, 16)].astype(BF16))
        return 0

    lax.fori_loop(0, 8, plane, 0)


def bricks_to_natural(lin, nat):
    def unstage(b, _):
        for ae in range(0, 64, 2):
            pair = [lin[pl.ds((ae + k) * LINE + b, 8, stride=17)] for k in range(2)]
            nat[b, ae * 8 : ae * 8 + 16] = jnp.concatenate(pair, axis=0).astype(BF16)
        return 0

    lax.fori_loop(0, 16, unstage, 0)


def own_table(x32, t32, faces):
    def one(b, _):
        base = b * ENTRY
        for low, p in ((A_LOW, 1), (A_HIGH, 8)):
            for e in range(8):
                t32[base + low + e] = x32[pl.ds(p * SP + (1 + e) * SQ + SR + b, 8, stride=SR)]
        for low, q in ((E_LOW, 1), (E_HIGH, 8)):
            for a in range(8):
                t32[base + low + a] = x32[pl.ds((1 + a) * SP + q * SQ + SR + b, 8, stride=SR)]
        for low, r in ((C_LOW, 1), (C_HIGH, 8)):
            for a in range(8):
                t32[base + low + a] = x32[pl.ds((1 + a) * SP + SQ + r * SR + b, 8, stride=SQ)]
        for n, (q, r) in enumerate(((1, 1), (1, 8), (8, 1), (8, 8))):
            t32[base + EDGES + n] = x32[pl.ds(SP + q * SQ + r * SR + b, 8, stride=SP)]
        faces[b, 0:128] = t32[pl.ds(base, 16)].reshape(128, CH).astype(BF16)
        for n, low in enumerate((E_LOW, E_HIGH, C_LOW, C_HIGH)):
            lines = t32[pl.ds(base + low + 1, 6)].reshape(48, CH)
            faces[b, 128 + 48 * n : 176 + 48 * n] = lines.astype(BF16)
        return 0

    lax.fori_loop(0, 16, one, 0)


def received_table(received, t32, wide):
    def one(n, _):
        base = (16 + n) * ENTRY
        k, r = n // 4, n % 4
        sides = received[k, r, 0:128].astype(F32)
        wide[0:128] = sides
        t32[pl.ds(base, 16)] = sides.reshape(16, 8, CH)
        for m, low in enumerate((E_LOW, E_HIGH, C_LOW, C_HIGH)):
            lines = received[k, r, 128 + 48 * m : 176 + 48 * m].astype(F32)
            t32[pl.ds(base + low + 1, 6)] = lines.reshape(6, 8, CH)
            if m < 2:
                wide[136 + 64 * m : 184 + 64 * m] = lines
        for a, side in ((0, 0), (7, 64)):
            low, high = wide[side : side + 8], wide[side + 56 : side + 64]
            t32[base + E_LOW + a] = low
            t32[base + E_HIGH + a] = high
            wide[128 + 8 * a : 136 + 8 * a] = low
            wide[192 + 8 * a : 200 + 8 * a] = high
            t32[base + C_LOW + a] = wide[pl.ds(side, 8, stride=8)]
            t32[base + C_HIGH + a] = wide[pl.ds(side + 7, 8, stride=8)]
        for m, start in enumerate((128, 135, 192, 199)):
            t32[base + EDGES + m] = wide[pl.ds(start, 8, stride=8)]
        return 0

    lax.fori_loop(0, 32, one, 0)
    t32[pl.ds(48 * ENTRY, ENTRY)] = jnp.zeros((ENTRY, 8, CH), F32)


def rim(kmap, t32, x32, planes, x):
    a_planes, e_planes, c_planes = planes

    def one(b, _):
        for o in range(27):
            a, e, c = o // 9 - 1, o // 3 % 3 - 1, o % 3 - 1
            if a == e == c == 0:
                continue
            base = kmap[b, o] * ENTRY
            p, q, r = [1 + 8 * (s > 0) - (s < 0) for s in (a, e, c)]
            dest = p * SP + q * SQ + r * SR + b
            fe, fc = 7 * (e < 0), 7 * (c < 0)
            if a != 0:
                side = base + (A_HIGH if a < 0 else A_LOW)
                if e == 0 and c == 0:
                    for n in range(8):
                        x32[pl.ds(dest + n * SQ, 8, stride=SR)] = t32[side + n]
                elif c == 0:
                    x32[pl.ds(dest, 8, stride=SR)] = t32[side + fe]
                elif e == 0:
                    line = base + (C_HIGH if c < 0 else C_LOW) + 7 * (a < 0)
                    x32[pl.ds(dest, 8, stride=SQ)] = t32[line]
                else:
                    x32[pl.ds(dest, 1)] = t32[side + fe][fc : fc + 1]
            elif e != 0:
                side = base + (E_HIGH if e < 0 else E_LOW)
                if c == 0:
                    for n in range(8):
                        x32[pl.ds(dest + n * SP, 8, stride=SR)] = t32[side + n]
                else:
                    x32[pl.ds(dest, 8, stride=SP)] = t32[base + EDGES + 2 * (e < 0) + (c < 0)]
            else:
                side = base + (C_HIGH if c < 0 else C_LOW)
                for n in range(8):
                    x32[pl.ds(dest + n * SP, 8, stride=SQ)] = t32[side + n]
        return 0

    lax.fori_loop(0, 16, one, 0)

    def pack(p, q, r):
        cell = x32[pl.ds(p * SP + q * SQ + r * SR, 16)].astype(BF16)
        if x is not None:
            x[p, q, r] = cell
        return cell

    def line(q, _):
        for side in range(2):
            for r in range(10):
                a_planes[side, q // 2, q % 2, r] = pack(9 * side, q, r)
        return 0

    lax.fori_loop(0, 10, line, 0)

    def ring(p, _):
        for side in range(2):
            for r in range(10):
                e_planes[side, p // 2, p % 2, r] = pack(p, 9 * side, r)
            for q in range(1, 9):
                c_planes[side, p // 2, p % 2, q] = pack(p, q, 9 * side)
        return 0

    lax.fori_loop(1, 9, ring, 0)


def clear_rims(planes, x, g):
    _, e_planes, c_planes = planes
    row = jnp.zeros((10, 16, CH), BF16)
    for side in range(2):
        for p in (0, 9):
            e_planes[side, p // 2, p % 2] = row
            c_planes[side, p // 2, p % 2] = row
        for p in range(1, 9):
            for q in (0, 9):
                c_planes[side, p // 2, p % 2, q] = row[0]

    def clear(n, _):
        for f in (x, g):
            for side in (0, 9):
                f[side, n] = row
                f[n, side] = row
                f[n, :, side] = row
        return 0

    lax.fori_loop(0, 10, clear, 0)


def wide_weights(w, w2, wa, back):
    zero = jnp.zeros((CH, CH), BF16)

    def put(ref, n, c, k, j, tap):
        ref[n, (c * 4 + k) * CH : (c * 4 + k + 1) * CH, j * CH : (j + 1) * CH] = tap

    for c in range(3):
        for k, j in ((0, 1), (3, 0)):
            for n in range(3):
                put(w2, n, c, k, j, zero)
            for n in range(2):
                put(wa, n, c, k, j, zero)
    for a in range(3):
        for e in range(3):
            for c in range(3):
                if back:
                    tap = w[(2 - a) * 9 + (2 - e) * 3 + 2 - c].astype(F32).T.astype(BF16)
                else:
                    tap = w[a * 9 + e * 3 + c]
                for j in range(2):
                    put(w2, e, c, a + j, j, tap)
                    if a != 1:
                        put(wa, a // 2, c, e + j, j, tap)


def inner_conv(x, w2, wa, lin, lo, hi):
    def pair(i, _):
        both = None
        for e in range(3):
            parts = [
                x[2 * i + k, e : e + 8, c : c + 8].reshape(1024, CH)
                for c in range(3)
                for k in (1, 2)
            ]
            taps = jnp.concatenate(
                [w2[e, (c * 4 + 1) * CH : (c * 4 + 3) * CH] for c in range(3)], axis=0
            )
            term = jnp.dot(jnp.concatenate(parts, axis=1), taps, preferred_element_type=F32)
            both = term if both is None else both + term
        for j in range(2):
            plane = x[2 * i + 3 * j].reshape(5, 2, 10, 16, CH)
            parts = [
                plane[k // 2 : k // 2 + 4, k % 2, c : c + 8].reshape(512, CH)
                for c in range(3)
                for k in range(4)
            ]
            one = jnp.dot(jnp.concatenate(parts, axis=1), wa[j], preferred_element_type=F32)
            for e in range(8):
                at = pl.multiple_of(((2 * i + j) * 8 + e) * LINE, 8)
                lin[pl.ds(at, 128)] = (
                    both[e * 128 : e * 128 + 128, j * CH : (j + 1) * CH]
                    + one[e // 2 * 128 : e // 2 * 128 + 128, e % 2 * CH : (e % 2 + 1) * CH]
                )
        return 0

    lax.fori_loop(lo, hi, pair, 0)


def rim_conv(planes, w2, wa, lin):
    a_planes, e_planes, c_planes = planes

    def windows(ref, side):
        parts = [
            ref[side, k // 2 : k // 2 + 4, k % 2, s : s + 8].reshape(512, CH)
            for s in range(3)
            for k in range(4)
        ]
        return jnp.concatenate(parts, axis=1)

    for side in range(2):
        near = 7 * side
        result = jnp.dot(windows(a_planes, side), wa[side], preferred_element_type=F32)
        for i in range(4):
            for j in range(2):
                at = (near * 8 + 2 * i + j) * LINE
                lin[at : at + 128] += result[i * 128 : i * 128 + 128, j * CH : (j + 1) * CH]
        result = jnp.dot(windows(e_planes, side), w2[2 * side], preferred_element_type=F32)
        for i in range(4):
            for j in range(2):
                at = ((2 * i + j) * 8 + near) * LINE
                lin[at : at + 128] += result[i * 128 : i * 128 + 128, j * CH : (j + 1) * CH]
        taps = jnp.concatenate(
            [w2[e, 2 * side * 4 * CH : (2 * side + 1) * 4 * CH] for e in range(3)], axis=0
        )
        result = jnp.dot(windows(c_planes, side), taps, preferred_element_type=F32)
        for i in range(4):
            for j in range(2):
                for e in range(8):
                    at = ((2 * i + j) * 8 + e) * LINE + near * 16
                    row = (i * 8 + e) * 16
                    lin[at : at + 16] += result[row : row + 16, j * CH : (j + 1) * CH]


def inside(i, j):
    return (i >= 0) & (i < lax.axis_size("gx")) & (j >= 0) & (j < lax.axis_size("gy"))


def greet_neighbours(barrier):
    i, j = lax.axis_index("gx"), lax.axis_index("gy")
    count = jnp.int32(0)
    for dx, dy in DIRECTIONS:
        there = inside(i + dx, j + dy)
        count += there.astype(jnp.int32)

        @pl.when(there)
        def _():
            pl.semaphore_signal(
                barrier, inc=1, device_id=(i + dx, j + dy), device_id_type=MESH
            )

    return count


def pack_lists(lists, faces, sending):
    for k in range(8):
        for r in range(4):
            sending[k, r] = faces[jnp.minimum(lists[r, k], 15)]


def halo_copy(k, sending, received, send_sem, recv_sem):
    i, j = lax.axis_index("gx"), lax.axis_index("gy")
    dx, dy = DIRECTIONS[k]
    return pltpu.make_async_remote_copy(
        src_ref=sending.at[k],
        dst_ref=received.at[k],
        send_sem=send_sem.at[k],
        recv_sem=recv_sem.at[k],
        device_id=(i + dx, j + dy),
        device_id_type=MESH,
    )


ORDER = (0, 2, 5, 7, 3, 4, 1, 6)


def start_halo(*halo):
    i, j = lax.axis_index("gx"), lax.axis_index("gy")
    for k in ORDER:
        dx, dy = DIRECTIONS[k]

        @pl.when(inside(i + dx, j + dy))
        def _():
            halo_copy(k, *halo).start()


def wait_halo(*halo):
    i, j = lax.axis_index("gx"), lax.axis_index("gy")
    for k in ORDER:
        dx, dy = DIRECTIONS[k]

        @pl.when(inside(i - dx, j - dy))
        def _():
            halo_copy(k, *halo).wait_recv()


def wait_halo_sent(*halo):
    i, j = lax.axis_index("gx"), lax.axis_index("gy")
    for k in ORDER:
        dx, dy = DIRECTIONS[k]

        @pl.when(inside(i + dx, j + dy))
        def _():
            halo_copy(k, *halo).wait_send()


ROWS = 3584
HALF = ROWS // 2
SHARE = HALF // 16


def place():
    i = lax.axis_index("gx")
    return i // 2, i % 2, lax.axis_index("gy")


def sibling_copy(src, dst, sems, n):
    z, core, j = place()
    return pltpu.make_async_remote_copy(
        src_ref=src, dst_ref=dst, send_sem=sems.at[0, n], recv_sem=sems.at[1, n],
        device_id=(2 * z + 1 - core, j), device_id_type=MESH,
    )


def in_plane(n):
    z, core, j = place()
    return 2 * (n // 4) + core, (n % 4) * 4 + j % 4


def plane_copy(src, dst, sems, d):
    z, core, j = place()
    return pltpu.make_async_remote_copy(
        src_ref=src, dst_ref=dst, send_sem=sems.at[0, d], recv_sem=sems.at[1, d],
        device_id=in_plane((z * 4 + j // 4 + d) % 16), device_id_type=MESH,
    )


def in_column(d):
    z, core, j = place()
    return 2 * z + core, j // 4 * 4 + (j + d) % 4


def column_copy(src, dst, sems, d):
    return pltpu.make_async_remote_copy(
        src_ref=src, dst_ref=dst, send_sem=sems.at[0, d], recv_sem=sems.at[1, d],
        device_id=in_column(d), device_id_type=MESH,
    )


def greet_summers(barrier):
    z, core, j = place()

    def greet(where):
        pl.semaphore_signal(barrier, inc=1, device_id=where, device_id_type=MESH)

    greet((2 * z + 1 - core, j))
    for d in range(1, 16):
        greet(in_plane((z * 4 + j // 4 + d) % 16))
    for d in range(1, 4):
        greet(in_column(d))
    return 19


def credit_neighbours(credit):
    i, j = lax.axis_index("gx"), lax.axis_index("gy")
    for dx, dy in DIRECTIONS:

        @pl.when(inside(i - dx, j - dy))
        def _():
            pl.semaphore_signal(
                credit, inc=1, device_id=(i - dx, j - dy), device_id_type=MESH
            )


def kernel(
    vol, cot, w, bias, lists, kmap, act, grad, total,
    nat, lin, x32, t32, wide, ct, faces, sending, received, x, g,
    a_planes, e_planes, c_planes, w2, wa, gt,
    d32, d16, from_sibling, h32, h16, from_plane, column, share, gathered, whole,
    send_sem, recv_sem, sib_sems, out_sems, col_sems, in_sems, own_sems, credit,
):
    halo = (sending, received, send_sem, recv_sem)
    planes = (a_planes, e_planes, c_planes)
    z, core, j = place()
    n = z * 4 + j // 4
    take_vol = pltpu.make_async_copy(vol, nat, own_sems.at[0])
    take_cot = pltpu.make_async_copy(cot, nat, own_sems.at[1])
    give_act = pltpu.make_async_copy(nat, act, own_sems.at[2])
    give_grad = pltpu.make_async_copy(nat, grad, own_sems.at[3])
    give_total = pltpu.make_async_copy(whole, total, own_sems.at[4])
    take_vol.start()
    barrier = pltpu.get_barrier_semaphore()
    neighbours = greet_neighbours(barrier)
    summers = greet_summers(barrier)

    take_vol.wait()
    natural_to_bricks(nat, x32)
    take_cot.start()
    own_table(x32, t32, faces)
    pack_lists(lists, faces, sending)
    pl.semaphore_wait(barrier, neighbours + summers)
    start_halo(*halo)

    def put_x(a, e, c, v):
        x[1 + a, 1 + e, 1 + c] = v

    each_inner(x32, put_x)

    def put_cot(a, e, c, v):
        ct[pl.ds(rows16((a * 64 + e * 8 + c) * 16), 16)] = v

    take_cot.wait()
    natural_to_bricks(nat, x32)
    each_inner(x32, put_cot)
    wide_weights(w, w2, wa, False)
    clear_rims(planes, x, g)
    inner_conv(x, w2, wa, lin, 0, 4)
    wait_halo(*halo)
    received_table(received, t32, wide)
    credit_neighbours(credit)
    rim(kmap, t32, x32, planes, x)
    rim_conv(planes, w2, wa, lin)

    def finish(ae, _):
        a, e = ae // 8, ae % 8
        line = pl.multiple_of(ae * LINE, 8)
        linear = lin[pl.ds(line, 128)] + bias[...]
        s = 1.0 / (1.0 + jnp.exp(-linear))
        activated = linear * s
        slope = ct[pl.ds(rows16(ae * 128), 128)].astype(F32) * s * (1.0 + linear * (1.0 - s))
        for c in range(8):
            lin[pl.ds(line + c * 17, 16)] = activated[c * 16 : c * 16 + 16]
            at = (1 + a) * SP + (1 + e) * SQ + (1 + c) * SR
            x32[pl.ds(at, 16)] = slope[c * 16 : c * 16 + 16]
        g[1 + a, 1 + e, 1:9] = slope.astype(BF16).reshape(8, 16, CH)
        return 0

    lax.fori_loop(0, 64, finish, 0)
    wait_halo_sent(*halo)
    own_table(x32, t32, faces)
    pack_lists(lists, faces, sending)
    pl.semaphore_wait(credit, neighbours)
    start_halo(*halo)

    bricks_to_natural(lin, nat)
    give_act.start()

    def turn(p, sums):
        for m in range(8):
            block = g[1 + p, 1 + m, 1:9].astype(F32).reshape(128, CH)
            gt[p // 2, pl.ds(rows16((p % 2) * CH), CH), m * 128 : m * 128 + 128] = (
                block.T.astype(BF16)
            )
            sums = sums + block
        return sums

    sums = lax.fori_loop(0, 8, turn, jnp.zeros((128, CH), F32))
    d32[27 * CH :] = jnp.concatenate(
        [jnp.sum(sums, axis=0, keepdims=True), jnp.zeros((127, CH), F32)], axis=0
    )

    slopes = jnp.concatenate([gt[i] for i in range(4)], axis=1)
    for e in range(3):
        for c in range(3):
            parts = [
                jnp.concatenate(
                    [x[2 * i + k, e : e + 8, c : c + 8].reshape(1024, CH) for i in range(4)],
                    axis=0,
                )
                for k in range(4)
            ]
            terms = jnp.dot(
                slopes, jnp.concatenate(parts, axis=1), preferred_element_type=F32
            )
            for a in range(3):
                term = (
                    terms[:CH, a * CH : (a + 1) * CH]
                    + terms[CH:, (a + 1) * CH : (a + 2) * CH]
                )
                at = (a * 9 + e * 3 + c) * CH
                d32[at : at + CH] = term.T

    mine = pl.ds(rows16(core * HALF), HALF)
    other = pl.ds(rows16((1 - core) * HALF), HALF)
    d16[...] = d32[other].astype(BF16)
    sibling_copy(d16, from_sibling, sib_sems, 0).start()
    wide_weights(w, w2, wa, True)
    inner_conv(g, w2, wa, lin, 0, 1)

    sibling_copy(d16, from_sibling, sib_sems, 0).wait()
    h32[...] = d32[mine] + from_sibling[...].astype(F32)
    h16[...] = h32[...].astype(BF16).reshape(16, SHARE, CH)
    for d in range(1, 16):
        plane_copy(h16.at[(n + d) % 16], from_plane.at[d - 1], out_sems, d).start()
    inner_conv(g, w2, wa, lin, 1, 4)
    for d in range(1, 16):
        plane_copy(h16.at[(n + d) % 16], from_plane.at[d - 1], out_sems, d).wait()
    part = h32[pl.ds(rows16(n * SHARE), SHARE)]
    for d in range(1, 16):
        part = part + from_plane[d - 1].astype(F32)
    column[j % 4] = part.astype(BF16)
    for d in range(1, 4):
        column_copy(column.at[j % 4], column.at[j % 4], col_sems, d).start()
    wait_halo(*halo)
    received_table(received, t32, wide)
    for d in range(1, 4):
        column_copy(column.at[j % 4], column.at[j % 4], col_sems, d).wait()
    part = column[0].astype(F32)
    for m in range(1, 4):
        part = part + column[m].astype(F32)
    voxels = lax.axis_size("gx") * lax.axis_size("gy") * 8192
    share[...] = (part * (1.0 / math.sqrt(voxels))).astype(BF16)
    gathered[n] = share[...]
    for d in range(1, 16):
        plane_copy(share, gathered.at[n], in_sems, d).start()
    rim(kmap, t32, x32, planes, None)
    for d in range(1, 16):
        plane_copy(share, gathered.at[n], in_sems, d).wait()
    sibling_copy(gathered, whole.at[core], sib_sems, 1).start()
    whole[core] = gathered[...]
    rim_conv(planes, w2, wa, lin)

    def settle(ae, _):
        line = pl.multiple_of(ae * LINE, 8)
        block = lin[pl.ds(line, 128)]
        for c in range(1, 8):
            lin[pl.ds(line + c * 17, 16)] = block[c * 16 : c * 16 + 16]
        return 0

    lax.fori_loop(0, 64, settle, 0)
    give_act.wait()
    bricks_to_natural(lin, nat)
    give_grad.start()
    sibling_copy(gathered, whole.at[core], sib_sems, 1).wait()
    give_total.start()
    wait_halo_sent(*halo)
    give_total.wait()
    give_grad.wait()


def layer(vol, cot, w, bias, lists, kmap):
    vm = pl.BlockSpec(memory_space=pltpu.VMEM)
    sm = pl.BlockSpec(memory_space=pltpu.SMEM)
    hbm = pl.BlockSpec(memory_space=pl.ANY)
    field = pltpu.VMEM((10, 10, 10, 16, CH), BF16)
    planes = pltpu.VMEM((2, 5, 2, 10, 16, CH), BF16)
    return pl.pallas_call(
        kernel,
        out_shape=(
            jax.ShapeDtypeStruct((16, 512, CH), BF16),
            jax.ShapeDtypeStruct((16, 512, CH), BF16),
            jax.ShapeDtypeStruct((2, 16, SHARE, CH), BF16),
        ),
        in_specs=[hbm, hbm, vm, vm, sm, sm],
        out_specs=(hbm, hbm, hbm),
        scratch_shapes=[
            pltpu.VMEM((16, 512, CH), BF16),
            pltpu.VMEM((64 * LINE, CH), F32),
            pltpu.VMEM((10 * SP + 2, CH), F32),
            pltpu.VMEM((49 * ENTRY, 8, CH), F32),
            pltpu.VMEM((256, CH), F32),
            pltpu.VMEM((8192, CH), BF16),
            pltpu.VMEM((16, SENT, CH), BF16),
            pltpu.VMEM((8, 4, SENT, CH), BF16),
            pltpu.VMEM((8, 4, SENT, CH), BF16),
            field,
            field,
            planes,
            planes,
            planes,
            pltpu.VMEM((3, 12 * CH, 2 * CH), BF16),
            pltpu.VMEM((2, 12 * CH, 2 * CH), BF16),
            pltpu.VMEM((4, 2 * CH, 1024), BF16),
            pltpu.VMEM((ROWS, CH), F32),
            pltpu.VMEM((HALF, CH), BF16),
            pltpu.VMEM((HALF, CH), BF16),
            pltpu.VMEM((HALF, CH), F32),
            pltpu.VMEM((16, SHARE, CH), BF16),
            pltpu.VMEM((15, SHARE, CH), BF16),
            pltpu.VMEM((4, SHARE, CH), BF16),
            pltpu.VMEM((SHARE, CH), BF16),
            pltpu.VMEM((16, SHARE, CH), BF16),
            pltpu.VMEM((2, 16, SHARE, CH), BF16),
            pltpu.SemaphoreType.DMA((8,)),
            pltpu.SemaphoreType.DMA((8,)),
            pltpu.SemaphoreType.DMA((2, 2)),
            pltpu.SemaphoreType.DMA((2, 16)),
            pltpu.SemaphoreType.DMA((2, 4)),
            pltpu.SemaphoreType.DMA((2, 16)),
            pltpu.SemaphoreType.DMA((5,)),
            pltpu.SemaphoreType.REGULAR,
        ],
        compiler_params=pltpu.CompilerParams(
            collective_id=0, has_side_effects=True, vmem_limit_bytes=63 * 2**20
        ),
        name="layer",
    )(vol, cot, w, bias, lists, kmap)


PIECES = 4


def deliver_kernel(act, grad, total, act_out, grad_out, weight_out, bias_out, sems):
    copies = [
        pltpu.make_async_copy(
            src.at[pl.ds(m * 16 // PIECES, 16 // PIECES)],
            dst.at[pl.ds(m * 16 // PIECES, 16 // PIECES)],
            sems.at[n, m],
        )
        for n, (src, dst) in enumerate(((act, act_out), (grad, grad_out)))
        for m in range(PIECES)
    ]
    for copy in copies:
        copy.start()
    weight_out[...] = total[: 27 * CH].astype(F32)
    bias_out[...] = total[27 * CH : 27 * CH + 16].astype(F32)[0:1]
    for copy in copies:
        copy.wait()


def deliver(act, grad, total):
    vm = pl.BlockSpec(memory_space=pltpu.VMEM)
    hbm = pl.BlockSpec(memory_space=pl.ANY)
    return pl.pallas_call(
        deliver_kernel,
        out_shape=(
            jax.ShapeDtypeStruct(act.shape, BF16),
            jax.ShapeDtypeStruct(grad.shape, BF16),
            jax.ShapeDtypeStruct((27 * CH, CH), F32),
            jax.ShapeDtypeStruct((1, CH), F32),
        ),
        in_specs=[hbm, hbm, vm],
        out_specs=(hbm, hbm, vm, vm),
        scratch_shapes=[pltpu.SemaphoreType.DMA((2, PIECES))],
        compiler_params=pltpu.CompilerParams(vmem_limit_bytes=63 * 2**20),
        name="deliver",
    )(act, grad, total)


def shards(features, cotangent, kernel_weight, conv_bias, send_lists, kernel_map):
    act, grad, total = layer(
        features.reshape(16, 512, CH),
        cotangent.reshape(16, 512, CH),
        kernel_weight.reshape(27, CH, CH),
        conv_bias.reshape(1, CH),
        send_lists[0, 0].T,
        kernel_map[0, 0],
    )
    act, grad, weight_total, bias_total = deliver(act, grad, total.reshape(ROWS, CH))
    return (
        act.reshape(features.shape),
        grad.reshape(features.shape),
        weight_total.reshape(kernel_weight.shape),
        bias_total.reshape(CH),
    )


def solution(mesh):
    block = P("gx", "gy", None, None, None, None, None)
    return jax.shard_map(
        shards,
        mesh=mesh,
        in_specs=(block, block, P(), P(), P("gx", "gy", None, None), P("gx", "gy", None, None)),
        out_specs=(block, block, P(), P()),
        check_vma=False,
    )
```

```python
import functools
import math

import jax
import jax.numpy as jnp
from jax import lax
from jax.experimental import pallas as pl
from jax.experimental.pallas import tpu as pltpu
from jax.sharding import PartitionSpec as P

MESH = pl.DeviceIdType.MESH
F32, BF16 = jnp.float32, jnp.bfloat16
DIRECTIONS = ((-1, -1), (-1, 0), (-1, 1), (0, -1), (0, 1), (1, -1), (1, 0), (1, 1))
CH = 128
ENTRY = 52
SENT = 320
A_LOW, A_HIGH, E_LOW, E_HIGH, C_LOW, C_HIGH, EDGES = 0, 8, 16, 24, 32, 40, 48
SP, SQ, SR = 1711, 171, 17
LINE = 136


def rows16(start):
    return pl.multiple_of(start, 16)


def natural_to_bricks(nat, x32):
    def stage(b, _):
        block = nat[b].astype(F32)
        for ae in range(64):
            at = (1 + ae // 8) * SP + (1 + ae % 8) * SQ + SR
            x32[pl.ds(at + b, 8, stride=SR)] = block[ae * 8 : ae * 8 + 8]
        return 0

    lax.fori_loop(0, 16, stage, 0)


def each_inner(x32, put):
    def plane(a, _):
        for e in range(8):
            for c in range(8):
                at = (1 + a) * SP + (1 + e) * SQ + (1 + c) * SR
                put(a, e, c, x32[pl.ds(at, 16)].astype(BF16))
        return 0

    lax.fori_loop(0, 8, plane, 0)


def bricks_to_natural(lin, nat):
    def unstage(b, _):
        for ae in range(0, 64, 2):
            pair = [lin[pl.ds((ae + k) * LINE + b, 8, stride=17)] for k in range(2)]
            nat[b, ae * 8 : ae * 8 + 16] = jnp.concatenate(pair, axis=0).astype(BF16)
        return 0

    lax.fori_loop(0, 16, unstage, 0)


def own_table(x32, t32, faces):
    def one(b, _):
        base = b * ENTRY
        for low, p in ((A_LOW, 1), (A_HIGH, 8)):
            for e in range(8):
                t32[base + low + e] = x32[pl.ds(p * SP + (1 + e) * SQ + SR + b, 8, stride=SR)]
        for low, q in ((E_LOW, 1), (E_HIGH, 8)):
            for a in range(8):
                t32[base + low + a] = x32[pl.ds((1 + a) * SP + q * SQ + SR + b, 8, stride=SR)]
        for low, r in ((C_LOW, 1), (C_HIGH, 8)):
            for a in range(8):
                t32[base + low + a] = x32[pl.ds((1 + a) * SP + SQ + r * SR + b, 8, stride=SQ)]
        for n, (q, r) in enumerate(((1, 1), (1, 8), (8, 1), (8, 8))):
            t32[base + EDGES + n] = x32[pl.ds(SP + q * SQ + r * SR + b, 8, stride=SP)]
        faces[b, 0:128] = t32[pl.ds(base, 16)].reshape(128, CH).astype(BF16)
        for n, low in enumerate((E_LOW, E_HIGH, C_LOW, C_HIGH)):
            lines = t32[pl.ds(base + low + 1, 6)].reshape(48, CH)
            faces[b, 128 + 48 * n : 176 + 48 * n] = lines.astype(BF16)
        return 0

    lax.fori_loop(0, 16, one, 0)


def received_table(received, t32, wide):
    def one(n, _):
        base = (16 + n) * ENTRY
        k, r = n // 4, n % 4
        sides = received[k, r, 0:128].astype(F32)
        wide[0:128] = sides
        t32[pl.ds(base, 16)] = sides.reshape(16, 8, CH)
        for m, low in enumerate((E_LOW, E_HIGH, C_LOW, C_HIGH)):
            lines = received[k, r, 128 + 48 * m : 176 + 48 * m].astype(F32)
            t32[pl.ds(base + low + 1, 6)] = lines.reshape(6, 8, CH)
            if m < 2:
                wide[136 + 64 * m : 184 + 64 * m] = lines
        for a, side in ((0, 0), (7, 64)):
            low, high = wide[side : side + 8], wide[side + 56 : side + 64]
            t32[base + E_LOW + a] = low
            t32[base + E_HIGH + a] = high
            wide[128 + 8 * a : 136 + 8 * a] = low
            wide[192 + 8 * a : 200 + 8 * a] = high
            t32[base + C_LOW + a] = wide[pl.ds(side, 8, stride=8)]
            t32[base + C_HIGH + a] = wide[pl.ds(side + 7, 8, stride=8)]
        for m, start in enumerate((128, 135, 192, 199)):
            t32[base + EDGES + m] = wide[pl.ds(start, 8, stride=8)]
        return 0

    lax.fori_loop(0, 32, one, 0)
    t32[pl.ds(48 * ENTRY, ENTRY)] = jnp.zeros((ENTRY, 8, CH), F32)


def rim(kmap, t32, x32, planes, x):
    a_planes, e_planes, c_planes = planes

    def one(b, _):
        for o in range(27):
            a, e, c = o // 9 - 1, o // 3 % 3 - 1, o % 3 - 1
            if a == e == c == 0:
                continue
            base = kmap[b, o] * ENTRY
            p, q, r = [1 + 8 * (s > 0) - (s < 0) for s in (a, e, c)]
            dest = p * SP + q * SQ + r * SR + b
            fe, fc = 7 * (e < 0), 7 * (c < 0)
            if a != 0:
                side = base + (A_HIGH if a < 0 else A_LOW)
                if e == 0 and c == 0:
                    for n in range(8):
                        x32[pl.ds(dest + n * SQ, 8, stride=SR)] = t32[side + n]
                elif c == 0:
                    x32[pl.ds(dest, 8, stride=SR)] = t32[side + fe]
                elif e == 0:
                    line = base + (C_HIGH if c < 0 else C_LOW) + 7 * (a < 0)
                    x32[pl.ds(dest, 8, stride=SQ)] = t32[line]
                else:
                    x32[pl.ds(dest, 1)] = t32[side + fe][fc : fc + 1]
            elif e != 0:
                side = base + (E_HIGH if e < 0 else E_LOW)
                if c == 0:
                    for n in range(8):
                        x32[pl.ds(dest + n * SP, 8, stride=SR)] = t32[side + n]
                else:
                    x32[pl.ds(dest, 8, stride=SP)] = t32[base + EDGES + 2 * (e < 0) + (c < 0)]
            else:
                side = base + (C_HIGH if c < 0 else C_LOW)
                for n in range(8):
                    x32[pl.ds(dest + n * SP, 8, stride=SQ)] = t32[side + n]
        return 0

    lax.fori_loop(0, 16, one, 0)

    def pack(p, q, r):
        cell = x32[pl.ds(p * SP + q * SQ + r * SR, 16)].astype(BF16)
        if x is not None:
            x[p, q, r] = cell
        return cell

    def line(q, _):
        for side in range(2):
            for r in range(10):
                a_planes[side, q // 2, q % 2, r] = pack(9 * side, q, r)
        return 0

    lax.fori_loop(0, 10, line, 0)

    def ring(p, _):
        for side in range(2):
            for r in range(10):
                e_planes[side, p // 2, p % 2, r] = pack(p, 9 * side, r)
            for q in range(1, 9):
                c_planes[side, p // 2, p % 2, q] = pack(p, q, 9 * side)
        return 0

    lax.fori_loop(1, 9, ring, 0)


def clear_rims(planes, x, g):
    _, e_planes, c_planes = planes
    row = jnp.zeros((10, 16, CH), BF16)
    for side in range(2):
        for p in (0, 9):
            e_planes[side, p // 2, p % 2] = row
            c_planes[side, p // 2, p % 2] = row
        for p in range(1, 9):
            for q in (0, 9):
                c_planes[side, p // 2, p % 2, q] = row[0]

    def clear(n, _):
        for f in (x, g):
            for side in (0, 9):
                f[side, n] = row
                f[n, side] = row
                f[n, :, side] = row
        return 0

    lax.fori_loop(0, 10, clear, 0)


def wide_weights(w, w2, wa, back):
    zero = jnp.zeros((CH, CH), BF16)

    def put(ref, n, c, k, j, tap):
        ref[n, (c * 4 + k) * CH : (c * 4 + k + 1) * CH, j * CH : (j + 1) * CH] = tap

    for c in range(3):
        for k, j in ((0, 1), (3, 0)):
            for n in range(3):
                put(w2, n, c, k, j, zero)
            for n in range(2):
                put(wa, n, c, k, j, zero)
    for a in range(3):
        for e in range(3):
            for c in range(3):
                if back:
                    tap = w[(2 - a) * 9 + (2 - e) * 3 + 2 - c].astype(F32).T.astype(BF16)
                else:
                    tap = w[a * 9 + e * 3 + c]
                for j in range(2):
                    put(w2, e, c, a + j, j, tap)
                    if a != 1:
                        put(wa, a // 2, c, e + j, j, tap)


def inner_conv(x, w2, wa, lin, lo, hi):
    def pair(i, _):
        both = None
        for e in range(3):
            parts = [
                x[2 * i + k, e : e + 8, c : c + 8].reshape(1024, CH)
                for c in range(3)
                for k in (1, 2)
            ]
            taps = jnp.concatenate(
                [w2[e, (c * 4 + 1) * CH : (c * 4 + 3) * CH] for c in range(3)], axis=0
            )
            term = jnp.dot(jnp.concatenate(parts, axis=1), taps, preferred_element_type=F32)
            both = term if both is None else both + term
        for j in range(2):
            plane = x[2 * i + 3 * j].reshape(5, 2, 10, 16, CH)
            parts = [
                plane[k // 2 : k // 2 + 4, k % 2, c : c + 8].reshape(512, CH)
                for c in range(3)
                for k in range(4)
            ]
            one = jnp.dot(jnp.concatenate(parts, axis=1), wa[j], preferred_element_type=F32)
            for e in range(8):
                at = pl.multiple_of(((2 * i + j) * 8 + e) * LINE, 8)
                lin[pl.ds(at, 128)] = (
                    both[e * 128 : e * 128 + 128, j * CH : (j + 1) * CH]
                    + one[e // 2 * 128 : e // 2 * 128 + 128, e % 2 * CH : (e % 2 + 1) * CH]
                )
        return 0

    lax.fori_loop(lo, hi, pair, 0)


def rim_conv(planes, w2, wa, lin):
    a_planes, e_planes, c_planes = planes

    def windows(ref, side):
        parts = [
            ref[side, k // 2 : k // 2 + 4, k % 2, s : s + 8].reshape(512, CH)
            for s in range(3)
            for k in range(4)
        ]
        return jnp.concatenate(parts, axis=1)

    for side in range(2):
        near = 7 * side
        result = jnp.dot(windows(a_planes, side), wa[side], preferred_element_type=F32)
        for i in range(4):
            for j in range(2):
                at = (near * 8 + 2 * i + j) * LINE
                lin[at : at + 128] += result[i * 128 : i * 128 + 128, j * CH : (j + 1) * CH]
        result = jnp.dot(windows(e_planes, side), w2[2 * side], preferred_element_type=F32)
        for i in range(4):
            for j in range(2):
                at = ((2 * i + j) * 8 + near) * LINE
                lin[at : at + 128] += result[i * 128 : i * 128 + 128, j * CH : (j + 1) * CH]
        taps = jnp.concatenate(
            [w2[e, 2 * side * 4 * CH : (2 * side + 1) * 4 * CH] for e in range(3)], axis=0
        )
        result = jnp.dot(windows(c_planes, side), taps, preferred_element_type=F32)
        for i in range(4):
            for j in range(2):
                for e in range(8):
                    at = ((2 * i + j) * 8 + e) * LINE + near * 16
                    row = (i * 8 + e) * 16
                    lin[at : at + 16] += result[row : row + 16, j * CH : (j + 1) * CH]


def inside(i, j):
    return (i >= 0) & (i < lax.axis_size("gx")) & (j >= 0) & (j < lax.axis_size("gy"))


def greet_neighbours(barrier):
    i, j = lax.axis_index("gx"), lax.axis_index("gy")
    count = jnp.int32(0)
    for dx, dy in DIRECTIONS:
        there = inside(i + dx, j + dy)
        count += there.astype(jnp.int32)

        @pl.when(there)
        def _():
            pl.semaphore_signal(
                barrier, inc=1, device_id=(i + dx, j + dy), device_id_type=MESH
            )

    return count


def pack_lists(lists, faces, sending):
    for k in range(8):
        for r in range(4):
            sending[k, r] = faces[jnp.minimum(lists[r, k], 15)]


def halo_copy(k, sending, received, send_sem, recv_sem):
    i, j = lax.axis_index("gx"), lax.axis_index("gy")
    dx, dy = DIRECTIONS[k]
    return pltpu.make_async_remote_copy(
        src_ref=sending.at[k],
        dst_ref=received.at[k],
        send_sem=send_sem.at[k],
        recv_sem=recv_sem.at[k],
        device_id=(i + dx, j + dy),
        device_id_type=MESH,
    )


ORDER = (0, 2, 5, 7, 3, 4, 1, 6)


def start_halo(*halo):
    i, j = lax.axis_index("gx"), lax.axis_index("gy")
    for k in ORDER:
        dx, dy = DIRECTIONS[k]

        @pl.when(inside(i + dx, j + dy))
        def _():
            halo_copy(k, *halo).start()


def wait_halo(*halo):
    i, j = lax.axis_index("gx"), lax.axis_index("gy")
    for k in ORDER:
        dx, dy = DIRECTIONS[k]

        @pl.when(inside(i - dx, j - dy))
        def _():
            halo_copy(k, *halo).wait_recv()


def wait_halo_sent(*halo):
    i, j = lax.axis_index("gx"), lax.axis_index("gy")
    for k in ORDER:
        dx, dy = DIRECTIONS[k]

        @pl.when(inside(i + dx, j + dy))
        def _():
            halo_copy(k, *halo).wait_send()


ROWS = 28 * CH
PARTS = ((0, 16), (16, 12))


def place():
    i = lax.axis_index("gx")
    return i // 2, i % 2, lax.axis_index("gy")


def sibling_copy(src, dst, sems, n):
    z, core, j = place()
    return pltpu.make_async_remote_copy(
        src_ref=src, dst_ref=dst, send_sem=sems.at[0, n], recv_sem=sems.at[1, n],
        device_id=(2 * z + 1 - core, j), device_id_type=MESH,
    )


def in_plane(n):
    z, core, j = place()
    return 2 * (n // 4) + core, (n % 4) * 4 + j % 4


def plane_copy(src, dst, sems, d):
    z, core, j = place()
    return pltpu.make_async_remote_copy(
        src_ref=src, dst_ref=dst, send_sem=sems.at[0, d], recv_sem=sems.at[1, d],
        device_id=in_plane((z * 4 + j // 4 + d) % 16), device_id_type=MESH,
    )


def in_column(d):
    z, core, j = place()
    return 2 * z + core, j // 4 * 4 + (j + d) % 4


def column_copy(src, dst, sems, d):
    return pltpu.make_async_remote_copy(
        src_ref=src, dst_ref=dst, send_sem=sems.at[0, d], recv_sem=sems.at[1, d],
        device_id=in_column(d), device_id_type=MESH,
    )


def greet_summers(barrier):
    z, core, j = place()

    def greet(where):
        pl.semaphore_signal(barrier, inc=1, device_id=where, device_id_type=MESH)

    greet((2 * z + 1 - core, j))
    for d in range(1, 16):
        greet(in_plane((z * 4 + j // 4 + d) % 16))
    for d in range(1, 4):
        greet(in_column(d))
    return 19


class Summed:
    def __init__(self, d32, first, refs):
        self.d32, self.first = d32, first
        (
            self.d16, self.from_sibling, self.h32, self.h16, self.from_plane, self.column,
            self.share, self.gathered, self.whole, self.sib, self.out, self.col, self.back,
        ) = refs
        self.half = self.d16.shape[0]
        self.rows = self.share.shape[0]
        z, self.core, j = place()
        self.n, self.y = z * 4 + j // 4, j % 4

    def first_pair(self):
        return sibling_copy(self.d16, self.from_sibling, self.sib, 0)

    def outward(self, d):
        there = (self.n + d) % 16
        return plane_copy(self.h16.at[there], self.from_plane.at[d - 1], self.out, d)

    def upward(self, d):
        return column_copy(self.column.at[self.y], self.column.at[self.y], self.col, d)

    def inward(self, d):
        return plane_copy(self.share, self.gathered.at[self.n], self.back, d)

    def last_pair(self):
        return sibling_copy(self.gathered, self.whole.at[self.core], self.sib, 1)

    def start_pair(self):
        other = pl.ds(rows16(self.first + (1 - self.core) * self.half), self.half)
        self.d16[...] = self.d32[other].astype(BF16)
        self.first_pair().start()

    def start_plane(self):
        self.first_pair().wait()
        mine = pl.ds(rows16(self.first + self.core * self.half), self.half)
        self.h32[...] = self.d32[mine] + self.from_sibling[...].astype(F32)
        self.h16[...] = self.h32[...].astype(BF16).reshape(self.h16.shape)
        for d in range(1, 16):
            self.outward(d).start()

    def start_column(self):
        for d in range(1, 16):
            self.outward(d).wait()
        part = self.h32[pl.ds(rows16(self.n * self.rows), self.rows)]
        for d in range(1, 16):
            part = part + self.from_plane[d - 1].astype(F32)
        self.column[self.y] = part.astype(BF16)
        for d in range(1, 4):
            self.upward(d).start()

    def start_back(self):
        for d in range(1, 4):
            self.upward(d).wait()
        part = self.column[0].astype(F32)
        for m in range(1, 4):
            part = part + self.column[m].astype(F32)
        voxels = lax.axis_size("gx") * lax.axis_size("gy") * 8192
        self.share[...] = (part * (1.0 / math.sqrt(voxels))).astype(BF16)
        self.gathered[self.n] = self.share[...]
        for d in range(1, 16):
            self.inward(d).start()

    def start_last(self):
        for d in range(1, 16):
            self.inward(d).wait()
        self.last_pair().start()
        self.whole[self.core] = self.gathered[...]

    def finish(self):
        self.last_pair().wait()


def sum_scratch(blocks):
    half = blocks * CH // 2
    rows = half // 16
    return [
        pltpu.VMEM((half, CH), BF16),
        pltpu.VMEM((half, CH), BF16),
        pltpu.VMEM((half, CH), F32),
        pltpu.VMEM((16, rows, CH), BF16),
        pltpu.VMEM((15, rows, CH), BF16),
        pltpu.VMEM((4, rows, CH), BF16),
        pltpu.VMEM((rows, CH), BF16),
        pltpu.VMEM((16, rows, CH), BF16),
        pltpu.VMEM((2, 16, rows, CH), BF16),
        pltpu.SemaphoreType.DMA((2, 2)),
        pltpu.SemaphoreType.DMA((2, 16)),
        pltpu.SemaphoreType.DMA((2, 4)),
        pltpu.SemaphoreType.DMA((2, 16)),
    ]


def credit_neighbours(credit):
    i, j = lax.axis_index("gx"), lax.axis_index("gy")
    for dx, dy in DIRECTIONS:

        @pl.when(inside(i - dx, j - dy))
        def _():
            pl.semaphore_signal(
                credit, inc=1, device_id=(i - dx, j - dy), device_id_type=MESH
            )


def kernel(
    vol, cot, w, bias, lists, kmap, act, grad, total_a, total_b,
    nat, lin, x32, t32, wide, ct, faces, sending, received, x, g,
    a_planes, e_planes, c_planes, w2, wa, gt, d32, send_sem, recv_sem, own_sems, credit, *sums,
):
    halo = (sending, received, send_sem, recv_sem)
    planes = (a_planes, e_planes, c_planes)
    early = Summed(d32, PARTS[0][0] * CH, sums[: len(sums) // 2])
    late = Summed(d32, PARTS[1][0] * CH, sums[len(sums) // 2 :])
    take_vol = pltpu.make_async_copy(vol, nat, own_sems.at[0])
    take_cot = pltpu.make_async_copy(cot, nat, own_sems.at[1])
    give_act = pltpu.make_async_copy(nat, act, own_sems.at[2])
    give_grad = pltpu.make_async_copy(nat, grad, own_sems.at[3])
    give_early = pltpu.make_async_copy(early.whole, total_a, own_sems.at[4])
    give_late = pltpu.make_async_copy(late.whole, total_b, own_sems.at[5])
    take_vol.start()
    barrier = pltpu.get_barrier_semaphore()
    neighbours = greet_neighbours(barrier)
    summers = greet_summers(barrier)

    take_vol.wait()
    natural_to_bricks(nat, x32)
    take_cot.start()
    own_table(x32, t32, faces)
    pack_lists(lists, faces, sending)
    pl.semaphore_wait(barrier, neighbours + summers)
    start_halo(*halo)

    def put_x(a, e, c, v):
        x[1 + a, 1 + e, 1 + c] = v

    each_inner(x32, put_x)

    def put_cot(a, e, c, v):
        ct[pl.ds(rows16((a * 64 + e * 8 + c) * 16), 16)] = v

    take_cot.wait()
    natural_to_bricks(nat, x32)
    each_inner(x32, put_cot)
    wide_weights(w, w2, wa, False)
    clear_rims(planes, x, g)
    inner_conv(x, w2, wa, lin, 0, 4)
    wait_halo(*halo)
    received_table(received, t32, wide)
    credit_neighbours(credit)
    rim(kmap, t32, x32, planes, x)
    rim_conv(planes, w2, wa, lin)

    def finish(ae, _):
        a, e = ae // 8, ae % 8
        line = pl.multiple_of(ae * LINE, 8)
        linear = lin[pl.ds(line, 128)] + bias[...]
        s = 1.0 / (1.0 + jnp.exp(-linear))
        activated = linear * s
        slope = ct[pl.ds(rows16(ae * 128), 128)].astype(F32) * s * (1.0 + linear * (1.0 - s))
        for c in range(8):
            lin[pl.ds(line + c * 17, 16)] = activated[c * 16 : c * 16 + 16]
            at = (1 + a) * SP + (1 + e) * SQ + (1 + c) * SR
            x32[pl.ds(at, 16)] = slope[c * 16 : c * 16 + 16]
        g[1 + a, 1 + e, 1:9] = slope.astype(BF16).reshape(8, 16, CH)
        return 0

    lax.fori_loop(0, 64, finish, 0)
    wait_halo_sent(*halo)
    own_table(x32, t32, faces)
    pack_lists(lists, faces, sending)
    pl.semaphore_wait(credit, neighbours)
    start_halo(*halo)

    bricks_to_natural(lin, nat)
    give_act.start()

    def turn(p, sums):
        for m in range(8):
            block = g[1 + p, 1 + m, 1:9].astype(F32).reshape(128, CH)
            gt[p // 2, pl.ds(rows16((p % 2) * CH), CH), m * 128 : m * 128 + 128] = (
                block.T.astype(BF16)
            )
            sums = sums + block
        return sums

    totals = lax.fori_loop(0, 8, turn, jnp.zeros((128, CH), F32))
    d32[27 * CH :] = jnp.concatenate(
        [jnp.sum(totals, axis=0, keepdims=True), jnp.zeros((127, CH), F32)], axis=0
    )

    slopes = jnp.concatenate([gt[i] for i in range(4)], axis=1)
    for e in range(3):
        for c in range(3):
            parts = [
                jnp.concatenate(
                    [x[2 * i + k, e : e + 8, c : c + 8].reshape(1024, CH) for i in range(4)],
                    axis=0,
                )
                for k in range(4)
            ]
            terms = jnp.dot(
                slopes, jnp.concatenate(parts, axis=1), preferred_element_type=F32
            )
            for a in range(3):
                term = (
                    terms[:CH, a * CH : (a + 1) * CH]
                    + terms[CH:, (a + 1) * CH : (a + 2) * CH]
                )
                at = (e * 9 + c * 3 + a) * CH
                d32[at : at + CH] = term.T
        if e == 1:
            early.start_pair()

    late.start_pair()
    early.start_plane()
    wide_weights(w, w2, wa, True)
    inner_conv(g, w2, wa, lin, 0, 1)
    late.start_plane()
    inner_conv(g, w2, wa, lin, 1, 3)
    early.start_column()
    inner_conv(g, w2, wa, lin, 3, 4)
    late.start_column()
    early.start_back()
    wait_halo(*halo)
    received_table(received, t32, wide)
    late.start_back()
    rim(kmap, t32, x32, planes, None)
    early.start_last()
    rim_conv(planes, w2, wa, lin)
    late.start_last()

    def settle(ae, _):
        line = pl.multiple_of(ae * LINE, 8)
        block = lin[pl.ds(line, 128)]
        for c in range(1, 8):
            lin[pl.ds(line + c * 17, 16)] = block[c * 16 : c * 16 + 16]
        return 0

    lax.fori_loop(0, 64, settle, 0)
    give_act.wait()
    bricks_to_natural(lin, nat)
    give_grad.start()
    early.finish()
    give_early.start()
    late.finish()
    give_late.start()
    wait_halo_sent(*halo)
    give_early.wait()
    give_late.wait()
    give_grad.wait()


def layer(vol, cot, w, bias, lists, kmap):
    vm = pl.BlockSpec(memory_space=pltpu.VMEM)
    sm = pl.BlockSpec(memory_space=pltpu.SMEM)
    hbm = pl.BlockSpec(memory_space=pl.ANY)
    field = pltpu.VMEM((10, 10, 10, 16, CH), BF16)
    planes = pltpu.VMEM((2, 5, 2, 10, 16, CH), BF16)
    return pl.pallas_call(
        kernel,
        out_shape=(
            jax.ShapeDtypeStruct((16, 512, CH), BF16),
            jax.ShapeDtypeStruct((16, 512, CH), BF16),
            *[
                jax.ShapeDtypeStruct((2, 16, blocks * 4, CH), BF16) for _, blocks in PARTS
            ],
        ),
        in_specs=[hbm, hbm, vm, vm, sm, sm],
        out_specs=(hbm, hbm, hbm, hbm),
        scratch_shapes=[
            pltpu.VMEM((16, 512, CH), BF16),
            pltpu.VMEM((64 * LINE, CH), F32),
            pltpu.VMEM((10 * SP + 2, CH), F32),
            pltpu.VMEM((49 * ENTRY, 8, CH), F32),
            pltpu.VMEM((256, CH), F32),
            pltpu.VMEM((8192, CH), BF16),
            pltpu.VMEM((16, SENT, CH), BF16),
            pltpu.VMEM((8, 4, SENT, CH), BF16),
            pltpu.VMEM((8, 4, SENT, CH), BF16),
            field,
            field,
            planes,
            planes,
            planes,
            pltpu.VMEM((3, 12 * CH, 2 * CH), BF16),
            pltpu.VMEM((2, 12 * CH, 2 * CH), BF16),
            pltpu.VMEM((4, 2 * CH, 1024), BF16),
            pltpu.VMEM((ROWS, CH), F32),
            pltpu.SemaphoreType.DMA((8,)),
            pltpu.SemaphoreType.DMA((8,)),
            pltpu.SemaphoreType.DMA((6,)),
            pltpu.SemaphoreType.REGULAR,
            *[ref for _, blocks in PARTS for ref in sum_scratch(blocks)],
        ],
        compiler_params=pltpu.CompilerParams(
            collective_id=0, has_side_effects=True, vmem_limit_bytes=63 * 2**20
        ),
        name="layer",
    )(vol, cot, w, bias, lists, kmap)


PIECES = 4


def deliver_kernel(act, grad, total_a, total_b, act_out, grad_out, weight_out, bias_out, held, sems):
    def piece(n, m, src, dst):
        at = pl.ds(m * 16 // PIECES, 16 // PIECES)
        return (
            pltpu.make_async_copy(src.at[at], held.at[n, at], sems.at[0, n, m]),
            pltpu.make_async_copy(held.at[n, at], dst.at[at], sems.at[1, n, m]),
        )

    pieces = [
        piece(n, m, src, dst)
        for n, (src, dst) in enumerate(((act, act_out), (grad, grad_out)))
        for m in range(PIECES)
    ]
    for take, _ in pieces:
        take.start()
    for take, give in pieces:
        take.wait()
        give.start()
    for n in range(28):
        total, at = (total_a, n * CH) if n < PARTS[1][0] else (total_b, (n - PARTS[1][0]) * CH)
        if n < 27:
            weight_out[n % 3 * 9 + n // 3] = total[at : at + CH].astype(F32)
        else:
            bias_out[...] = total[at : at + 16].astype(F32)[0:1]
    for _, give in pieces:
        give.wait()


def deliver(act, grad, total_a, total_b):
    vm = pl.BlockSpec(memory_space=pltpu.VMEM)
    hbm = pl.BlockSpec(memory_space=pl.ANY)
    return pl.pallas_call(
        deliver_kernel,
        out_shape=(
            jax.ShapeDtypeStruct(act.shape, BF16),
            jax.ShapeDtypeStruct(grad.shape, BF16),
            jax.ShapeDtypeStruct((27, CH, CH), F32),
            jax.ShapeDtypeStruct((1, CH), F32),
        ),
        in_specs=[hbm, hbm, vm, vm],
        out_specs=(hbm, hbm, vm, vm),
        scratch_shapes=[
            pltpu.VMEM((2, 16, 512, CH), BF16),
            pltpu.SemaphoreType.DMA((2, 2, PIECES)),
        ],
        compiler_params=pltpu.CompilerParams(vmem_limit_bytes=63 * 2**20),
        name="deliver",
    )(act, grad, total_a, total_b)


def shards(features, cotangent, kernel_weight, conv_bias, send_lists, kernel_map):
    act, grad, total_a, total_b = layer(
        features.reshape(16, 512, CH),
        cotangent.reshape(16, 512, CH),
        kernel_weight.reshape(27, CH, CH),
        conv_bias.reshape(1, CH),
        send_lists[0, 0].T,
        kernel_map[0, 0],
    )
    act, grad, weight_total, bias_total = deliver(
        act, grad, total_a.reshape(-1, CH), total_b.reshape(-1, CH)
    )
    return (
        act.reshape(features.shape),
        grad.reshape(features.shape),
        weight_total.reshape(kernel_weight.shape),
        bias_total.reshape(CH),
    )


def solution(mesh):
    block = P("gx", "gy", None, None, None, None, None)
    return jax.shard_map(
        shards,
        mesh=mesh,
        in_specs=(block, block, P(), P(), P("gx", "gy", None, None), P("gx", "gy", None, None)),
        out_specs=(block, block, P(), P()),
        check_vma=False,
    )
```

```python
import functools
import math

import jax
import jax.numpy as jnp
from jax import lax
from jax.experimental import pallas as pl
from jax.experimental.pallas import tpu as pltpu
from jax.sharding import PartitionSpec as P

MESH = pl.DeviceIdType.MESH
F32, BF16 = jnp.float32, jnp.bfloat16
DIRECTIONS = ((-1, -1), (-1, 0), (-1, 1), (0, -1), (0, 1), (1, -1), (1, 0), (1, 1))
CH = 128
ENTRY = 52
SENT = 320
A_LOW, A_HIGH, E_LOW, E_HIGH, C_LOW, C_HIGH, EDGES = 0, 8, 16, 24, 32, 40, 48
SP, SQ, SR = 1711, 171, 17
LINE = 136


def rows16(start):
    return pl.multiple_of(start, 16)


def natural_to_bricks(nat, x32):
    def stage(b, _):
        block = nat[b].astype(F32)
        for ae in range(64):
            at = (1 + ae // 8) * SP + (1 + ae % 8) * SQ + SR
            x32[pl.ds(at + b, 8, stride=SR)] = block[ae * 8 : ae * 8 + 8]
        return 0

    lax.fori_loop(0, 16, stage, 0)


def each_inner(x32, put):
    def plane(a, _):
        for e in range(8):
            for c in range(8):
                at = (1 + a) * SP + (1 + e) * SQ + (1 + c) * SR
                put(a, e, c, x32[pl.ds(at, 16)].astype(BF16))
        return 0

    lax.fori_loop(0, 8, plane, 0)


def bricks_to_natural(lin, nat):
    def unstage(b, _):
        for ae in range(0, 64, 2):
            pair = [lin[pl.ds((ae + k) * LINE + b, 8, stride=17)] for k in range(2)]
            nat[b, ae * 8 : ae * 8 + 16] = jnp.concatenate(pair, axis=0).astype(BF16)
        return 0

    lax.fori_loop(0, 16, unstage, 0)


def own_table(x32, t32, faces):
    def one(b, _):
        base = b * ENTRY
        for low, p in ((A_LOW, 1), (A_HIGH, 8)):
            for e in range(8):
                t32[base + low + e] = x32[pl.ds(p * SP + (1 + e) * SQ + SR + b, 8, stride=SR)]
        for low, q in ((E_LOW, 1), (E_HIGH, 8)):
            for a in range(8):
                t32[base + low + a] = x32[pl.ds((1 + a) * SP + q * SQ + SR + b, 8, stride=SR)]
        for low, r in ((C_LOW, 1), (C_HIGH, 8)):
            for a in range(8):
                t32[base + low + a] = x32[pl.ds((1 + a) * SP + SQ + r * SR + b, 8, stride=SQ)]
        for n, (q, r) in enumerate(((1, 1), (1, 8), (8, 1), (8, 8))):
            t32[base + EDGES + n] = x32[pl.ds(SP + q * SQ + r * SR + b, 8, stride=SP)]
        faces[b, 0:128] = t32[pl.ds(base, 16)].reshape(128, CH).astype(BF16)
        for n, low in enumerate((E_LOW, E_HIGH, C_LOW, C_HIGH)):
            lines = t32[pl.ds(base + low + 1, 6)].reshape(48, CH)
            faces[b, 128 + 48 * n : 176 + 48 * n] = lines.astype(BF16)
        return 0

    lax.fori_loop(0, 16, one, 0)


def received_table(received, t32, wide):
    def one(n, _):
        base = (16 + n) * ENTRY
        k, r = n // 4, n % 4
        sides = received[k, r, 0:128].astype(F32)
        wide[0:128] = sides
        t32[pl.ds(base, 16)] = sides.reshape(16, 8, CH)
        for m, low in enumerate((E_LOW, E_HIGH, C_LOW, C_HIGH)):
            lines = received[k, r, 128 + 48 * m : 176 + 48 * m].astype(F32)
            t32[pl.ds(base + low + 1, 6)] = lines.reshape(6, 8, CH)
            if m < 2:
                wide[136 + 64 * m : 184 + 64 * m] = lines
        for a, side in ((0, 0), (7, 64)):
            low, high = wide[side : side + 8], wide[side + 56 : side + 64]
            t32[base + E_LOW + a] = low
            t32[base + E_HIGH + a] = high
            wide[128 + 8 * a : 136 + 8 * a] = low
            wide[192 + 8 * a : 200 + 8 * a] = high
            t32[base + C_LOW + a] = wide[pl.ds(side, 8, stride=8)]
            t32[base + C_HIGH + a] = wide[pl.ds(side + 7, 8, stride=8)]
        for m, start in enumerate((128, 135, 192, 199)):
            t32[base + EDGES + m] = wide[pl.ds(start, 8, stride=8)]
        return 0

    lax.fori_loop(0, 32, one, 0)
    t32[pl.ds(48 * ENTRY, ENTRY)] = jnp.zeros((ENTRY, 8, CH), F32)


def rim(kmap, t32, x32, planes, x):
    a_planes, e_planes, c_planes = planes

    def one(b, _):
        for o in range(27):
            a, e, c = o // 9 - 1, o // 3 % 3 - 1, o % 3 - 1
            if a == e == c == 0:
                continue
            base = kmap[b, o] * ENTRY
            p, q, r = [1 + 8 * (s > 0) - (s < 0) for s in (a, e, c)]
            dest = p * SP + q * SQ + r * SR + b
            fe, fc = 7 * (e < 0), 7 * (c < 0)
            if a != 0:
                side = base + (A_HIGH if a < 0 else A_LOW)
                if e == 0 and c == 0:
                    for n in range(8):
                        x32[pl.ds(dest + n * SQ, 8, stride=SR)] = t32[side + n]
                elif c == 0:
                    x32[pl.ds(dest, 8, stride=SR)] = t32[side + fe]
                elif e == 0:
                    line = base + (C_HIGH if c < 0 else C_LOW) + 7 * (a < 0)
                    x32[pl.ds(dest, 8, stride=SQ)] = t32[line]
                else:
                    x32[pl.ds(dest, 1)] = t32[side + fe][fc : fc + 1]
            elif e != 0:
                side = base + (E_HIGH if e < 0 else E_LOW)
                if c == 0:
                    for n in range(8):
                        x32[pl.ds(dest + n * SP, 8, stride=SR)] = t32[side + n]
                else:
                    x32[pl.ds(dest, 8, stride=SP)] = t32[base + EDGES + 2 * (e < 0) + (c < 0)]
            else:
                side = base + (C_HIGH if c < 0 else C_LOW)
                for n in range(8):
                    x32[pl.ds(dest + n * SP, 8, stride=SQ)] = t32[side + n]
        return 0

    lax.fori_loop(0, 16, one, 0)

    def pack(p, q, r):
        cell = x32[pl.ds(p * SP + q * SQ + r * SR, 16)].astype(BF16)
        if x is not None:
            x[p, q, r] = cell
        return cell

    def line(q, _):
        for side in range(2):
            for r in range(10):
                a_planes[side, q // 2, q % 2, r] = pack(9 * side, q, r)
        return 0

    lax.fori_loop(0, 10, line, 0)

    def ring(p, _):
        for side in range(2):
            for r in range(10):
                e_planes[side, p // 2, p % 2, r] = pack(p, 9 * side, r)
            for q in range(1, 9):
                c_planes[side, p // 2, p % 2, q] = pack(p, q, 9 * side)
        return 0

    lax.fori_loop(1, 9, ring, 0)


def clear_rims(planes, x, g):
    _, e_planes, c_planes = planes
    row = jnp.zeros((10, 16, CH), BF16)
    for side in range(2):
        for p in (0, 9):
            e_planes[side, p // 2, p % 2] = row
            c_planes[side, p // 2, p % 2] = row
        for p in range(1, 9):
            for q in (0, 9):
                c_planes[side, p // 2, p % 2, q] = row[0]

    def clear(n, _):
        for f in (x, g):
            for side in (0, 9):
                f[side, n] = row
                f[n, side] = row
                f[n, :, side] = row
        return 0

    lax.fori_loop(0, 10, clear, 0)


def wide_weights(w, w2, wa, back):
    zero = jnp.zeros((CH, CH), BF16)

    def put(ref, n, c, k, j, tap):
        ref[n, (c * 4 + k) * CH : (c * 4 + k + 1) * CH, j * CH : (j + 1) * CH] = tap

    for c in range(3):
        for k, j in ((0, 1), (3, 0)):
            for n in range(3):
                put(w2, n, c, k, j, zero)
            for n in range(2):
                put(wa, n, c, k, j, zero)
    for a in range(3):
        for e in range(3):
            for c in range(3):
                if back:
                    tap = w[(2 - a) * 9 + (2 - e) * 3 + 2 - c].astype(F32).T.astype(BF16)
                else:
                    tap = w[a * 9 + e * 3 + c]
                for j in range(2):
                    put(w2, e, c, a + j, j, tap)
                    if a != 1:
                        put(wa, a // 2, c, e + j, j, tap)


def inner_conv(x, w2, wa, lin, lo, hi):
    def pair(i, _):
        both = None
        for e in range(3):
            parts = [
                x[2 * i + k, e : e + 8, c : c + 8].reshape(1024, CH)
                for c in range(3)
                for k in (1, 2)
            ]
            taps = jnp.concatenate(
                [w2[e, (c * 4 + 1) * CH : (c * 4 + 3) * CH] for c in range(3)], axis=0
            )
            term = jnp.dot(jnp.concatenate(parts, axis=1), taps, preferred_element_type=F32)
            both = term if both is None else both + term
        for j in range(2):
            plane = x[2 * i + 3 * j].reshape(5, 2, 10, 16, CH)
            parts = [
                plane[k // 2 : k // 2 + 4, k % 2, c : c + 8].reshape(512, CH)
                for c in range(3)
                for k in range(4)
            ]
            one = jnp.dot(jnp.concatenate(parts, axis=1), wa[j], preferred_element_type=F32)
            for e in range(8):
                at = pl.multiple_of(((2 * i + j) * 8 + e) * LINE, 8)
                lin[pl.ds(at, 128)] = (
                    both[e * 128 : e * 128 + 128, j * CH : (j + 1) * CH]
                    + one[e // 2 * 128 : e // 2 * 128 + 128, e % 2 * CH : (e % 2 + 1) * CH]
                )
        return 0

    lax.fori_loop(lo, hi, pair, 0)


def rim_conv(planes, w2, wa, lin):
    a_planes, e_planes, c_planes = planes

    def windows(ref, side):
        parts = [
            ref[side, k // 2 : k // 2 + 4, k % 2, s : s + 8].reshape(512, CH)
            for s in range(3)
            for k in range(4)
        ]
        return jnp.concatenate(parts, axis=1)

    for side in range(2):
        near = 7 * side
        result = jnp.dot(windows(a_planes, side), wa[side], preferred_element_type=F32)
        for i in range(4):
            for j in range(2):
                at = (near * 8 + 2 * i + j) * LINE
                lin[at : at + 128] += result[i * 128 : i * 128 + 128, j * CH : (j + 1) * CH]
        result = jnp.dot(windows(e_planes, side), w2[2 * side], preferred_element_type=F32)
        for i in range(4):
            for j in range(2):
                at = ((2 * i + j) * 8 + near) * LINE
                lin[at : at + 128] += result[i * 128 : i * 128 + 128, j * CH : (j + 1) * CH]
        taps = jnp.concatenate(
            [w2[e, 2 * side * 4 * CH : (2 * side + 1) * 4 * CH] for e in range(3)], axis=0
        )
        result = jnp.dot(windows(c_planes, side), taps, preferred_element_type=F32)
        for i in range(4):
            for j in range(2):
                for e in range(8):
                    at = ((2 * i + j) * 8 + e) * LINE + near * 16
                    row = (i * 8 + e) * 16
                    lin[at : at + 16] += result[row : row + 16, j * CH : (j + 1) * CH]


def inside(i, j):
    return (i >= 0) & (i < lax.axis_size("gx")) & (j >= 0) & (j < lax.axis_size("gy"))


def greet_neighbours(barrier):
    i, j = lax.axis_index("gx"), lax.axis_index("gy")
    count = jnp.int32(0)
    for dx, dy in DIRECTIONS:
        there = inside(i + dx, j + dy)
        count += there.astype(jnp.int32)

        @pl.when(there)
        def _():
            pl.semaphore_signal(
                barrier, inc=1, device_id=(i + dx, j + dy), device_id_type=MESH
            )

    return count


def pack_lists(lists, faces, sending):
    for k in range(8):
        for r in range(4):
            sending[k, r] = faces[jnp.minimum(lists[r, k], 15)]


def halo_copy(k, sending, received, send_sem, recv_sem):
    i, j = lax.axis_index("gx"), lax.axis_index("gy")
    dx, dy = DIRECTIONS[k]
    return pltpu.make_async_remote_copy(
        src_ref=sending.at[k],
        dst_ref=received.at[k],
        send_sem=send_sem.at[k],
        recv_sem=recv_sem.at[k],
        device_id=(i + dx, j + dy),
        device_id_type=MESH,
    )


ORDER = (0, 2, 5, 7, 3, 4, 1, 6)


def start_halo(*halo):
    i, j = lax.axis_index("gx"), lax.axis_index("gy")
    for k in ORDER:
        dx, dy = DIRECTIONS[k]

        @pl.when(inside(i + dx, j + dy))
        def _():
            halo_copy(k, *halo).start()


def wait_halo(*halo):
    i, j = lax.axis_index("gx"), lax.axis_index("gy")
    for k in ORDER:
        dx, dy = DIRECTIONS[k]

        @pl.when(inside(i - dx, j - dy))
        def _():
            halo_copy(k, *halo).wait_recv()


def wait_halo_sent(*halo):
    i, j = lax.axis_index("gx"), lax.axis_index("gy")
    for k in ORDER:
        dx, dy = DIRECTIONS[k]

        @pl.when(inside(i + dx, j + dy))
        def _():
            halo_copy(k, *halo).wait_send()


BLOCKS = 28
ROWS = BLOCKS * CH


def place():
    i = lax.axis_index("gx")
    return i // 2, i % 2, lax.axis_index("gy")


def sibling_copy(src, dst, sems, n):
    z, core, j = place()
    return pltpu.make_async_remote_copy(
        src_ref=src, dst_ref=dst, send_sem=sems.at[0, n], recv_sem=sems.at[1, n],
        device_id=(2 * z + 1 - core, j), device_id_type=MESH,
    )


def in_plane(n):
    z, core, j = place()
    return 2 * (n // 4) + core, (n % 4) * 4 + j % 4


def plane_copy(src, dst, sems, d):
    z, core, j = place()
    return pltpu.make_async_remote_copy(
        src_ref=src, dst_ref=dst, send_sem=sems.at[0, d], recv_sem=sems.at[1, d],
        device_id=in_plane((z * 4 + j // 4 + d) % 16), device_id_type=MESH,
    )


def in_column(d):
    z, core, j = place()
    return 2 * z + core, j // 4 * 4 + (j + d) % 4


def column_copy(src, dst, sems, d):
    return pltpu.make_async_remote_copy(
        src_ref=src, dst_ref=dst, send_sem=sems.at[0, d], recv_sem=sems.at[1, d],
        device_id=in_column(d), device_id_type=MESH,
    )


def greet_summers(barrier):
    z, core, j = place()

    def greet(where):
        pl.semaphore_signal(barrier, inc=1, device_id=where, device_id_type=MESH)

    greet((2 * z + 1 - core, j))
    for d in range(1, 16):
        greet(in_plane((z * 4 + j // 4 + d) % 16))
    for d in range(1, 4):
        greet(in_column(d))
    return 19


def settle(lin):
    def line(ae, _):
        at = pl.multiple_of(ae * LINE, 8)
        block = lin[pl.ds(at, 128)]
        for c in range(1, 8):
            lin[pl.ds(at + c * 17, 16)] = block[c * 16 : c * 16 + 16]
        return 0

    lax.fori_loop(0, 64, line, 0)


def weight_terms(x, gt, d32):
    def block(e, c, a):
        at = (e * 9 + c * 3 + a) * CH
        return slice(at, at + CH)

    for j in range(2):
        pairs = jnp.concatenate(
            [
                jnp.concatenate(
                    [
                        gt[i, j * CH : (j + 1) * CH, (2 * m + n) * CH : (2 * m + n + 1) * CH]
                        for i in range(4)
                        for m in range(4)
                    ],
                    axis=1,
                )
                for n in range(2)
            ],
            axis=0,
        )
        for c in range(3):
            parts = [
                jnp.concatenate(
                    [
                        x[2 * i + 3 * j]
                        .reshape(5, 2, 10, 16, CH)[k // 2 : k // 2 + 4, k % 2, c : c + 8]
                        .reshape(512, CH)
                        for i in range(4)
                    ],
                    axis=0,
                )
                for k in range(4)
            ]
            terms = jnp.dot(pairs, jnp.concatenate(parts, axis=1), preferred_element_type=F32)
            for e in range(3):
                term = (
                    terms[:CH, e * CH : (e + 1) * CH]
                    + terms[CH:, (e + 1) * CH : (e + 2) * CH]
                )
                d32[block(e, c, 2 * j)] = term.T
    slopes = jnp.concatenate([gt[i] for i in range(4)], axis=1)
    for e in range(3):
        for c in range(3):
            parts = [
                jnp.concatenate(
                    [x[2 * i + k, e : e + 8, c : c + 8].reshape(1024, CH) for i in range(4)],
                    axis=0,
                )
                for k in (1, 2)
            ]
            terms = jnp.dot(
                slopes, jnp.concatenate(parts, axis=1), preferred_element_type=F32
            )
            d32[block(e, c, 0)] += terms[CH:, :CH].T
            d32[block(e, c, 1)] = (terms[:CH, :CH] + terms[CH:, CH:]).T
            d32[block(e, c, 2)] += terms[:CH, CH:].T


class Summed:
    def __init__(self, d32, first, refs):
        self.d32, self.first = d32, first
        (
            self.d16, self.from_sibling, self.h32, self.h16, self.from_plane, self.column,
            self.share, self.gathered, self.whole, self.sib, self.out, self.col, self.back,
        ) = refs
        self.half = self.d16.shape[0]
        self.rows = self.share.shape[0]
        z, self.core, j = place()
        self.n, self.y = z * 4 + j // 4, j % 4

    def first_pair(self):
        return sibling_copy(self.d16, self.from_sibling, self.sib, 0)

    def outward(self, d):
        there = (self.n + d) % 16
        return plane_copy(self.h16.at[there], self.from_plane.at[d - 1], self.out, d)

    def upward(self, d):
        return column_copy(self.column.at[self.y], self.column.at[self.y], self.col, d)

    def inward(self, d):
        return plane_copy(self.share, self.gathered.at[self.n], self.back, d)

    def last_pair(self):
        return sibling_copy(self.gathered, self.whole.at[self.core], self.sib, 1)

    def start_pair(self):
        other = pl.ds(rows16(self.first + (1 - self.core) * self.half), self.half)
        self.d16[...] = self.d32[other].astype(BF16)
        self.first_pair().start()

    def start_plane(self):
        self.first_pair().wait()
        mine = pl.ds(rows16(self.first + self.core * self.half), self.half)
        self.h32[...] = self.d32[mine] + self.from_sibling[...].astype(F32)
        self.h16[...] = self.h32[...].astype(BF16).reshape(self.h16.shape)
        for d in range(1, 16):
            self.outward(d).start()

    def start_column(self):
        for d in range(1, 16):
            self.outward(d).wait()
        part = self.h32[pl.ds(rows16(self.n * self.rows), self.rows)]
        for d in range(1, 16):
            part = part + self.from_plane[d - 1].astype(F32)
        self.column[self.y] = part.astype(BF16)
        for d in range(1, 4):
            self.upward(d).start()

    def start_back(self):
        for d in range(1, 4):
            self.upward(d).wait()
        part = self.column[0].astype(F32)
        for m in range(1, 4):
            part = part + self.column[m].astype(F32)
        voxels = lax.axis_size("gx") * lax.axis_size("gy") * 8192
        self.share[...] = (part * (1.0 / math.sqrt(voxels))).astype(BF16)
        self.gathered[self.n] = self.share[...]
        for d in range(1, 16):
            self.inward(d).start()

    def start_last(self):
        for d in range(1, 16):
            self.inward(d).wait()
        self.last_pair().start()
        self.whole[self.core] = self.gathered[...]

    def finish(self):
        self.last_pair().wait()


def sum_scratch(blocks):
    half = blocks * CH // 2
    rows = half // 16
    return [
        pltpu.VMEM((half, CH), BF16),
        pltpu.VMEM((half, CH), BF16),
        pltpu.VMEM((half, CH), F32),
        pltpu.VMEM((16, rows, CH), BF16),
        pltpu.VMEM((15, rows, CH), BF16),
        pltpu.VMEM((4, rows, CH), BF16),
        pltpu.VMEM((rows, CH), BF16),
        pltpu.VMEM((16, rows, CH), BF16),
        pltpu.VMEM((2, 16, rows, CH), BF16),
        pltpu.SemaphoreType.DMA((2, 2)),
        pltpu.SemaphoreType.DMA((2, 16)),
        pltpu.SemaphoreType.DMA((2, 4)),
        pltpu.SemaphoreType.DMA((2, 16)),
    ]


def credit_neighbours(credit):
    i, j = lax.axis_index("gx"), lax.axis_index("gy")
    for dx, dy in DIRECTIONS:

        @pl.when(inside(i - dx, j - dy))
        def _():
            pl.semaphore_signal(
                credit, inc=1, device_id=(i - dx, j - dy), device_id_type=MESH
            )


def kernel(
    vol, cot, w, bias, lists, kmap, act, grad, total,
    nat, lin, x32, t32, wide, ct, faces, sending, received, x, g,
    a_planes, e_planes, c_planes, w2, wa, gt, d32, send_sem, recv_sem, own_sems, credit, *sums,
):
    halo = (sending, received, send_sem, recv_sem)
    planes = (a_planes, e_planes, c_planes)
    terms_sum = Summed(d32, 0, sums)
    take_vol = pltpu.make_async_copy(vol, nat, own_sems.at[0])
    take_cot = pltpu.make_async_copy(cot, nat, own_sems.at[1])
    give_act = pltpu.make_async_copy(nat, act, own_sems.at[2])
    give_grad = pltpu.make_async_copy(nat, grad, own_sems.at[3])
    give_total = pltpu.make_async_copy(terms_sum.whole, total, own_sems.at[4])
    take_vol.start()
    barrier = pltpu.get_barrier_semaphore()
    neighbours = greet_neighbours(barrier)
    summers = greet_summers(barrier)

    take_vol.wait()
    natural_to_bricks(nat, x32)
    take_cot.start()
    own_table(x32, t32, faces)
    pack_lists(lists, faces, sending)
    pl.semaphore_wait(barrier, neighbours + summers)
    start_halo(*halo)

    def put_x(a, e, c, v):
        x[1 + a, 1 + e, 1 + c] = v

    each_inner(x32, put_x)

    def put_cot(a, e, c, v):
        ct[pl.ds(rows16((a * 64 + e * 8 + c) * 16), 16)] = v

    take_cot.wait()
    natural_to_bricks(nat, x32)
    each_inner(x32, put_cot)
    wide_weights(w, w2, wa, False)
    clear_rims(planes, x, g)
    inner_conv(x, w2, wa, lin, 0, 4)
    wait_halo(*halo)
    received_table(received, t32, wide)
    credit_neighbours(credit)
    rim(kmap, t32, x32, planes, x)
    rim_conv(planes, w2, wa, lin)

    def finish(ae, _):
        a, e = ae // 8, ae % 8
        line = pl.multiple_of(ae * LINE, 8)
        linear = lin[pl.ds(line, 128)] + bias[...]
        s = 1.0 / (1.0 + jnp.exp(-linear))
        activated = linear * s
        slope = ct[pl.ds(rows16(ae * 128), 128)].astype(F32) * s * (1.0 + linear * (1.0 - s))
        lin[pl.ds(line, 128)] = activated
        for c in range(8):
            at = (1 + a) * SP + (1 + e) * SQ + (1 + c) * SR
            x32[pl.ds(at, 16)] = slope[c * 16 : c * 16 + 16]
        g[1 + a, 1 + e, 1:9] = slope.astype(BF16).reshape(8, 16, CH)
        return 0

    lax.fori_loop(0, 64, finish, 0)
    wait_halo_sent(*halo)
    own_table(x32, t32, faces)
    pack_lists(lists, faces, sending)
    pl.semaphore_wait(credit, neighbours)
    start_halo(*halo)

    def turn(p, sums):
        for m in range(8):
            block = g[1 + p, 1 + m, 1:9].astype(F32).reshape(128, CH)
            gt[p // 2, pl.ds(rows16((p % 2) * CH), CH), m * 128 : m * 128 + 128] = (
                block.T.astype(BF16)
            )
            sums = sums + block
        return sums

    totals = lax.fori_loop(0, 8, turn, jnp.zeros((128, CH), F32))
    d32[27 * CH :] = jnp.concatenate(
        [jnp.sum(totals, axis=0, keepdims=True), jnp.zeros((127, CH), F32)], axis=0
    )

    weight_terms(x, gt, d32)
    terms_sum.start_pair()
    settle(lin)
    bricks_to_natural(lin, nat)
    give_act.start()
    wide_weights(w, w2, wa, True)
    terms_sum.start_plane()
    inner_conv(g, w2, wa, lin, 0, 3)
    terms_sum.start_column()
    inner_conv(g, w2, wa, lin, 3, 4)
    terms_sum.start_back()
    wait_halo(*halo)
    received_table(received, t32, wide)
    rim(kmap, t32, x32, planes, None)
    rim_conv(planes, w2, wa, lin)
    terms_sum.start_last()
    settle(lin)
    give_act.wait()
    bricks_to_natural(lin, nat)
    give_grad.start()
    terms_sum.finish()
    give_total.start()
    wait_halo_sent(*halo)
    give_total.wait()
    give_grad.wait()


def layer(vol, cot, w, bias, lists, kmap):
    vm = pl.BlockSpec(memory_space=pltpu.VMEM)
    sm = pl.BlockSpec(memory_space=pltpu.SMEM)
    hbm = pl.BlockSpec(memory_space=pl.ANY)
    field = pltpu.VMEM((10, 10, 10, 16, CH), BF16)
    planes = pltpu.VMEM((2, 5, 2, 10, 16, CH), BF16)
    return pl.pallas_call(
        kernel,
        out_shape=(
            jax.ShapeDtypeStruct((16, 512, CH), BF16),
            jax.ShapeDtypeStruct((16, 512, CH), BF16),
            jax.ShapeDtypeStruct((2, 16, BLOCKS * 4, CH), BF16),
        ),
        in_specs=[hbm, hbm, vm, vm, sm, sm],
        out_specs=(hbm, hbm, hbm),
        scratch_shapes=[
            pltpu.VMEM((16, 512, CH), BF16),
            pltpu.VMEM((64 * LINE, CH), F32),
            pltpu.VMEM((10 * SP + 2, CH), F32),
            pltpu.VMEM((49 * ENTRY, 8, CH), F32),
            pltpu.VMEM((256, CH), F32),
            pltpu.VMEM((8192, CH), BF16),
            pltpu.VMEM((16, SENT, CH), BF16),
            pltpu.VMEM((8, 4, SENT, CH), BF16),
            pltpu.VMEM((8, 4, SENT, CH), BF16),
            field,
            field,
            planes,
            planes,
            planes,
            pltpu.VMEM((3, 12 * CH, 2 * CH), BF16),
            pltpu.VMEM((2, 12 * CH, 2 * CH), BF16),
            pltpu.VMEM((4, 2 * CH, 1024), BF16),
            pltpu.VMEM((ROWS, CH), F32),
            pltpu.SemaphoreType.DMA((8,)),
            pltpu.SemaphoreType.DMA((8,)),
            pltpu.SemaphoreType.DMA((5,)),
            pltpu.SemaphoreType.REGULAR,
            *sum_scratch(BLOCKS),
        ],
        compiler_params=pltpu.CompilerParams(
            collective_id=0, has_side_effects=True, vmem_limit_bytes=63 * 2**20
        ),
        name="layer",
    )(vol, cot, w, bias, lists, kmap)


PIECES = 4


def deliver_kernel(
    act, grad, total, act_out, grad_out, weight_out, bias_out, held, terms, weights, sems, more
):
    def piece(n, m, src, dst):
        at = pl.ds(m * 16 // PIECES, 16 // PIECES)
        return (
            pltpu.make_async_copy(src.at[at], held.at[n, at], sems.at[0, n, m]),
            pltpu.make_async_copy(held.at[n, at], dst.at[at], sems.at[1, n, m]),
        )

    take_terms = pltpu.make_async_copy(total, terms, more.at[0])
    give_weights = pltpu.make_async_copy(weights, weight_out, more.at[1])
    pieces = [
        piece(n, m, src, dst)
        for n, (src, dst) in enumerate(((act, act_out), (grad, grad_out)))
        for m in range(PIECES)
    ]
    take_terms.start()
    for take, _ in pieces:
        take.start()
    take_terms.wait()
    for n in range(27):
        weights[n % 3 * 9 + n // 3] = terms[n * CH : (n + 1) * CH].astype(F32)
    bias_out[...] = terms[27 * CH : 27 * CH + 16].astype(F32)[0:1]
    give_weights.start()
    for take, give in pieces:
        take.wait()
        give.start()
    for _, give in pieces:
        give.wait()
    give_weights.wait()


def deliver(act, grad, total):
    vm = pl.BlockSpec(memory_space=pltpu.VMEM)
    hbm = pl.BlockSpec(memory_space=pl.ANY)
    return pl.pallas_call(
        deliver_kernel,
        out_shape=(
            jax.ShapeDtypeStruct(act.shape, BF16),
            jax.ShapeDtypeStruct(grad.shape, BF16),
            jax.ShapeDtypeStruct((27, CH, CH), F32),
            jax.ShapeDtypeStruct((1, CH), F32),
        ),
        in_specs=[hbm, hbm, hbm],
        out_specs=(hbm, hbm, hbm, vm),
        scratch_shapes=[
            pltpu.VMEM((2, 16, 512, CH), BF16),
            pltpu.VMEM((ROWS, CH), BF16),
            pltpu.VMEM((27, CH, CH), F32),
            pltpu.SemaphoreType.DMA((2, 2, PIECES)),
            pltpu.SemaphoreType.DMA((2,)),
        ],
        compiler_params=pltpu.CompilerParams(vmem_limit_bytes=63 * 2**20),
        name="deliver",
    )(act, grad, total)


def shards(features, cotangent, kernel_weight, conv_bias, send_lists, kernel_map):
    act, grad, total = layer(
        features.reshape(16, 512, CH),
        cotangent.reshape(16, 512, CH),
        kernel_weight.reshape(27, CH, CH),
        conv_bias.reshape(1, CH),
        send_lists[0, 0].T,
        kernel_map[0, 0],
    )
    act, grad, weight_total, bias_total = deliver(act, grad, total.reshape(ROWS, CH))
    return (
        act.reshape(features.shape),
        grad.reshape(features.shape),
        weight_total.reshape(kernel_weight.shape),
        bias_total.reshape(CH),
    )


def solution(mesh):
    block = P("gx", "gy", None, None, None, None, None)
    return jax.shard_map(
        shards,
        mesh=mesh,
        in_specs=(block, block, P(), P(), P("gx", "gy", None, None), P("gx", "gy", None, None)),
        out_specs=(block, block, P(), P()),
        check_vma=False,
    )
```

```python
import functools
import math

import jax
import jax.numpy as jnp
from jax import lax
from jax.experimental import pallas as pl
from jax.experimental.pallas import tpu as pltpu
from jax.sharding import PartitionSpec as P

MESH = pl.DeviceIdType.MESH
F32, BF16 = jnp.float32, jnp.bfloat16
DIRECTIONS = ((-1, -1), (-1, 0), (-1, 1), (0, -1), (0, 1), (1, -1), (1, 0), (1, 1))
CH = 128
ENTRY = 52
SENT = 320
A_LOW, A_HIGH, E_LOW, E_HIGH, C_LOW, C_HIGH, EDGES = 0, 8, 16, 24, 32, 40, 48
SP, SQ, SR = 1711, 171, 17
LINE = 136


def rows16(start):
    return pl.multiple_of(start, 16)


def natural_to_bricks(nat, x32):
    def stage(b, _):
        block = nat[b].astype(F32)
        for ae in range(64):
            at = (1 + ae // 8) * SP + (1 + ae % 8) * SQ + SR
            x32[pl.ds(at + b, 8, stride=SR)] = block[ae * 8 : ae * 8 + 8]
        return 0

    lax.fori_loop(0, 16, stage, 0)


def each_inner(x32, put):
    def plane(a, _):
        for e in range(8):
            for c in range(8):
                at = (1 + a) * SP + (1 + e) * SQ + (1 + c) * SR
                put(a, e, c, x32[pl.ds(at, 16)].astype(BF16))
        return 0

    lax.fori_loop(0, 8, plane, 0)


def bricks_to_natural(lin, nat):
    def unstage(b, _):
        for ae in range(0, 64, 2):
            pair = [lin[pl.ds((ae + k) * LINE + b, 8, stride=17)] for k in range(2)]
            nat[b, ae * 8 : ae * 8 + 16] = jnp.concatenate(pair, axis=0).astype(BF16)
        return 0

    lax.fori_loop(0, 16, unstage, 0)


def own_table(x32, t32, faces):
    def one(b, _):
        base = b * ENTRY
        for low, p in ((A_LOW, 1), (A_HIGH, 8)):
            for e in range(8):
                t32[base + low + e] = x32[pl.ds(p * SP + (1 + e) * SQ + SR + b, 8, stride=SR)]
        for low, q in ((E_LOW, 1), (E_HIGH, 8)):
            for a in range(8):
                t32[base + low + a] = x32[pl.ds((1 + a) * SP + q * SQ + SR + b, 8, stride=SR)]
        for low, r in ((C_LOW, 1), (C_HIGH, 8)):
            for a in range(8):
                t32[base + low + a] = x32[pl.ds((1 + a) * SP + SQ + r * SR + b, 8, stride=SQ)]
        for n, (q, r) in enumerate(((1, 1), (1, 8), (8, 1), (8, 8))):
            t32[base + EDGES + n] = x32[pl.ds(SP + q * SQ + r * SR + b, 8, stride=SP)]
        faces[b, 0:128] = t32[pl.ds(base, 16)].reshape(128, CH).astype(BF16)
        for n, low in enumerate((E_LOW, E_HIGH, C_LOW, C_HIGH)):
            lines = t32[pl.ds(base + low + 1, 6)].reshape(48, CH)
            faces[b, 128 + 48 * n : 176 + 48 * n] = lines.astype(BF16)
        return 0

    lax.fori_loop(0, 16, one, 0)


def received_table(received, t32, wide):
    def one(n, _):
        base = (16 + n) * ENTRY
        k, r = n // 4, n % 4
        sides = received[k, r, 0:128].astype(F32)
        wide[0:128] = sides
        t32[pl.ds(base, 16)] = sides.reshape(16, 8, CH)
        for m, low in enumerate((E_LOW, E_HIGH, C_LOW, C_HIGH)):
            lines = received[k, r, 128 + 48 * m : 176 + 48 * m].astype(F32)
            t32[pl.ds(base + low + 1, 6)] = lines.reshape(6, 8, CH)
            if m < 2:
                wide[136 + 64 * m : 184 + 64 * m] = lines
        for a, side in ((0, 0), (7, 64)):
            low, high = wide[side : side + 8], wide[side + 56 : side + 64]
            t32[base + E_LOW + a] = low
            t32[base + E_HIGH + a] = high
            wide[128 + 8 * a : 136 + 8 * a] = low
            wide[192 + 8 * a : 200 + 8 * a] = high
            t32[base + C_LOW + a] = wide[pl.ds(side, 8, stride=8)]
            t32[base + C_HIGH + a] = wide[pl.ds(side + 7, 8, stride=8)]
        for m, start in enumerate((128, 135, 192, 199)):
            t32[base + EDGES + m] = wide[pl.ds(start, 8, stride=8)]
        return 0

    lax.fori_loop(0, 32, one, 0)
    t32[pl.ds(48 * ENTRY, ENTRY)] = jnp.zeros((ENTRY, 8, CH), F32)


def rim(kmap, t32, x32, planes, x):
    a_planes, e_planes, c_planes = planes

    def one(b, _):
        for o in range(27):
            a, e, c = o // 9 - 1, o // 3 % 3 - 1, o % 3 - 1
            if a == e == c == 0:
                continue
            base = kmap[b, o] * ENTRY
            p, q, r = [1 + 8 * (s > 0) - (s < 0) for s in (a, e, c)]
            dest = p * SP + q * SQ + r * SR + b
            fe, fc = 7 * (e < 0), 7 * (c < 0)
            if a != 0:
                side = base + (A_HIGH if a < 0 else A_LOW)
                if e == 0 and c == 0:
                    for n in range(8):
                        x32[pl.ds(dest + n * SQ, 8, stride=SR)] = t32[side + n]
                elif c == 0:
                    x32[pl.ds(dest, 8, stride=SR)] = t32[side + fe]
                elif e == 0:
                    line = base + (C_HIGH if c < 0 else C_LOW) + 7 * (a < 0)
                    x32[pl.ds(dest, 8, stride=SQ)] = t32[line]
                else:
                    x32[pl.ds(dest, 1)] = t32[side + fe][fc : fc + 1]
            elif e != 0:
                side = base + (E_HIGH if e < 0 else E_LOW)
                if c == 0:
                    for n in range(8):
                        x32[pl.ds(dest + n * SP, 8, stride=SR)] = t32[side + n]
                else:
                    x32[pl.ds(dest, 8, stride=SP)] = t32[base + EDGES + 2 * (e < 0) + (c < 0)]
            else:
                side = base + (C_HIGH if c < 0 else C_LOW)
                for n in range(8):
                    x32[pl.ds(dest + n * SP, 8, stride=SQ)] = t32[side + n]
        return 0

    lax.fori_loop(0, 16, one, 0)

    def pack(p, q, r):
        cell = x32[pl.ds(p * SP + q * SQ + r * SR, 16)].astype(BF16)
        if x is not None:
            x[p, q, r] = cell
        return cell

    def line(q, _):
        for side in range(2):
            for r in range(10):
                a_planes[side, q // 2, q % 2, r] = pack(9 * side, q, r)
        return 0

    lax.fori_loop(0, 10, line, 0)

    def ring(p, _):
        for side in range(2):
            for r in range(10):
                e_planes[side, p // 2, p % 2, r] = pack(p, 9 * side, r)
            for q in range(1, 9):
                c_planes[side, p // 2, p % 2, q] = pack(p, q, 9 * side)
        return 0

    lax.fori_loop(1, 9, ring, 0)


def clear_rims(planes, x, g):
    _, e_planes, c_planes = planes
    row = jnp.zeros((10, 16, CH), BF16)
    for side in range(2):
        for p in (0, 9):
            e_planes[side, p // 2, p % 2] = row
            c_planes[side, p // 2, p % 2] = row
        for p in range(1, 9):
            for q in (0, 9):
                c_planes[side, p // 2, p % 2, q] = row[0]

    def clear(n, _):
        for f in (x, g):
            for side in (0, 9):
                f[side, n] = row
                f[n, side] = row
                f[n, :, side] = row
        return 0

    lax.fori_loop(0, 10, clear, 0)


def wide_weights(w, w2, wa, back):
    zero = jnp.zeros((CH, CH), BF16)

    def put(ref, n, c, k, j, tap):
        ref[n, (c * 4 + k) * CH : (c * 4 + k + 1) * CH, j * CH : (j + 1) * CH] = tap

    for c in range(3):
        for k, j in ((0, 1), (3, 0)):
            for n in range(3):
                put(w2, n, c, k, j, zero)
            for n in range(2):
                put(wa, n, c, k, j, zero)
    for a in range(3):
        for e in range(3):
            for c in range(3):
                if back:
                    tap = w[(2 - a) * 9 + (2 - e) * 3 + 2 - c].astype(F32).T.astype(BF16)
                else:
                    tap = w[a * 9 + e * 3 + c]
                for j in range(2):
                    put(w2, e, c, a + j, j, tap)
                    if a != 1:
                        put(wa, a // 2, c, e + j, j, tap)


def inner_conv(x, w2, wa, lin, lo, hi):
    def pair(i, _):
        both = None
        for e in range(3):
            parts = [
                x[2 * i + k, e : e + 8, c : c + 8].reshape(1024, CH)
                for c in range(3)
                for k in (1, 2)
            ]
            taps = jnp.concatenate(
                [w2[e, (c * 4 + 1) * CH : (c * 4 + 3) * CH] for c in range(3)], axis=0
            )
            term = jnp.dot(jnp.concatenate(parts, axis=1), taps, preferred_element_type=F32)
            both = term if both is None else both + term
        for j in range(2):
            plane = x[2 * i + 3 * j].reshape(5, 2, 10, 16, CH)
            parts = [
                plane[k // 2 : k // 2 + 4, k % 2, c : c + 8].reshape(512, CH)
                for c in range(3)
                for k in range(4)
            ]
            one = jnp.dot(jnp.concatenate(parts, axis=1), wa[j], preferred_element_type=F32)
            for e in range(8):
                at = pl.multiple_of(((2 * i + j) * 8 + e) * LINE, 8)
                lin[pl.ds(at, 128)] = (
                    both[e * 128 : e * 128 + 128, j * CH : (j + 1) * CH]
                    + one[e // 2 * 128 : e // 2 * 128 + 128, e % 2 * CH : (e % 2 + 1) * CH]
                )
        return 0

    lax.fori_loop(lo, hi, pair, 0)


def rim_conv(planes, w2, wa, lin):
    a_planes, e_planes, c_planes = planes

    def windows(ref, side):
        parts = [
            ref[side, k // 2 : k // 2 + 4, k % 2, s : s + 8].reshape(512, CH)
            for s in range(3)
            for k in range(4)
        ]
        return jnp.concatenate(parts, axis=1)

    for side in range(2):
        near = 7 * side
        result = jnp.dot(windows(a_planes, side), wa[side], preferred_element_type=F32)
        for i in range(4):
            for j in range(2):
                at = (near * 8 + 2 * i + j) * LINE
                lin[at : at + 128] += result[i * 128 : i * 128 + 128, j * CH : (j + 1) * CH]
        result = jnp.dot(windows(e_planes, side), w2[2 * side], preferred_element_type=F32)
        for i in range(4):
            for j in range(2):
                at = ((2 * i + j) * 8 + near) * LINE
                lin[at : at + 128] += result[i * 128 : i * 128 + 128, j * CH : (j + 1) * CH]
        taps = jnp.concatenate(
            [w2[e, 2 * side * 4 * CH : (2 * side + 1) * 4 * CH] for e in range(3)], axis=0
        )
        result = jnp.dot(windows(c_planes, side), taps, preferred_element_type=F32)
        for i in range(4):
            for j in range(2):
                for e in range(8):
                    at = ((2 * i + j) * 8 + e) * LINE + near * 16
                    row = (i * 8 + e) * 16
                    lin[at : at + 16] += result[row : row + 16, j * CH : (j + 1) * CH]


def inside(i, j):
    return (i >= 0) & (i < lax.axis_size("gx")) & (j >= 0) & (j < lax.axis_size("gy"))


def greet_neighbours(barrier):
    i, j = lax.axis_index("gx"), lax.axis_index("gy")
    count = jnp.int32(0)
    for dx, dy in DIRECTIONS:
        there = inside(i + dx, j + dy)
        count += there.astype(jnp.int32)

        @pl.when(there)
        def _():
            pl.semaphore_signal(
                barrier, inc=1, device_id=(i + dx, j + dy), device_id_type=MESH
            )

    return count


def pack_lists(lists, faces, sending):
    for k in range(8):
        for r in range(4):
            sending[k, r] = faces[jnp.minimum(lists[r, k], 15)]


SENDINGS = ((0, 2), (2, 1), (3, 1))


def halo_copy(k, m, sending, received, send_sem, recv_sem):
    i, j = lax.axis_index("gx"), lax.axis_index("gy")
    dx, dy = DIRECTIONS[k]
    slots = pl.ds(*SENDINGS[m])
    return pltpu.make_async_remote_copy(
        src_ref=sending.at[k, slots],
        dst_ref=received.at[k, slots],
        send_sem=send_sem.at[m, k],
        recv_sem=recv_sem.at[m, k],
        device_id=(i + dx, j + dy),
        device_id_type=MESH,
    )


ORDER = (0, 2, 5, 7, 3, 4, 1, 6)


def start_halo(parts, *halo):
    i, j = lax.axis_index("gx"), lax.axis_index("gy")
    for k in ORDER:
        dx, dy = DIRECTIONS[k]

        @pl.when(inside(i + dx, j + dy))
        def _():
            for m in parts:
                halo_copy(k, m, *halo).start()


def wait_halo(*halo):
    i, j = lax.axis_index("gx"), lax.axis_index("gy")
    for k in ORDER:
        dx, dy = DIRECTIONS[k]

        @pl.when(inside(i - dx, j - dy))
        def _():
            for m in range(3):
                halo_copy(k, m, *halo).wait_recv()


def wait_halo_sent(*halo):
    i, j = lax.axis_index("gx"), lax.axis_index("gy")
    for k in ORDER:
        dx, dy = DIRECTIONS[k]

        @pl.when(inside(i + dx, j + dy))
        def _():
            for m in range(3):
                halo_copy(k, m, *halo).wait_send()


BLOCKS = 28
ROWS = BLOCKS * CH


def place():
    i = lax.axis_index("gx")
    return i // 2, i % 2, lax.axis_index("gy")


def sibling_copy(src, dst, sems, n):
    z, core, j = place()
    return pltpu.make_async_remote_copy(
        src_ref=src, dst_ref=dst, send_sem=sems.at[0, n], recv_sem=sems.at[1, n],
        device_id=(2 * z + 1 - core, j), device_id_type=MESH,
    )


def in_plane(n):
    z, core, j = place()
    return 2 * (n // 4) + core, (n % 4) * 4 + j % 4


def plane_copy(src, dst, sems, d):
    z, core, j = place()
    return pltpu.make_async_remote_copy(
        src_ref=src, dst_ref=dst, send_sem=sems.at[0, d], recv_sem=sems.at[1, d],
        device_id=in_plane((z * 4 + j // 4 + d) % 16), device_id_type=MESH,
    )


def in_column(d):
    z, core, j = place()
    return 2 * z + core, j // 4 * 4 + (j + d) % 4


def column_copy(src, dst, sems, d):
    return pltpu.make_async_remote_copy(
        src_ref=src, dst_ref=dst, send_sem=sems.at[0, d], recv_sem=sems.at[1, d],
        device_id=in_column(d), device_id_type=MESH,
    )


def greet_summers(barrier):
    z, core, j = place()

    def greet(where):
        pl.semaphore_signal(barrier, inc=1, device_id=where, device_id_type=MESH)

    greet((2 * z + 1 - core, j))
    for d in range(1, 16):
        greet(in_plane((z * 4 + j // 4 + d) % 16))
    for d in range(1, 4):
        greet(in_column(d))
    return 19


def settle(lin):
    def line(ae, _):
        at = pl.multiple_of(ae * LINE, 8)
        block = lin[pl.ds(at, 128)]
        for c in range(1, 8):
            lin[pl.ds(at + c * 17, 16)] = block[c * 16 : c * 16 + 16]
        return 0

    lax.fori_loop(0, 64, line, 0)


def weight_terms(x, gt, d32):
    def block(e, c, a):
        at = (e * 9 + c * 3 + a) * CH
        return slice(at, at + CH)

    for j in range(2):
        pairs = jnp.concatenate(
            [
                jnp.concatenate(
                    [
                        gt[i, j * CH : (j + 1) * CH, (2 * m + n) * CH : (2 * m + n + 1) * CH]
                        for i in range(4)
                        for m in range(4)
                    ],
                    axis=1,
                )
                for n in range(2)
            ],
            axis=0,
        )
        for c in range(3):
            parts = [
                jnp.concatenate(
                    [
                        x[2 * i + 3 * j]
                        .reshape(5, 2, 10, 16, CH)[k // 2 : k // 2 + 4, k % 2, c : c + 8]
                        .reshape(512, CH)
                        for i in range(4)
                    ],
                    axis=0,
                )
                for k in range(4)
            ]
            terms = jnp.dot(pairs, jnp.concatenate(parts, axis=1), preferred_element_type=F32)
            for e in range(3):
                term = (
                    terms[:CH, e * CH : (e + 1) * CH]
                    + terms[CH:, (e + 1) * CH : (e + 2) * CH]
                )
                d32[block(e, c, 2 * j)] = term.T
    slopes = jnp.concatenate([gt[i] for i in range(4)], axis=1)
    for e in range(3):
        for c in range(3):
            parts = [
                jnp.concatenate(
                    [x[2 * i + k, e : e + 8, c : c + 8].reshape(1024, CH) for i in range(4)],
                    axis=0,
                )
                for k in (1, 2)
            ]
            terms = jnp.dot(
                slopes, jnp.concatenate(parts, axis=1), preferred_element_type=F32
            )
            d32[block(e, c, 0)] += terms[CH:, :CH].T
            d32[block(e, c, 1)] = (terms[:CH, :CH] + terms[CH:, CH:]).T
            d32[block(e, c, 2)] += terms[:CH, CH:].T


class Summed:
    def __init__(self, d32, first, refs):
        self.d32, self.first = d32, first
        (
            self.d16, self.from_sibling, self.h32, self.h16, self.from_plane, self.column,
            self.share, self.gathered, self.whole, self.sib, self.out, self.col, self.back,
        ) = refs
        self.half = self.d16.shape[0]
        self.rows = self.share.shape[0]
        z, self.core, j = place()
        self.n, self.y = z * 4 + j // 4, j % 4

    def first_pair(self):
        return sibling_copy(self.d16, self.from_sibling, self.sib, 0)

    def outward(self, d):
        there = (self.n + d) % 16
        return plane_copy(self.h16.at[there], self.from_plane.at[d - 1], self.out, d)

    def upward(self, d):
        return column_copy(self.column.at[self.y], self.column.at[self.y], self.col, d)

    def inward(self, d):
        return plane_copy(self.share, self.gathered.at[self.n], self.back, d)

    def last_pair(self):
        return sibling_copy(self.gathered, self.whole.at[self.core], self.sib, 1)

    def start_pair(self):
        other = pl.ds(rows16(self.first + (1 - self.core) * self.half), self.half)
        self.d16[...] = self.d32[other].astype(BF16)
        self.first_pair().start()

    def start_plane(self):
        self.first_pair().wait()
        mine = pl.ds(rows16(self.first + self.core * self.half), self.half)
        self.h32[...] = self.d32[mine] + self.from_sibling[...].astype(F32)
        self.h16[...] = self.h32[...].astype(BF16).reshape(self.h16.shape)
        for d in range(1, 16):
            self.outward(d).start()

    def start_column(self):
        for d in range(1, 16):
            self.outward(d).wait()
        part = self.h32[pl.ds(rows16(self.n * self.rows), self.rows)]
        for d in range(1, 16):
            part = part + self.from_plane[d - 1].astype(F32)
        self.column[self.y] = part.astype(BF16)
        for d in range(1, 4):
            self.upward(d).start()

    def start_back(self):
        for d in range(1, 4):
            self.upward(d).wait()
        part = self.column[0].astype(F32)
        for m in range(1, 4):
            part = part + self.column[m].astype(F32)
        voxels = lax.axis_size("gx") * lax.axis_size("gy") * 8192
        self.share[...] = (part * (1.0 / math.sqrt(voxels))).astype(BF16)
        self.gathered[self.n] = self.share[...]
        for d in range(1, 16):
            self.inward(d).start()

    def start_last(self):
        for d in range(1, 16):
            self.inward(d).wait()
        self.last_pair().start()
        self.whole[self.core] = self.gathered[...]

    def finish(self):
        self.last_pair().wait()


def sum_scratch(blocks):
    half = blocks * CH // 2
    rows = half // 16
    return [
        pltpu.VMEM((half, CH), BF16),
        pltpu.VMEM((half, CH), BF16),
        pltpu.VMEM((half, CH), F32),
        pltpu.VMEM((16, rows, CH), BF16),
        pltpu.VMEM((15, rows, CH), BF16),
        pltpu.VMEM((4, rows, CH), BF16),
        pltpu.VMEM((rows, CH), BF16),
        pltpu.VMEM((16, rows, CH), BF16),
        pltpu.VMEM((2, 16, rows, CH), BF16),
        pltpu.SemaphoreType.DMA((2, 2)),
        pltpu.SemaphoreType.DMA((2, 16)),
        pltpu.SemaphoreType.DMA((2, 4)),
        pltpu.SemaphoreType.DMA((2, 16)),
    ]


def credit_neighbours(credit):
    i, j = lax.axis_index("gx"), lax.axis_index("gy")
    for dx, dy in DIRECTIONS:

        @pl.when(inside(i - dx, j - dy))
        def _():
            pl.semaphore_signal(
                credit, inc=1, device_id=(i - dx, j - dy), device_id_type=MESH
            )


def kernel(
    vol, cot, w, bias, lists, kmap, act, grad, total,
    nat, lin, x32, t32, wide, ct, faces, sending, received, x, g,
    a_planes, e_planes, c_planes, w2, wa, gt, d32, send_sem, recv_sem, own_sems, credit, *sums,
):
    halo = (sending, received, send_sem, recv_sem)
    planes = (a_planes, e_planes, c_planes)
    terms_sum = Summed(d32, 0, sums)
    take_vol = pltpu.make_async_copy(vol, nat, own_sems.at[0])
    take_cot = pltpu.make_async_copy(cot, nat, own_sems.at[1])
    give_act = pltpu.make_async_copy(nat, act, own_sems.at[2])
    give_grad = pltpu.make_async_copy(nat, grad, own_sems.at[3])
    give_total = pltpu.make_async_copy(terms_sum.whole, total, own_sems.at[4])
    take_vol.start()
    barrier = pltpu.get_barrier_semaphore()
    neighbours = greet_neighbours(barrier)
    summers = greet_summers(barrier)

    take_vol.wait()
    natural_to_bricks(nat, x32)
    take_cot.start()
    own_table(x32, t32, faces)
    pack_lists(lists, faces, sending)
    pl.semaphore_wait(barrier, neighbours + summers)
    start_halo((0, 1, 2), *halo)

    def put_x(a, e, c, v):
        x[1 + a, 1 + e, 1 + c] = v

    each_inner(x32, put_x)

    def put_cot(a, e, c, v):
        ct[pl.ds(rows16((a * 64 + e * 8 + c) * 16), 16)] = v

    take_cot.wait()
    natural_to_bricks(nat, x32)
    each_inner(x32, put_cot)
    wide_weights(w, w2, wa, False)
    clear_rims(planes, x, g)
    inner_conv(x, w2, wa, lin, 0, 4)
    wait_halo(*halo)
    received_table(received, t32, wide)
    credit_neighbours(credit)
    rim(kmap, t32, x32, planes, x)
    rim_conv(planes, w2, wa, lin)

    def finish(ae, _):
        a, e = ae // 8, ae % 8
        line = pl.multiple_of(ae * LINE, 8)
        linear = lin[pl.ds(line, 128)] + bias[...]
        s = 1.0 / (1.0 + jnp.exp(-linear))
        activated = linear * s
        slope = ct[pl.ds(rows16(ae * 128), 128)].astype(F32) * s * (1.0 + linear * (1.0 - s))
        lin[pl.ds(line, 128)] = activated
        for c in range(8):
            at = (1 + a) * SP + (1 + e) * SQ + (1 + c) * SR
            x32[pl.ds(at, 16)] = slope[c * 16 : c * 16 + 16]
        g[1 + a, 1 + e, 1:9] = slope.astype(BF16).reshape(8, 16, CH)
        return 0

    lax.fori_loop(0, 64, finish, 0)
    wait_halo_sent(*halo)
    own_table(x32, t32, faces)
    pack_lists(lists, faces, sending)
    pl.semaphore_wait(credit, neighbours)
    start_halo((0,), *halo)

    def turn(p, sums):
        for m in range(8):
            block = g[1 + p, 1 + m, 1:9].astype(F32).reshape(128, CH)
            gt[p // 2, pl.ds(rows16((p % 2) * CH), CH), m * 128 : m * 128 + 128] = (
                block.T.astype(BF16)
            )
            sums = sums + block
        return sums

    totals = lax.fori_loop(0, 8, turn, jnp.zeros((128, CH), F32))
    d32[27 * CH :] = jnp.concatenate(
        [jnp.sum(totals, axis=0, keepdims=True), jnp.zeros((127, CH), F32)], axis=0
    )

    weight_terms(x, gt, d32)
    terms_sum.start_pair()
    settle(lin)
    bricks_to_natural(lin, nat)
    give_act.start()
    wide_weights(w, w2, wa, True)
    terms_sum.start_plane()
    start_halo((1,), *halo)
    inner_conv(g, w2, wa, lin, 0, 3)
    terms_sum.start_column()
    start_halo((2,), *halo)
    inner_conv(g, w2, wa, lin, 3, 4)
    terms_sum.start_back()
    wait_halo(*halo)
    received_table(received, t32, wide)
    rim(kmap, t32, x32, planes, None)
    rim_conv(planes, w2, wa, lin)
    terms_sum.start_last()
    settle(lin)
    give_act.wait()
    bricks_to_natural(lin, nat)
    give_grad.start()
    terms_sum.finish()
    give_total.start()
    wait_halo_sent(*halo)
    give_total.wait()
    give_grad.wait()


def layer(vol, cot, w, bias, lists, kmap):
    vm = pl.BlockSpec(memory_space=pltpu.VMEM)
    sm = pl.BlockSpec(memory_space=pltpu.SMEM)
    hbm = pl.BlockSpec(memory_space=pl.ANY)
    field = pltpu.VMEM((10, 10, 10, 16, CH), BF16)
    planes = pltpu.VMEM((2, 5, 2, 10, 16, CH), BF16)
    return pl.pallas_call(
        kernel,
        out_shape=(
            jax.ShapeDtypeStruct((16, 512, CH), BF16),
            jax.ShapeDtypeStruct((16, 512, CH), BF16),
            jax.ShapeDtypeStruct((2, 16, BLOCKS * 4, CH), BF16),
        ),
        in_specs=[hbm, hbm, vm, vm, sm, sm],
        out_specs=(hbm, hbm, hbm),
        scratch_shapes=[
            pltpu.VMEM((16, 512, CH), BF16),
            pltpu.VMEM((64 * LINE, CH), F32),
            pltpu.VMEM((10 * SP + 2, CH), F32),
            pltpu.VMEM((49 * ENTRY, 8, CH), F32),
            pltpu.VMEM((256, CH), F32),
            pltpu.VMEM((8192, CH), BF16),
            pltpu.VMEM((16, SENT, CH), BF16),
            pltpu.VMEM((8, 4, SENT, CH), BF16),
            pltpu.VMEM((8, 4, SENT, CH), BF16),
            field,
            field,
            planes,
            planes,
            planes,
            pltpu.VMEM((3, 12 * CH, 2 * CH), BF16),
            pltpu.VMEM((2, 12 * CH, 2 * CH), BF16),
            pltpu.VMEM((4, 2 * CH, 1024), BF16),
            pltpu.VMEM((ROWS, CH), F32),
            pltpu.SemaphoreType.DMA((3, 8)),
            pltpu.SemaphoreType.DMA((3, 8)),
            pltpu.SemaphoreType.DMA((5,)),
            pltpu.SemaphoreType.REGULAR,
            *sum_scratch(BLOCKS),
        ],
        compiler_params=pltpu.CompilerParams(
            collective_id=0, has_side_effects=True, vmem_limit_bytes=63 * 2**20
        ),
        name="layer",
    )(vol, cot, w, bias, lists, kmap)


PIECES = 4


def deliver_kernel(
    act, grad, total, act_out, grad_out, weight_out, bias_out, held, terms, weights, sems, more
):
    def piece(n, m, src, dst):
        at = pl.ds(m * 16 // PIECES, 16 // PIECES)
        return (
            pltpu.make_async_copy(src.at[at], held.at[n, at], sems.at[0, n, m]),
            pltpu.make_async_copy(held.at[n, at], dst.at[at], sems.at[1, n, m]),
        )

    take_terms = pltpu.make_async_copy(total, terms, more.at[0])
    give_weights = pltpu.make_async_copy(weights, weight_out, more.at[1])
    pieces = [
        piece(n, m, src, dst)
        for n, (src, dst) in enumerate(((act, act_out), (grad, grad_out)))
        for m in range(PIECES)
    ]
    take_terms.start()
    for take, _ in pieces:
        take.start()
    take_terms.wait()
    for n in range(27):
        weights[n % 3 * 9 + n // 3] = terms[n * CH : (n + 1) * CH].astype(F32)
    bias_out[...] = terms[27 * CH : 27 * CH + 16].astype(F32)[0:1]
    give_weights.start()
    for take, give in pieces:
        take.wait()
        give.start()
    for _, give in pieces:
        give.wait()
    give_weights.wait()


def deliver(act, grad, total):
    vm = pl.BlockSpec(memory_space=pltpu.VMEM)
    hbm = pl.BlockSpec(memory_space=pl.ANY)
    return pl.pallas_call(
        deliver_kernel,
        out_shape=(
            jax.ShapeDtypeStruct(act.shape, BF16),
            jax.ShapeDtypeStruct(grad.shape, BF16),
            jax.ShapeDtypeStruct((27, CH, CH), F32),
            jax.ShapeDtypeStruct((1, CH), F32),
        ),
        in_specs=[hbm, hbm, hbm],
        out_specs=(hbm, hbm, hbm, vm),
        scratch_shapes=[
            pltpu.VMEM((2, 16, 512, CH), BF16),
            pltpu.VMEM((ROWS, CH), BF16),
            pltpu.VMEM((27, CH, CH), F32),
            pltpu.SemaphoreType.DMA((2, 2, PIECES)),
            pltpu.SemaphoreType.DMA((2,)),
        ],
        compiler_params=pltpu.CompilerParams(vmem_limit_bytes=63 * 2**20),
        name="deliver",
    )(act, grad, total)


def shards(features, cotangent, kernel_weight, conv_bias, send_lists, kernel_map):
    act, grad, total = layer(
        features.reshape(16, 512, CH),
        cotangent.reshape(16, 512, CH),
        kernel_weight.reshape(27, CH, CH),
        conv_bias.reshape(1, CH),
        send_lists[0, 0].T,
        kernel_map[0, 0],
    )
    act, grad, weight_total, bias_total = deliver(act, grad, total.reshape(ROWS, CH))
    return (
        act.reshape(features.shape),
        grad.reshape(features.shape),
        weight_total.reshape(kernel_weight.shape),
        bias_total.reshape(CH),
    )


def solution(mesh):
    block = P("gx", "gy", None, None, None, None, None)
    return jax.shard_map(
        shards,
        mesh=mesh,
        in_specs=(block, block, P(), P(), P("gx", "gy", None, None), P("gx", "gy", None, None)),
        out_specs=(block, block, P(), P()),
        check_vma=False,
    )
```

```python
import functools
import math

import jax
import jax.numpy as jnp
from jax import lax
from jax.experimental import pallas as pl
from jax.experimental.pallas import tpu as pltpu
from jax.sharding import PartitionSpec as P

MESH = pl.DeviceIdType.MESH
F32, BF16 = jnp.float32, jnp.bfloat16
DIRECTIONS = ((-1, -1), (-1, 0), (-1, 1), (0, -1), (0, 1), (1, -1), (1, 0), (1, 1))
CH = 128
ENTRY = 52
SENT = 320
A_LOW, A_HIGH, E_LOW, E_HIGH, C_LOW, C_HIGH, EDGES = 0, 8, 16, 24, 32, 40, 48
SP, SQ, SR = 1711, 171, 17
LINE = 136


def rows16(start):
    return pl.multiple_of(start, 16)


def natural_to_bricks(nat, x32):
    def stage(b, _):
        block = nat[b].astype(F32)
        for ae in range(64):
            at = (1 + ae // 8) * SP + (1 + ae % 8) * SQ + SR
            x32[pl.ds(at + b, 8, stride=SR)] = block[ae * 8 : ae * 8 + 8]
        return 0

    lax.fori_loop(0, 16, stage, 0)


def each_inner(x32, put):
    def plane(a, _):
        for e in range(8):
            for c in range(8):
                at = (1 + a) * SP + (1 + e) * SQ + (1 + c) * SR
                put(a, e, c, x32[pl.ds(at, 16)].astype(BF16))
        return 0

    lax.fori_loop(0, 8, plane, 0)


def bricks_to_natural(lin, nat):
    def unstage(b, _):
        for ae in range(0, 64, 2):
            pair = [lin[pl.ds((ae + k) * LINE + b, 8, stride=17)] for k in range(2)]
            nat[b, ae * 8 : ae * 8 + 16] = jnp.concatenate(pair, axis=0).astype(BF16)
        return 0

    lax.fori_loop(0, 16, unstage, 0)


def own_table(x32, t32, faces):
    def one(b, _):
        base = b * ENTRY
        for low, p in ((A_LOW, 1), (A_HIGH, 8)):
            for e in range(8):
                t32[base + low + e] = x32[pl.ds(p * SP + (1 + e) * SQ + SR + b, 8, stride=SR)]
        for low, q in ((E_LOW, 1), (E_HIGH, 8)):
            for a in range(8):
                t32[base + low + a] = x32[pl.ds((1 + a) * SP + q * SQ + SR + b, 8, stride=SR)]
        for low, r in ((C_LOW, 1), (C_HIGH, 8)):
            for a in range(8):
                t32[base + low + a] = x32[pl.ds((1 + a) * SP + SQ + r * SR + b, 8, stride=SQ)]
        for n, (q, r) in enumerate(((1, 1), (1, 8), (8, 1), (8, 8))):
            t32[base + EDGES + n] = x32[pl.ds(SP + q * SQ + r * SR + b, 8, stride=SP)]
        faces[b, 0:128] = t32[pl.ds(base, 16)].reshape(128, CH).astype(BF16)
        for n, low in enumerate((E_LOW, E_HIGH, C_LOW, C_HIGH)):
            lines = t32[pl.ds(base + low + 1, 6)].reshape(48, CH)
            faces[b, 128 + 48 * n : 176 + 48 * n] = lines.astype(BF16)
        return 0

    lax.fori_loop(0, 16, one, 0)


def received_table(k, received, t32, wide):
    def one(r, _):
        n = 4 * k + r
        base = (16 + n) * ENTRY
        sides = received[k, r, 0:128].astype(F32)
        wide[0:128] = sides
        t32[pl.ds(base, 16)] = sides.reshape(16, 8, CH)
        for m, low in enumerate((E_LOW, E_HIGH, C_LOW, C_HIGH)):
            lines = received[k, r, 128 + 48 * m : 176 + 48 * m].astype(F32)
            t32[pl.ds(base + low + 1, 6)] = lines.reshape(6, 8, CH)
            if m < 2:
                wide[136 + 64 * m : 184 + 64 * m] = lines
        for a, side in ((0, 0), (7, 64)):
            low, high = wide[side : side + 8], wide[side + 56 : side + 64]
            t32[base + E_LOW + a] = low
            t32[base + E_HIGH + a] = high
            wide[128 + 8 * a : 136 + 8 * a] = low
            wide[192 + 8 * a : 200 + 8 * a] = high
            t32[base + C_LOW + a] = wide[pl.ds(side, 8, stride=8)]
            t32[base + C_HIGH + a] = wide[pl.ds(side + 7, 8, stride=8)]
        for m, start in enumerate((128, 135, 192, 199)):
            t32[base + EDGES + m] = wide[pl.ds(start, 8, stride=8)]
        return 0

    lax.fori_loop(0, 4, one, 0)


def rim(kmap, t32, x32, planes, x):
    a_planes, e_planes, c_planes = planes

    def one(b, _):
        for o in range(27):
            a, e, c = o // 9 - 1, o // 3 % 3 - 1, o % 3 - 1
            if a == e == c == 0:
                continue
            base = kmap[b, o] * ENTRY
            p, q, r = [1 + 8 * (s > 0) - (s < 0) for s in (a, e, c)]
            dest = p * SP + q * SQ + r * SR + b
            fe, fc = 7 * (e < 0), 7 * (c < 0)
            if a != 0:
                side = base + (A_HIGH if a < 0 else A_LOW)
                if e == 0 and c == 0:
                    for n in range(8):
                        x32[pl.ds(dest + n * SQ, 8, stride=SR)] = t32[side + n]
                elif c == 0:
                    x32[pl.ds(dest, 8, stride=SR)] = t32[side + fe]
                elif e == 0:
                    line = base + (C_HIGH if c < 0 else C_LOW) + 7 * (a < 0)
                    x32[pl.ds(dest, 8, stride=SQ)] = t32[line]
                else:
                    x32[pl.ds(dest, 1)] = t32[side + fe][fc : fc + 1]
            elif e != 0:
                side = base + (E_HIGH if e < 0 else E_LOW)
                if c == 0:
                    for n in range(8):
                        x32[pl.ds(dest + n * SP, 8, stride=SR)] = t32[side + n]
                else:
                    x32[pl.ds(dest, 8, stride=SP)] = t32[base + EDGES + 2 * (e < 0) + (c < 0)]
            else:
                side = base + (C_HIGH if c < 0 else C_LOW)
                for n in range(8):
                    x32[pl.ds(dest + n * SP, 8, stride=SQ)] = t32[side + n]
        return 0

    lax.fori_loop(0, 16, one, 0)

    def pack(p, q, r):
        cell = x32[pl.ds(p * SP + q * SQ + r * SR, 16)].astype(BF16)
        if x is not None:
            x[p, q, r] = cell
        return cell

    def line(q, _):
        for side in range(2):
            for r in range(10):
                a_planes[side, q // 2, q % 2, r] = pack(9 * side, q, r)
        return 0

    lax.fori_loop(0, 10, line, 0)

    def ring(p, _):
        for side in range(2):
            for r in range(10):
                e_planes[side, p // 2, p % 2, r] = pack(p, 9 * side, r)
            for q in range(1, 9):
                c_planes[side, p // 2, p % 2, q] = pack(p, q, 9 * side)
        return 0

    lax.fori_loop(1, 9, ring, 0)


def clear_rims(planes, x, g):
    _, e_planes, c_planes = planes
    row = jnp.zeros((10, 16, CH), BF16)
    for side in range(2):
        for p in (0, 9):
            e_planes[side, p // 2, p % 2] = row
            c_planes[side, p // 2, p % 2] = row
        for p in range(1, 9):
            for q in (0, 9):
                c_planes[side, p // 2, p % 2, q] = row[0]

    def clear(n, _):
        for f in (x, g):
            for side in (0, 9):
                f[side, n] = row
                f[n, side] = row
                f[n, :, side] = row
        return 0

    lax.fori_loop(0, 10, clear, 0)


def wide_weights(w, w2, wa, back):
    zero = jnp.zeros((CH, CH), BF16)

    def put(ref, n, c, k, j, tap):
        ref[n, (c * 4 + k) * CH : (c * 4 + k + 1) * CH, j * CH : (j + 1) * CH] = tap

    for c in range(3):
        for k, j in ((0, 1), (3, 0)):
            for n in range(3):
                put(w2, n, c, k, j, zero)
            for n in range(2):
                put(wa, n, c, k, j, zero)
    for a in range(3):
        for e in range(3):
            for c in range(3):
                if back:
                    tap = w[(2 - a) * 9 + (2 - e) * 3 + 2 - c].astype(F32).T.astype(BF16)
                else:
                    tap = w[a * 9 + e * 3 + c]
                for j in range(2):
                    put(w2, e, c, a + j, j, tap)
                    if a != 1:
                        put(wa, a // 2, c, e + j, j, tap)


def inner_conv(x, w2, wa, lin, lo, hi):
    def pair(i, _):
        both = None
        for e in range(3):
            parts = [
                x[2 * i + k, e : e + 8, c : c + 8].reshape(1024, CH)
                for c in range(3)
                for k in (1, 2)
            ]
            taps = jnp.concatenate(
                [w2[e, (c * 4 + 1) * CH : (c * 4 + 3) * CH] for c in range(3)], axis=0
            )
            term = jnp.dot(jnp.concatenate(parts, axis=1), taps, preferred_element_type=F32)
            both = term if both is None else both + term
        for j in range(2):
            plane = x[2 * i + 3 * j].reshape(5, 2, 10, 16, CH)
            parts = [
                plane[k // 2 : k // 2 + 4, k % 2, c : c + 8].reshape(512, CH)
                for c in range(3)
                for k in range(4)
            ]
            one = jnp.dot(jnp.concatenate(parts, axis=1), wa[j], preferred_element_type=F32)
            for e in range(8):
                at = pl.multiple_of(((2 * i + j) * 8 + e) * LINE, 8)
                lin[pl.ds(at, 128)] = (
                    both[e * 128 : e * 128 + 128, j * CH : (j + 1) * CH]
                    + one[e // 2 * 128 : e // 2 * 128 + 128, e % 2 * CH : (e % 2 + 1) * CH]
                )
        return 0

    lax.fori_loop(lo, hi, pair, 0)


def rim_conv(planes, w2, wa, lin):
    a_planes, e_planes, c_planes = planes

    def windows(ref, side):
        parts = [
            ref[side, k // 2 : k // 2 + 4, k % 2, s : s + 8].reshape(512, CH)
            for s in range(3)
            for k in range(4)
        ]
        return jnp.concatenate(parts, axis=1)

    for side in range(2):
        near = 7 * side
        result = jnp.dot(windows(a_planes, side), wa[side], preferred_element_type=F32)
        for i in range(4):
            for j in range(2):
                at = (near * 8 + 2 * i + j) * LINE
                lin[at : at + 128] += result[i * 128 : i * 128 + 128, j * CH : (j + 1) * CH]
        result = jnp.dot(windows(e_planes, side), w2[2 * side], preferred_element_type=F32)
        for i in range(4):
            for j in range(2):
                at = ((2 * i + j) * 8 + near) * LINE
                lin[at : at + 128] += result[i * 128 : i * 128 + 128, j * CH : (j + 1) * CH]
        taps = jnp.concatenate(
            [w2[e, 2 * side * 4 * CH : (2 * side + 1) * 4 * CH] for e in range(3)], axis=0
        )
        result = jnp.dot(windows(c_planes, side), taps, preferred_element_type=F32)
        for i in range(4):
            for j in range(2):
                for e in range(8):
                    at = ((2 * i + j) * 8 + e) * LINE + near * 16
                    row = (i * 8 + e) * 16
                    lin[at : at + 16] += result[row : row + 16, j * CH : (j + 1) * CH]


def inside(i, j):
    return (i >= 0) & (i < lax.axis_size("gx")) & (j >= 0) & (j < lax.axis_size("gy"))


def greet_neighbours(barrier):
    i, j = lax.axis_index("gx"), lax.axis_index("gy")
    count = jnp.int32(0)
    for dx, dy in DIRECTIONS:
        there = inside(i + dx, j + dy)
        count += there.astype(jnp.int32)

        @pl.when(there)
        def _():
            pl.semaphore_signal(
                barrier, inc=1, device_id=(i + dx, j + dy), device_id_type=MESH
            )

    return count


def pack_lists(lists, faces, sending):
    for k in range(8):
        for r in range(4):
            sending[k, r] = faces[jnp.minimum(lists[r, k], 15)]


def halo_copy(k, sending, received, send_sem, recv_sem):
    i, j = lax.axis_index("gx"), lax.axis_index("gy")
    dx, dy = DIRECTIONS[k]
    return pltpu.make_async_remote_copy(
        src_ref=sending.at[k],
        dst_ref=received.at[k],
        send_sem=send_sem.at[k],
        recv_sem=recv_sem.at[k],
        device_id=(i + dx, j + dy),
        device_id_type=MESH,
    )


ORDER = (0, 2, 5, 7, 3, 4, 1, 6)


def start_halo(*halo):
    i, j = lax.axis_index("gx"), lax.axis_index("gy")
    for k in ORDER:
        dx, dy = DIRECTIONS[k]

        @pl.when(inside(i + dx, j + dy))
        def _():
            halo_copy(k, *halo).start()


def take_halo(t32, wide, *halo):
    i, j = lax.axis_index("gx"), lax.axis_index("gy")
    t32[pl.ds(48 * ENTRY, ENTRY)] = jnp.zeros((ENTRY, 8, CH), F32)
    for k in (1, 6, 0, 2, 5, 7, 3, 4):
        dx, dy = DIRECTIONS[k]

        @pl.when(inside(i - dx, j - dy))
        def _():
            halo_copy(k, *halo).wait_recv()

        received_table(k, halo[1], t32, wide)


def wait_halo_sent(*halo):
    i, j = lax.axis_index("gx"), lax.axis_index("gy")
    for k in ORDER:
        dx, dy = DIRECTIONS[k]

        @pl.when(inside(i + dx, j + dy))
        def _():
            halo_copy(k, *halo).wait_send()


BLOCKS = 28
ROWS = BLOCKS * CH


def place():
    i = lax.axis_index("gx")
    return i // 2, i % 2, lax.axis_index("gy")


def sibling_copy(src, dst, sems, n):
    z, core, j = place()
    return pltpu.make_async_remote_copy(
        src_ref=src, dst_ref=dst, send_sem=sems.at[0, n], recv_sem=sems.at[1, n],
        device_id=(2 * z + 1 - core, j), device_id_type=MESH,
    )


def in_plane(n):
    z, core, j = place()
    return 2 * (n // 4) + core, (n % 4) * 4 + j % 4


def plane_copy(src, dst, sems, d):
    z, core, j = place()
    return pltpu.make_async_remote_copy(
        src_ref=src, dst_ref=dst, send_sem=sems.at[0, d], recv_sem=sems.at[1, d],
        device_id=in_plane((z * 4 + j // 4 + d) % 16), device_id_type=MESH,
    )


def in_column(d):
    z, core, j = place()
    return 2 * z + core, j // 4 * 4 + (j + d) % 4


def column_copy(src, dst, sems, d):
    return pltpu.make_async_remote_copy(
        src_ref=src, dst_ref=dst, send_sem=sems.at[0, d], recv_sem=sems.at[1, d],
        device_id=in_column(d), device_id_type=MESH,
    )


def greet_summers(barrier):
    z, core, j = place()

    def greet(where):
        pl.semaphore_signal(barrier, inc=1, device_id=where, device_id_type=MESH)

    greet((2 * z + 1 - core, j))
    for d in range(1, 16):
        greet(in_plane((z * 4 + j // 4 + d) % 16))
    for d in range(1, 4):
        greet(in_column(d))
    return 19


def settle(lin):
    def line(ae, _):
        at = pl.multiple_of(ae * LINE, 8)
        block = lin[pl.ds(at, 128)]
        for c in range(1, 8):
            lin[pl.ds(at + c * 17, 16)] = block[c * 16 : c * 16 + 16]
        return 0

    lax.fori_loop(0, 64, line, 0)


def weight_terms(x, gt, d32):
    def block(e, c, a):
        at = (e * 9 + c * 3 + a) * CH
        return slice(at, at + CH)

    for j in range(2):
        pairs = jnp.concatenate(
            [
                jnp.concatenate(
                    [
                        gt[i, j * CH : (j + 1) * CH, (2 * m + n) * CH : (2 * m + n + 1) * CH]
                        for i in range(4)
                        for m in range(4)
                    ],
                    axis=1,
                )
                for n in range(2)
            ],
            axis=0,
        )
        for c in range(3):
            parts = [
                jnp.concatenate(
                    [
                        x[2 * i + 3 * j]
                        .reshape(5, 2, 10, 16, CH)[k // 2 : k // 2 + 4, k % 2, c : c + 8]
                        .reshape(512, CH)
                        for i in range(4)
                    ],
                    axis=0,
                )
                for k in range(4)
            ]
            terms = jnp.dot(pairs, jnp.concatenate(parts, axis=1), preferred_element_type=F32)
            for e in range(3):
                term = (
                    terms[:CH, e * CH : (e + 1) * CH]
                    + terms[CH:, (e + 1) * CH : (e + 2) * CH]
                )
                d32[block(e, c, 2 * j)] = term.T
    slopes = jnp.concatenate([gt[i] for i in range(4)], axis=1)
    for e in range(3):
        for c in range(3):
            parts = [
                jnp.concatenate(
                    [x[2 * i + k, e : e + 8, c : c + 8].reshape(1024, CH) for i in range(4)],
                    axis=0,
                )
                for k in (1, 2)
            ]
            terms = jnp.dot(
                slopes, jnp.concatenate(parts, axis=1), preferred_element_type=F32
            )
            d32[block(e, c, 0)] += terms[CH:, :CH].T
            d32[block(e, c, 1)] = (terms[:CH, :CH] + terms[CH:, CH:]).T
            d32[block(e, c, 2)] += terms[:CH, CH:].T


class Summed:
    def __init__(self, d32, first, refs):
        self.d32, self.first = d32, first
        (
            self.d16, self.from_sibling, self.h32, self.h16, self.from_plane, self.column,
            self.share, self.gathered, self.whole, self.sib, self.out, self.col, self.back,
        ) = refs
        self.half = self.d16.shape[0]
        self.rows = self.share.shape[0]
        z, self.core, j = place()
        self.n, self.y = z * 4 + j // 4, j % 4

    def first_pair(self):
        return sibling_copy(self.d16, self.from_sibling, self.sib, 0)

    def outward(self, d):
        there = (self.n + d) % 16
        return plane_copy(self.h16.at[there], self.from_plane.at[d - 1], self.out, d)

    def upward(self, d):
        return column_copy(self.column.at[self.y], self.column.at[self.y], self.col, d)

    def inward(self, d):
        return plane_copy(self.share, self.gathered.at[self.n], self.back, d)

    def last_pair(self):
        return sibling_copy(self.gathered, self.whole.at[self.core], self.sib, 1)

    def start_pair(self):
        other = pl.ds(rows16(self.first + (1 - self.core) * self.half), self.half)
        self.d16[...] = self.d32[other].astype(BF16)
        self.first_pair().start()

    def start_plane(self):
        self.first_pair().wait()
        mine = pl.ds(rows16(self.first + self.core * self.half), self.half)
        self.h32[...] = self.d32[mine] + self.from_sibling[...].astype(F32)
        self.h16[...] = self.h32[...].astype(BF16).reshape(self.h16.shape)
        for d in range(1, 16):
            self.outward(d).start()

    def start_column(self):
        for d in range(1, 16):
            self.outward(d).wait()
        part = self.h32[pl.ds(rows16(self.n * self.rows), self.rows)]
        for d in range(1, 16):
            part = part + self.from_plane[d - 1].astype(F32)
        self.column[self.y] = part.astype(BF16)
        for d in range(1, 4):
            self.upward(d).start()

    def start_back(self):
        for d in range(1, 4):
            self.upward(d).wait()
        part = self.column[0].astype(F32)
        for m in range(1, 4):
            part = part + self.column[m].astype(F32)
        voxels = lax.axis_size("gx") * lax.axis_size("gy") * 8192
        self.share[...] = (part * (1.0 / math.sqrt(voxels))).astype(BF16)
        self.gathered[self.n] = self.share[...]
        for d in range(1, 16):
            self.inward(d).start()

    def start_last(self):
        for d in range(1, 16):
            self.inward(d).wait()
        self.last_pair().start()
        self.whole[self.core] = self.gathered[...]

    def finish(self):
        self.last_pair().wait()


def sum_scratch(blocks):
    half = blocks * CH // 2
    rows = half // 16
    return [
        pltpu.VMEM((half, CH), BF16),
        pltpu.VMEM((half, CH), BF16),
        pltpu.VMEM((half, CH), F32),
        pltpu.VMEM((16, rows, CH), BF16),
        pltpu.VMEM((15, rows, CH), BF16),
        pltpu.VMEM((4, rows, CH), BF16),
        pltpu.VMEM((rows, CH), BF16),
        pltpu.VMEM((16, rows, CH), BF16),
        pltpu.VMEM((2, 16, rows, CH), BF16),
        pltpu.SemaphoreType.DMA((2, 2)),
        pltpu.SemaphoreType.DMA((2, 16)),
        pltpu.SemaphoreType.DMA((2, 4)),
        pltpu.SemaphoreType.DMA((2, 16)),
    ]


def credit_neighbours(credit):
    i, j = lax.axis_index("gx"), lax.axis_index("gy")
    for dx, dy in DIRECTIONS:

        @pl.when(inside(i - dx, j - dy))
        def _():
            pl.semaphore_signal(
                credit, inc=1, device_id=(i - dx, j - dy), device_id_type=MESH
            )


def kernel(
    vol, cot, w, bias, lists, kmap, act, grad, total,
    nat, lin, x32, t32, wide, ct, faces, sending, received, x, g,
    a_planes, e_planes, c_planes, w2, wa, gt, d32, send_sem, recv_sem, own_sems, credit, *sums,
):
    halo = (sending, received, send_sem, recv_sem)
    planes = (a_planes, e_planes, c_planes)
    terms_sum = Summed(d32, 0, sums)
    take_vol = pltpu.make_async_copy(vol, nat, own_sems.at[0])
    take_cot = pltpu.make_async_copy(cot, nat, own_sems.at[1])
    give_act = pltpu.make_async_copy(nat, act, own_sems.at[2])
    give_grad = pltpu.make_async_copy(nat, grad, own_sems.at[3])
    give_total = pltpu.make_async_copy(terms_sum.whole, total, own_sems.at[4])
    take_vol.start()
    barrier = pltpu.get_barrier_semaphore()
    neighbours = greet_neighbours(barrier)
    summers = greet_summers(barrier)

    take_vol.wait()
    natural_to_bricks(nat, x32)
    take_cot.start()
    own_table(x32, t32, faces)
    pack_lists(lists, faces, sending)
    pl.semaphore_wait(barrier, neighbours + summers)
    start_halo(*halo)

    def put_x(a, e, c, v):
        x[1 + a, 1 + e, 1 + c] = v

    each_inner(x32, put_x)

    def put_cot(a, e, c, v):
        ct[pl.ds(rows16((a * 64 + e * 8 + c) * 16), 16)] = v

    take_cot.wait()
    natural_to_bricks(nat, x32)
    each_inner(x32, put_cot)
    wide_weights(w, w2, wa, False)
    clear_rims(planes, x, g)
    inner_conv(x, w2, wa, lin, 0, 4)
    take_halo(t32, wide, *halo)
    credit_neighbours(credit)
    rim(kmap, t32, x32, planes, x)
    rim_conv(planes, w2, wa, lin)

    def finish(ae, _):
        a, e = ae // 8, ae % 8
        line = pl.multiple_of(ae * LINE, 8)
        linear = lin[pl.ds(line, 128)] + bias[...]
        s = 1.0 / (1.0 + jnp.exp(-linear))
        activated = linear * s
        slope = ct[pl.ds(rows16(ae * 128), 128)].astype(F32) * s * (1.0 + linear * (1.0 - s))
        lin[pl.ds(line, 128)] = activated
        for c in range(8):
            at = (1 + a) * SP + (1 + e) * SQ + (1 + c) * SR
            x32[pl.ds(at, 16)] = slope[c * 16 : c * 16 + 16]
        g[1 + a, 1 + e, 1:9] = slope.astype(BF16).reshape(8, 16, CH)
        return 0

    lax.fori_loop(0, 64, finish, 0)
    wait_halo_sent(*halo)
    own_table(x32, t32, faces)
    pack_lists(lists, faces, sending)
    pl.semaphore_wait(credit, neighbours)
    start_halo(*halo)

    def turn(p, sums):
        for m in range(8):
            block = g[1 + p, 1 + m, 1:9].astype(F32).reshape(128, CH)
            gt[p // 2, pl.ds(rows16((p % 2) * CH), CH), m * 128 : m * 128 + 128] = (
                block.T.astype(BF16)
            )
            sums = sums + block
        return sums

    totals = lax.fori_loop(0, 8, turn, jnp.zeros((128, CH), F32))
    d32[27 * CH :] = jnp.concatenate(
        [jnp.sum(totals, axis=0, keepdims=True), jnp.zeros((127, CH), F32)], axis=0
    )

    weight_terms(x, gt, d32)
    terms_sum.start_pair()
    settle(lin)
    bricks_to_natural(lin, nat)
    give_act.start()
    wide_weights(w, w2, wa, True)
    terms_sum.start_plane()
    inner_conv(g, w2, wa, lin, 0, 3)
    terms_sum.start_column()
    inner_conv(g, w2, wa, lin, 3, 4)
    terms_sum.start_back()
    take_halo(t32, wide, *halo)
    rim(kmap, t32, x32, planes, None)
    rim_conv(planes, w2, wa, lin)
    terms_sum.start_last()
    settle(lin)
    give_act.wait()
    bricks_to_natural(lin, nat)
    give_grad.start()
    terms_sum.finish()
    give_total.start()
    wait_halo_sent(*halo)
    give_total.wait()
    give_grad.wait()


def layer(vol, cot, w, bias, lists, kmap):
    vm = pl.BlockSpec(memory_space=pltpu.VMEM)
    sm = pl.BlockSpec(memory_space=pltpu.SMEM)
    hbm = pl.BlockSpec(memory_space=pl.ANY)
    field = pltpu.VMEM((10, 10, 10, 16, CH), BF16)
    planes = pltpu.VMEM((2, 5, 2, 10, 16, CH), BF16)
    return pl.pallas_call(
        kernel,
        out_shape=(
            jax.ShapeDtypeStruct((16, 512, CH), BF16),
            jax.ShapeDtypeStruct((16, 512, CH), BF16),
            jax.ShapeDtypeStruct((2, 16, BLOCKS * 4, CH), BF16),
        ),
        in_specs=[hbm, hbm, vm, vm, sm, sm],
        out_specs=(hbm, hbm, hbm),
        scratch_shapes=[
            pltpu.VMEM((16, 512, CH), BF16),
            pltpu.VMEM((64 * LINE, CH), F32),
            pltpu.VMEM((10 * SP + 2, CH), F32),
            pltpu.VMEM((49 * ENTRY, 8, CH), F32),
            pltpu.VMEM((256, CH), F32),
            pltpu.VMEM((8192, CH), BF16),
            pltpu.VMEM((16, SENT, CH), BF16),
            pltpu.VMEM((8, 4, SENT, CH), BF16),
            pltpu.VMEM((8, 4, SENT, CH), BF16),
            field,
            field,
            planes,
            planes,
            planes,
            pltpu.VMEM((3, 12 * CH, 2 * CH), BF16),
            pltpu.VMEM((2, 12 * CH, 2 * CH), BF16),
            pltpu.VMEM((4, 2 * CH, 1024), BF16),
            pltpu.VMEM((ROWS, CH), F32),
            pltpu.SemaphoreType.DMA((8,)),
            pltpu.SemaphoreType.DMA((8,)),
            pltpu.SemaphoreType.DMA((5,)),
            pltpu.SemaphoreType.REGULAR,
            *sum_scratch(BLOCKS),
        ],
        compiler_params=pltpu.CompilerParams(
            collective_id=0, has_side_effects=True, vmem_limit_bytes=63 * 2**20
        ),
        name="layer",
    )(vol, cot, w, bias, lists, kmap)


PIECES = 4


def deliver_kernel(
    act, grad, total, act_out, grad_out, weight_out, bias_out, held, terms, weights, sems, more
):
    def piece(n, m, src, dst):
        at = pl.ds(m * 16 // PIECES, 16 // PIECES)
        return (
            pltpu.make_async_copy(src.at[at], held.at[n, at], sems.at[0, n, m]),
            pltpu.make_async_copy(held.at[n, at], dst.at[at], sems.at[1, n, m]),
        )

    take_terms = pltpu.make_async_copy(total, terms, more.at[0])
    give_weights = pltpu.make_async_copy(weights, weight_out, more.at[1])
    pieces = [
        piece(n, m, src, dst)
        for n, (src, dst) in enumerate(((act, act_out), (grad, grad_out)))
        for m in range(PIECES)
    ]
    take_terms.start()
    for take, _ in pieces:
        take.start()
    take_terms.wait()
    for n in range(27):
        weights[n % 3 * 9 + n // 3] = terms[n * CH : (n + 1) * CH].astype(F32)
    bias_out[...] = terms[27 * CH : 27 * CH + 16].astype(F32)[0:1]
    give_weights.start()
    for take, give in pieces:
        take.wait()
        give.start()
    for _, give in pieces:
        give.wait()
    give_weights.wait()


def deliver(act, grad, total):
    vm = pl.BlockSpec(memory_space=pltpu.VMEM)
    hbm = pl.BlockSpec(memory_space=pl.ANY)
    return pl.pallas_call(
        deliver_kernel,
        out_shape=(
            jax.ShapeDtypeStruct(act.shape, BF16),
            jax.ShapeDtypeStruct(grad.shape, BF16),
            jax.ShapeDtypeStruct((27, CH, CH), F32),
            jax.ShapeDtypeStruct((1, CH), F32),
        ),
        in_specs=[hbm, hbm, hbm],
        out_specs=(hbm, hbm, hbm, vm),
        scratch_shapes=[
            pltpu.VMEM((2, 16, 512, CH), BF16),
            pltpu.VMEM((ROWS, CH), BF16),
            pltpu.VMEM((27, CH, CH), F32),
            pltpu.SemaphoreType.DMA((2, 2, PIECES)),
            pltpu.SemaphoreType.DMA((2,)),
        ],
        compiler_params=pltpu.CompilerParams(vmem_limit_bytes=63 * 2**20),
        name="deliver",
    )(act, grad, total)


def shards(features, cotangent, kernel_weight, conv_bias, send_lists, kernel_map):
    act, grad, total = layer(
        features.reshape(16, 512, CH),
        cotangent.reshape(16, 512, CH),
        kernel_weight.reshape(27, CH, CH),
        conv_bias.reshape(1, CH),
        send_lists[0, 0].T,
        kernel_map[0, 0],
    )
    act, grad, weight_total, bias_total = deliver(act, grad, total.reshape(ROWS, CH))
    return (
        act.reshape(features.shape),
        grad.reshape(features.shape),
        weight_total.reshape(kernel_weight.shape),
        bias_total.reshape(CH),
    )


def solution(mesh):
    block = P("gx", "gy", None, None, None, None, None)
    return jax.shard_map(
        shards,
        mesh=mesh,
        in_specs=(block, block, P(), P(), P("gx", "gy", None, None), P("gx", "gy", None, None)),
        out_specs=(block, block, P(), P()),
        check_vma=False,
    )
```
